128 devices in a mesh: row: 16 (over x, z), col: 8 (over y, core).
Axes of the slice: x: 4, y: 4, z: 4, core: 2. Of those that a mesh axis runs over, the one named last changes fastest.
Arguments:
- object_slices: float32 [2, 2, 4096, 4096], P(None, None, 'row', 'col'), may hold values from -5 to 5
- probe: float32 [2, 128, 128], replicated, may hold values from -4 to 4
- measured: float32 [2048, 128, 128], P(('row', 'col')), may hold values from 0.1 to 2
- offsets: int32 [2, 2048], P(None, ('row', 'col')), may hold values from 0 to 3968, as said below
Outputs:
- object_gradient: float32 [2, 2, 4096, 4096], P(None, None, 'row', 'col')
The draws below stay inside these ranges and needn't reach their ends.
Inputs may be any that keep to these rules, and one draw needn't show every extreme that they name: `offsets`: every offset is a multiple of 64 and every patch lies inside the object. The positions of the device at (row r, col c), which hold entries r * 16 * 8 + c * 16 onward, have their corner column inside tile column c. Among one device's positions at most 2 have their corner row in any one tile row, and in every tile column one tile row has exactly 2 corners from every device of that column.
All inputs are finite; a program needn't handle non-finite values.
Results may differ from the reference program's by a relative error of at most 0.0003.
Values sent between devices are 32-bit elements; how exact they have to be, the bound alone decides.
No kernel may reach another device: no remote copies, remote signals or barrier semaphores. Data moves between devices by JAX's collectives and lax.ppermute only.
A program may use at most 128 MiB of HBM per device.

```python
import math
import jax
import jax.numpy as jnp
from jax import lax

PATCH = 128
BLOCK = 64
SLICES = 2
TR = 256
TC = 512
P_DEV = 16
CAP = 2
POSITIONS = 2048
NY = 4096
NX = 4096
N_ROW = 16
N_COL = 8


def draw_offsets(key, part):
    key = jax.random.fold_in(key, 7)
    hot_key, order_key, shuffle_key, row_key, col_key = jax.random.split(key, 5)
    devices = N_ROW * N_COL
    slot_total = N_ROW * CAP
    hot_rows = jax.random.randint(hot_key, (N_COL,), 0, N_ROW)
    device_col = jnp.arange(devices, dtype=jnp.int32) % N_COL
    device_hot = hot_rows[device_col]
    order_keys = jax.random.split(order_key, devices)
    scores = jax.vmap(lambda subkey: jax.random.permutation(subkey, slot_total))(order_keys).astype(jnp.int32)
    slot_index = jnp.arange(slot_total, dtype=jnp.int32)
    slot_owner = slot_index // CAP
    scores = jnp.where(slot_owner[None, :] == device_hot[:, None], -1 - slot_index[None, :], scores)
    chosen = jnp.argsort(scores, axis=1, stable=True)[:, :P_DEV].astype(jnp.int32)
    shuffle_keys = jax.random.split(shuffle_key, devices)
    reorder = jax.vmap(lambda subkey: jax.random.permutation(subkey, P_DEV))(shuffle_keys).astype(jnp.int32)
    chosen = jnp.take_along_axis(chosen, reorder, axis=1)
    owner_row = chosen // CAP
    block_row = jax.random.randint(row_key, (devices, P_DEV), 0, TR // BLOCK)
    block_col = jax.random.randint(col_key, (devices, P_DEV), 0, TC // BLOCK)
    block_row = jnp.where(owner_row == N_ROW - 1, jnp.minimum(block_row, TR // BLOCK - 2), block_row)
    last_col = (device_col == N_COL - 1)[:, None]
    block_col = jnp.where(last_col, jnp.minimum(block_col, TC // BLOCK - 2), block_col)
    corner_y = owner_row * TR + block_row * BLOCK
    corner_x = device_col[:, None] * TC + block_col * BLOCK
    return jnp.stack([corner_y.reshape(-1), corner_x.reshape(-1)]).astype(jnp.int32)


def block_scale(stream_key, dims, cuts, low, largest):
    factor_of = 1.0
    for dim, shards_of in cuts:
        draws = jax.random.uniform(jax.random.fold_in(jax.random.fold_in(stream_key, 6), dim), (shards_of,), jnp.float32, low / len(cuts), largest / len(cuts))
        factor_of = factor_of * jnp.repeat(jnp.exp(draws), dims[dim] // shards_of).reshape((-1,) + (1,) * (len(dims) - 1 - dim))
    return factor_of


def scatter_about(stream_key, shape, scale, bound, shards=(), kind=jnp.bfloat16):
    drawn = jax.random.normal(stream_key, shape, jnp.float32) * scale
    if len(shards) > 0:
        drawn = block_scale(stream_key, shape, shards, -0.22, 0.18) * drawn
    return jnp.clip(drawn, min=-bound, max=bound).astype(kind)


def setup_inputs(seed: int = 0) -> dict:
    streams_of = jax.random.split(jax.random.key(seed), 5)
    object_slices = scatter_about(streams_of[0], (SLICES, 2, NY, NX), 0.8, 5.0, ((2, 16), (3, 8)), jnp.float32)
    probe = scatter_about(streams_of[1], (2, PATCH, PATCH), 0.5, 4.0, (), jnp.float32)
    measured = jnp.clip(jnp.exp(math.log(2.0) - 2.9957323 * jax.random.uniform(streams_of[2], (POSITIONS, PATCH, PATCH), jnp.float32) ** block_scale(streams_of[2], (POSITIONS, PATCH, PATCH), ((0, 128),), -0.2, 0.2)), 0.1, 2.0)
    offsets = draw_offsets(jax.random.fold_in(streams_of[4], 71), 0)
    return dict(object_slices=object_slices, probe=probe, measured=measured, offsets=offsets)


PHASE = 40.0
batch_rows = 64


def fresnel_kernel(length):
    index = jnp.arange(length, dtype=jnp.int32)
    freq = jnp.where(index < length // 2, index, index - length).astype(jnp.float32) / length
    phase = PHASE * (freq[:, None] * freq[:, None] + freq[None, :] * freq[None, :])
    return jnp.cos(phase), -jnp.sin(phase)


def fft_two(field):
    return jnp.fft.fft2(field, norm="ortho")


def ifft_two(field):
    return jnp.fft.ifft2(field, norm="ortho")


def patch_gradients(patches, measured_rows, probe_field, kernel):
    slices = patches.shape[1]
    trans = [lax.complex(patches[:, level, 0], patches[:, level, 1]) for level in range(slices)]
    wave = probe_field[None] * trans[0]
    entering = []
    for level in range(1, slices):
        wave = ifft_two(kernel * fft_two(wave))
        entering.append(wave)
        wave = wave * trans[level]
    far = fft_two(wave)
    misfit = jnp.real(far) * jnp.real(far) + jnp.imag(far) * jnp.imag(far) - measured_rows
    back = ifft_two(2.0 * misfit * far)
    grads = [back] * slices
    for level in range(slices - 1, 0, -1):
        grads[level] = jnp.conj(entering[level - 1]) * back
        back = jnp.conj(trans[level]) * back
        back = ifft_two(jnp.conj(kernel) * fft_two(back))
    grads[0] = jnp.conj(probe_field)[None] * back
    return jnp.stack([jnp.stack([jnp.real(grad_one), jnp.imag(grad_one)], axis=1) for grad_one in grads], axis=1)


def reference(object_slices, probe, measured, offsets):
    slices = object_slices.shape[0]
    length = measured.shape[1]
    kernel_re, kernel_im = fresnel_kernel(length)
    kernel = lax.complex(kernel_re, kernel_im)
    probe_field = lax.complex(probe[0], probe[1])
    groups = measured.shape[0] // batch_rows
    zero_index = jnp.zeros((), jnp.int32)
    window = (slices, 2, length, length)

    def take_patch(corner_y, corner_x):
        return lax.dynamic_slice(object_slices, (zero_index, zero_index, corner_y, corner_x), window)

    def step(total, group):
        start = (group * batch_rows).astype(jnp.int32)
        corner_ys = lax.dynamic_slice_in_dim(offsets[0], start, batch_rows)
        corner_xs = lax.dynamic_slice_in_dim(offsets[1], start, batch_rows)
        rows_here = lax.dynamic_slice_in_dim(measured, start, batch_rows, 0)
        patches = jax.vmap(take_patch)(corner_ys, corner_xs)
        grads = patch_gradients(patches, rows_here, probe_field, kernel)

        def add_one(item, acc):
            place = (zero_index, zero_index, corner_ys[item], corner_xs[item])
            current = lax.dynamic_slice(acc, place, window)
            return lax.dynamic_update_slice(acc, current + grads[item], place)

        total = lax.fori_loop(0, batch_rows, add_one, total)
        return total, None

    result, _ = lax.scan(step, jnp.zeros_like(object_slices), jnp.arange(groups, dtype=jnp.int32))
    return result
```

```python
import math

import jax
import jax.numpy as jnp
import ml_dtypes
import numpy as np
from jax import lax
from jax.experimental import pallas as pl
from jax.experimental.pallas import tpu as pltpu
from jax.sharding import PartitionSpec as P

PHASE = 40.0
SIDE = 128
BLOCK = 64
CAP = 2
META = 8
VMEM_LIMIT = 48 * 1024 * 1024


def dft_matrix():
    index = np.arange(SIDE)
    angle = (index[:, None] * index[None, :] % SIDE) * (-2.0 * math.pi / SIDE)
    return np.exp(1j * angle) / math.sqrt(SIDE)


def propagation_matrix():
    index = np.arange(SIDE)
    freq = np.where(index < SIDE // 2, index, index - SIDE) / SIDE
    dft = dft_matrix()
    return np.conj(dft) @ (np.exp(-1j * PHASE * freq * freq)[:, None] * dft)


def real_forms(matrix):
    right = np.block([[matrix.real, matrix.imag], [-matrix.imag, matrix.real]])
    out = []
    for form in (right, right.T):
        form = form.astype(np.float32)
        high = form.astype(ml_dtypes.bfloat16)
        out.append(high)
        out.append((form - high.astype(np.float32)).astype(ml_dtypes.bfloat16))
    return np.stack(out)


TABLES = np.concatenate([real_forms(propagation_matrix()), real_forms(dft_matrix())])


def split(field):
    high = field.astype(jnp.bfloat16)
    low = (field - high.astype(jnp.float32)).astype(jnp.bfloat16)
    return high, low


def from_right(rows, tables, at):
    high, low = split(rows)
    left = jnp.concatenate([high, low, high], axis=1)
    right = jnp.concatenate([tables[at], tables[at], tables[at + 1]], axis=0)
    return jnp.dot(left, right, preferred_element_type=jnp.float32)


def from_left(columns, tables, at):
    high, low = split(columns)
    left = jnp.concatenate([tables[at], tables[at], tables[at + 1]], axis=1)
    right = jnp.concatenate([high, low, high], axis=0)
    return jnp.dot(left, right, preferred_element_type=jnp.float32)


def swap(pair):
    top = jnp.concatenate([pair[:SIDE, :SIDE], pair[SIDE:, :SIDE]], axis=1)
    bottom = jnp.concatenate([pair[:SIDE, SIDE:], pair[SIDE:, SIDE:]], axis=1)
    return jnp.concatenate([top, bottom], axis=0)


def two_sided(rows, tables, right_at, left_at):
    return from_left(swap(from_right(rows, tables, right_at)), tables, left_at)


def low_lanes(shape):
    return lax.broadcasted_iota(jnp.int32, shape, len(shape) - 1) < BLOCK


def cut_pair(ext_ref, comp, row, col):
    first = ext_ref[comp, pl.ds(row, SIDE), col : col + SIDE]
    second = ext_ref[comp, pl.ds(row, SIDE), col + SIDE : col + 2 * SIDE]
    mixed = jnp.where(low_lanes(first.shape), second, first)
    return first, pltpu.roll(mixed, BLOCK, 1)


def times(left_re, left_im, right_re, right_im):
    return (left_re * right_re - left_im * right_im, left_re * right_im + left_im * right_re)


def conj_times(left_re, left_im, right_re, right_im):
    return (left_re * right_re + left_im * right_im, left_re * right_im - left_im * right_re)


def load_extended(tile_ref, below_ref, right_ref, diag_ref, ext_ref, sems, comps):
    count = len(comps)
    rows, cols = tile_ref.shape[1:]
    first = comps[0]
    pieces = (
        (tile_ref, pl.ds(0, rows), pl.ds(0, cols)),
        (below_ref, pl.ds(rows, BLOCK), pl.ds(0, cols)),
        (right_ref, pl.ds(0, rows), pl.ds(cols, SIDE)),
        (diag_ref, pl.ds(rows, BLOCK), pl.ds(cols, SIDE)),
    )
    return [
        pltpu.make_async_copy(
            source.at[pl.ds(first, count)], ext_ref.at[pl.ds(0, count), at_rows, at_cols], sems.at[n]
        )
        for n, (source, at_rows, at_cols) in enumerate(pieces)
    ]


def pack_kernel(off_ref, meas_ref, send_ref, meta_ref, count_ref, corner_ref, sems):
    owners = send_ref.shape[0]
    positions = meas_ref.shape[0]
    for owner in range(owners):
        count_ref[owner] = 0
        for rank in range(CAP):
            corner_ref[owner * CAP + rank] = -1
    copies = []
    for pos in range(positions):
        y = off_ref[0, pos]
        x = off_ref[1, pos]
        owner = lax.shift_right_logical(y, 8)
        rank = jnp.minimum(count_ref[owner], CAP - 1)
        count_ref[owner] = rank + 1
        corner = (lax.shift_right_logical(y, 6) & 3) * 8 + (lax.shift_right_logical(x, 6) & 7)
        corner_ref[owner * CAP + rank] = corner
        copy = pltpu.make_async_copy(
            meas_ref.at[pos],
            send_ref.at[owner, pl.ds(pl.multiple_of(rank * SIDE, SIDE), SIDE)],
            sems.at[pos],
        )
        copy.start()
        copies.append(copy)
    row = lax.broadcasted_iota(jnp.int32, (META, SIDE), 0)
    for owner in range(owners):
        both = jnp.where(row == 0, corner_ref[owner * CAP], corner_ref[owner * CAP + 1])
        meta_ref[owner] = both.astype(jnp.float32)
    copy = pltpu.make_async_copy(
        meta_ref, send_ref.at[:, pl.ds(CAP * SIDE, META)], sems.at[positions]
    )
    copy.start()
    copies.append(copy)
    for copy in copies:
        copy.wait()


def pack(offsets, measured, owners):
    positions = measured.shape[0]
    return pl.pallas_call(
        pack_kernel,
        out_shape=jax.ShapeDtypeStruct((owners, CAP * SIDE + META, SIDE), jnp.float32),
        in_specs=[
            pl.BlockSpec(memory_space=pltpu.SMEM),
            pl.BlockSpec(memory_space=pl.ANY),
        ],
        out_specs=pl.BlockSpec(memory_space=pl.ANY),
        scratch_shapes=[
            pltpu.VMEM((owners, META, SIDE), jnp.float32),
            pltpu.SMEM((owners,), jnp.int32),
            pltpu.SMEM((owners * CAP,), jnp.int32),
            pltpu.SemaphoreType.DMA((positions + 1,)),
        ],
        name="pack_measured",
    )(offsets, measured)


def forward_kernel(
    tile_ref, below_ref, right_ref, diag_ref, probe_ref, tables, far_ref, enter_ref, ext_ref, sems
):
    step = pl.program_id(0)
    copies = load_extended(
        tile_ref, below_ref, right_ref, diag_ref, ext_ref, sems, range(tile_ref.shape[0])
    )

    @pl.when(step == 0)
    def _():
        for copy in copies:
            copy.start()
        for copy in copies:
            copy.wait()

    row = pl.multiple_of(step * BLOCK, BLOCK)
    probe_re = probe_ref[0]
    probe_im = probe_ref[1]
    for pair in range(far_ref.shape[0]):
        trans = [cut_pair(ext_ref, comp, row, pair * SIDE) for comp in range(4)]
        waves = [times(probe_re, probe_im, trans[0][n], trans[1][n]) for n in range(2)]
        rows = jnp.concatenate([jnp.concatenate(wave, axis=1) for wave in waves], axis=0)
        enter = two_sided(rows, tables, 0, 2)
        enter_ref[pair] = enter
        waves = [
            times(
                enter[:SIDE, n * SIDE : (n + 1) * SIDE],
                enter[SIDE:, n * SIDE : (n + 1) * SIDE],
                trans[2][n],
                trans[3][n],
            )
            for n in range(2)
        ]
        rows = jnp.concatenate([jnp.concatenate(wave, axis=1) for wave in waves], axis=0)
        far_ref[pair] = two_sided(rows, tables, 4, 6)


def stage_cost(pairs):
    return pl.CostEstimate(
        flops=pairs * 4 * 3 * 2 * 256**3, bytes_accessed=14 * 1024 * 1024, transcendentals=0
    )


def forward(tile, below, right, diag, probe, tables):
    steps = tile.shape[1] // BLOCK
    pairs = tile.shape[2] // SIDE
    field = jax.ShapeDtypeStruct((steps * pairs, 2 * SIDE, 2 * SIDE), jnp.float32)
    whole = pl.BlockSpec(memory_space=pl.ANY)
    block = pl.BlockSpec((pairs, 2 * SIDE, 2 * SIDE), lambda step: (step, 0, 0))
    return pl.pallas_call(
        forward_kernel,
        out_shape=(field, field),
        grid=(steps,),
        in_specs=[
            whole,
            whole,
            whole,
            whole,
            pl.BlockSpec(probe.shape, lambda step: (0, 0, 0)),
            pl.BlockSpec(tables.shape, lambda step: (0, 0, 0)),
        ],
        out_specs=(block, block),
        scratch_shapes=[
            pltpu.VMEM(
                (tile.shape[0], tile.shape[1] + BLOCK, tile.shape[2] + SIDE), jnp.float32
            ),
            pltpu.SemaphoreType.DMA((4,)),
        ],
        compiler_params=pltpu.CompilerParams(vmem_limit_bytes=VMEM_LIMIT),
        cost_estimate=stage_cost(steps * pairs),
        name="forward_fields",
    )(tile, below, right, diag, probe, tables)


def backward_kernel(
    corner_ref,
    recv_ref,
    tile_ref,
    below_ref,
    right_ref,
    diag_ref,
    probe_ref,
    tables,
    far_ref,
    enter_ref,
    out_ref,
    out_right_ref,
    out_below_ref,
    out_diag_ref,
    ext_ref,
    sum_ref,
    count_ref,
    even_ref,
    odd_ref,
    sems,
):
    step = pl.program_id(0)
    pairs = far_ref.shape[0]
    corners = sum_ref.shape[0]
    copies = load_extended(tile_ref, below_ref, right_ref, diag_ref, ext_ref, sems, (2, 3))

    @pl.when(step == 0)
    def _():
        for copy in copies:
            copy.start()
        sum_ref[...] = jnp.zeros_like(sum_ref)
        even_ref[...] = jnp.zeros_like(even_ref)
        odd_ref[...] = jnp.zeros_like(odd_ref)
        for corner in range(corners):
            count_ref[corner] = 0
        for source in range(recv_ref.shape[0]):
            for rank in range(CAP):
                corner = corner_ref[source, rank]

                @pl.when(corner >= 0)
                def _():
                    count_ref[corner] = count_ref[corner] + 1
                    sum_ref[corner] = (
                        sum_ref[corner] + recv_ref[source, rank * SIDE : (rank + 1) * SIDE]
                    )

        for copy in copies:
            copy.wait()

    row = pl.multiple_of(step * BLOCK, BLOCK)
    probe_re = probe_ref[0]
    probe_im = probe_ref[1]
    for pair in range(pairs):
        trans = [cut_pair(ext_ref, comp, row, pair * SIDE) for comp in range(2)]
        waves = []
        for n in range(2):
            corner = step * (2 * pairs) + 2 * pair + n
            hits = count_ref[corner].astype(jnp.float32)
            far_re = far_ref[pair, :SIDE, n * SIDE : (n + 1) * SIDE]
            far_im = far_ref[pair, SIDE:, n * SIDE : (n + 1) * SIDE]
            misfit = 2.0 * (hits * (far_re * far_re + far_im * far_im) - sum_ref[corner])
            waves.append((misfit * far_re, misfit * far_im))
        rows = jnp.concatenate([jnp.concatenate(wave, axis=1) for wave in waves], axis=0)
        back = two_sided(rows, tables, 6, 4)
        waves = []
        grads = []
        for n in range(2):
            back_re = back[:SIDE, n * SIDE : (n + 1) * SIDE]
            back_im = back[SIDE:, n * SIDE : (n + 1) * SIDE]
            enter_re = enter_ref[pair, :SIDE, n * SIDE : (n + 1) * SIDE]
            enter_im = enter_ref[pair, SIDE:, n * SIDE : (n + 1) * SIDE]
            grads.append(conj_times(enter_re, enter_im, back_re, back_im))
            waves.append(conj_times(trans[0][n], trans[1][n], back_re, back_im))
        rows = jnp.concatenate([jnp.concatenate(wave, axis=1) for wave in waves], axis=0)
        back = two_sided(rows, tables, 2, 0)
        for n, acc in ((0, even_ref), (1, odd_ref)):
            first = conj_times(
                probe_re,
                probe_im,
                back[:SIDE, n * SIDE : (n + 1) * SIDE],
                back[SIDE:, n * SIDE : (n + 1) * SIDE],
            )
            for comp, value in enumerate(first + grads[n]):
                at = (comp, slice(None), slice(pair * SIDE, (pair + 1) * SIDE))
                acc[comp, :BLOCK, at[2]] = acc[comp, BLOCK:, at[2]] + value[:BLOCK]
                acc[comp, BLOCK:, at[2]] = value[BLOCK:]

    def merged(comp, rows, col):
        here = odd_ref[comp, rows, col : col + SIDE] if col < pairs * SIDE else None
        before = odd_ref[comp, rows, col - SIDE : col] if col > 0 else None
        if here is None:
            here = jnp.zeros_like(before)
        if before is None:
            before = jnp.zeros_like(here)
        mixed = jnp.where(low_lanes(here.shape), here, before)
        shifted = pltpu.roll(mixed, BLOCK, 1)
        if col < pairs * SIDE:
            shifted = shifted + even_ref[comp, rows, col : col + SIDE]
        return shifted

    top = slice(0, BLOCK)
    for comp in range(4):
        for col in range(0, pairs * SIDE, SIDE):
            out_ref[comp, :, col : col + SIDE] = merged(comp, top, col)
        out_right_ref[comp] = merged(comp, top, pairs * SIDE)

    @pl.when(step == pl.num_programs(0) - 1)
    def _():
        bottom = slice(BLOCK, 2 * BLOCK)
        for comp in range(4):
            for col in range(0, pairs * SIDE, SIDE):
                out_below_ref[comp, :, col : col + SIDE] = merged(comp, bottom, col)
            out_diag_ref[comp] = merged(comp, bottom, pairs * SIDE)


def backward(corner, recv, tile, below, right, diag, probe, tables, far, enter):
    steps = tile.shape[1] // BLOCK
    pairs = tile.shape[2] // SIDE
    comps, rows, cols = tile.shape
    whole = pl.BlockSpec(memory_space=pl.ANY)
    block = pl.BlockSpec((pairs, 2 * SIDE, 2 * SIDE), lambda step: (step, 0, 0))

    def full(shape):
        return pl.BlockSpec(shape, lambda step: (0, 0, 0))

    return pl.pallas_call(
        backward_kernel,
        out_shape=(
            jax.ShapeDtypeStruct(tile.shape, jnp.float32),
            jax.ShapeDtypeStruct((comps, rows, SIDE), jnp.float32),
            jax.ShapeDtypeStruct((comps, BLOCK, cols), jnp.float32),
            jax.ShapeDtypeStruct((comps, BLOCK, SIDE), jnp.float32),
        ),
        grid=(steps,),
        in_specs=[
            pl.BlockSpec(memory_space=pltpu.SMEM),
            full(recv.shape),
            whole,
            whole,
            whole,
            whole,
            full(probe.shape),
            full(tables.shape),
            block,
            block,
        ],
        out_specs=(
            pl.BlockSpec((comps, BLOCK, cols), lambda step: (0, step, 0)),
            pl.BlockSpec((comps, BLOCK, SIDE), lambda step: (0, step, 0)),
            full((comps, BLOCK, cols)),
            full((comps, BLOCK, SIDE)),
        ),
        scratch_shapes=[
            pltpu.VMEM((2, rows + BLOCK, cols + SIDE), jnp.float32),
            pltpu.VMEM((steps * pairs * 2, SIDE, SIDE), jnp.float32),
            pltpu.SMEM((steps * pairs * 2,), jnp.int32),
            pltpu.VMEM((comps, SIDE, cols), jnp.float32),
            pltpu.VMEM((comps, SIDE, cols), jnp.float32),
            pltpu.SemaphoreType.DMA((4,)),
        ],
        compiler_params=pltpu.CompilerParams(vmem_limit_bytes=VMEM_LIMIT),
        cost_estimate=stage_cost(steps * pairs),
        name="backward_fields",
    )(corner, recv, tile, below, right, diag, probe, tables, far, enter)


def border_kernel(own_ref, above_ref, left_ref, diag_ref, out_ref, top_ref, side_ref, sems):
    comps, rows, cols = out_ref.shape
    top = out_ref.at[:, pl.ds(0, BLOCK)]
    side = out_ref.at[:, pl.ds(BLOCK, rows - BLOCK), pl.ds(0, SIDE)]
    loads = [
        pltpu.make_async_copy(top, top_ref, sems.at[0]),
        pltpu.make_async_copy(side, side_ref, sems.at[1]),
    ]
    for copy in loads:
        copy.start()
    for copy in loads:
        copy.wait()
    top_ref[...] = top_ref[...] + above_ref[...]
    top_ref[:, :, :SIDE] = top_ref[:, :, :SIDE] + left_ref[:, :BLOCK] + diag_ref[...]
    side_ref[...] = side_ref[...] + left_ref[:, BLOCK:]
    stores = [
        pltpu.make_async_copy(top_ref, top, sems.at[0]),
        pltpu.make_async_copy(side_ref, side, sems.at[1]),
    ]
    for copy in stores:
        copy.start()
    for copy in stores:
        copy.wait()


def add_borders(own, above, left, diag):
    comps, rows, cols = own.shape
    vmem = pl.BlockSpec(memory_space=pltpu.VMEM)
    return pl.pallas_call(
        border_kernel,
        out_shape=jax.ShapeDtypeStruct(own.shape, jnp.float32),
        in_specs=[pl.BlockSpec(memory_space=pl.ANY), vmem, vmem, vmem],
        out_specs=pl.BlockSpec(memory_space=pl.ANY),
        scratch_shapes=[
            pltpu.VMEM((comps, BLOCK, cols), jnp.float32),
            pltpu.VMEM((comps, rows - BLOCK, SIDE), jnp.float32),
            pltpu.SemaphoreType.DMA((2,)),
        ],
        input_output_aliases={0: 0},
        compiler_params=pltpu.CompilerParams(vmem_limit_bytes=VMEM_LIMIT),
        name="add_borders",
    )(own, above, left, diag)


def moved(shard, down, across):
    row_total = lax.axis_size("row")
    col_total = lax.axis_size("col")
    if across == 0:
        pairs = [(r, r + down) for r in range(row_total) if 0 <= r + down < row_total]
        return lax.ppermute(shard, "row", pairs)
    if down == 0:
        pairs = [(c, c + across) for c in range(col_total) if 0 <= c + across < col_total]
        return lax.ppermute(shard, "col", pairs)
    pairs = [
        (r * col_total + c, (r + down) * col_total + c + across)
        for r in range(row_total)
        for c in range(col_total)
        if 0 <= r + down < row_total and 0 <= c + across < col_total
    ]
    return lax.ppermute(shard, ("row", "col"), pairs)


def body(object_slices, probe, measured, offsets):
    slices, parts, tile_rows, tile_cols = object_slices.shape
    tile = object_slices.reshape(slices * parts, tile_rows, tile_cols)
    row_total = lax.axis_size("row")
    tables = jnp.asarray(TABLES)
    send = pack(offsets, measured, row_total)
    recv = lax.all_to_all(send, "row", split_axis=0, concat_axis=0, tiled=True)
    below = moved(tile[:, :BLOCK, :], -1, 0)
    right = moved(tile[:, :, :SIDE], 0, -1)
    diag = moved(tile[:, :BLOCK, :SIDE], -1, -1)
    far, enter = forward(tile, below, right, diag, probe, tables)
    corner = recv[:, CAP * SIDE : CAP * SIDE + CAP, 0].astype(jnp.int32)
    own, to_right, to_below, to_diag = backward(
        corner, recv, tile, below, right, diag, probe, tables, far, enter
    )
    above = moved(to_below, 1, 0)
    left = moved(to_right, 0, 1)
    corner_part = moved(to_diag, 1, 1)
    result = add_borders(own, above, left, corner_part)
    return result.reshape(object_slices.shape)


def solution(mesh):
    placed = (
        P(None, None, "row", "col"),
        P(),
        P(("row", "col"), None, None),
        P(None, ("row", "col")),
    )
    return jax.shard_map(
        body, mesh=mesh, in_specs=placed, out_specs=P(None, None, "row", "col"), check_vma=False
    )
```

```python
import functools
import math

import jax
import jax.numpy as jnp
import ml_dtypes
import numpy as np
from jax import lax
from jax.experimental import pallas as pl
from jax.experimental.pallas import tpu as pltpu
from jax.sharding import PartitionSpec as P

PHASE = 40.0
SIDE = 128
BLOCK = 64
CAP = 2
META = 8
VMEM_LIMIT = 48 * 1024 * 1024


def dft_matrix():
    index = np.arange(SIDE)
    angle = (index[:, None] * index[None, :] % SIDE) * (-2.0 * math.pi / SIDE)
    return np.exp(1j * angle) / math.sqrt(SIDE)


def propagation_matrix():
    index = np.arange(SIDE)
    freq = np.where(index < SIDE // 2, index, index - SIDE) / SIDE
    dft = dft_matrix()
    return np.conj(dft) @ (np.exp(-1j * PHASE * freq * freq)[:, None] * dft)


def real_forms(matrix):
    right = np.block([[matrix.real, matrix.imag], [-matrix.imag, matrix.real]])
    out = []
    for form in (right, right.T):
        form = form.astype(np.float32)
        high = form.astype(ml_dtypes.bfloat16)
        out.append(high)
        out.append((form - high.astype(np.float32)).astype(ml_dtypes.bfloat16))
    return np.stack(out)


TABLES = np.concatenate([real_forms(propagation_matrix()), real_forms(dft_matrix())])


def split(field):
    high = field.astype(jnp.bfloat16)
    low = (field - high.astype(jnp.float32)).astype(jnp.bfloat16)
    return high, low


def from_right(rows, tables, at):
    high, low = split(rows)
    left = jnp.concatenate([high, low, high], axis=1)
    right = jnp.concatenate([tables[at], tables[at], tables[at + 1]], axis=0)
    return jnp.dot(left, right, preferred_element_type=jnp.float32)


def from_left(columns, tables, at):
    high, low = split(columns)
    left = jnp.concatenate([tables[at], tables[at], tables[at + 1]], axis=1)
    right = jnp.concatenate([high, low, high], axis=0)
    return jnp.dot(left, right, preferred_element_type=jnp.float32)


def swap(pair):
    top = jnp.concatenate([pair[:SIDE, :SIDE], pair[SIDE:, :SIDE]], axis=1)
    bottom = jnp.concatenate([pair[:SIDE, SIDE:], pair[SIDE:, SIDE:]], axis=1)
    return jnp.concatenate([top, bottom], axis=0)


def two_sided(pairs, tables, right_at, left_at):
    pairs = [from_right(rows, tables, right_at) for rows in pairs]
    return [from_left(swap(rows), tables, left_at) for rows in pairs]


def stacked(fields):
    return jnp.concatenate([jnp.concatenate(field, axis=1) for field in fields], axis=0)


def halves(pair, n):
    return pair[:SIDE, n * SIDE : (n + 1) * SIDE], pair[SIDE:, n * SIDE : (n + 1) * SIDE]


def low_lanes(shape):
    return lax.broadcasted_iota(jnp.int32, shape, len(shape) - 1) < BLOCK


def cut_pair(ext_ref, comp, row, col):
    first = ext_ref[comp, row : row + SIDE, col : col + SIDE]
    second = ext_ref[comp, row : row + SIDE, col + SIDE : col + 2 * SIDE]
    mixed = jnp.where(low_lanes(first.shape), second, first)
    return first, pltpu.roll(mixed, BLOCK, 1)


def times(left_re, left_im, right_re, right_im):
    return (left_re * right_re - left_im * right_im, left_re * right_im + left_im * right_re)


def conj_times(left_re, left_im, right_re, right_im):
    return (left_re * right_re + left_im * right_im, left_re * right_im - left_im * right_re)


def pack_kernel(off_ref, meas_ref, send_ref, meta_ref, count_ref, corner_ref, sems):
    owners = send_ref.shape[0]
    positions = meas_ref.shape[0]
    for owner in range(owners):
        count_ref[owner] = 0
        for rank in range(CAP):
            corner_ref[owner * CAP + rank] = -1
    copies = []
    for pos in range(positions):
        y = off_ref[0, pos]
        x = off_ref[1, pos]
        owner = lax.shift_right_logical(y, 8)
        rank = jnp.minimum(count_ref[owner], CAP - 1)
        count_ref[owner] = rank + 1
        corner = (lax.shift_right_logical(y, 6) & 3) * 8 + (lax.shift_right_logical(x, 6) & 7)
        corner_ref[owner * CAP + rank] = corner
        copy = pltpu.make_async_copy(
            meas_ref.at[pos],
            send_ref.at[owner, pl.ds(pl.multiple_of(rank * SIDE, SIDE), SIDE)],
            sems.at[pos],
        )
        copy.start()
        copies.append(copy)
    row = lax.broadcasted_iota(jnp.int32, (META, SIDE), 0)
    for owner in range(owners):
        both = jnp.where(row == 0, corner_ref[owner * CAP], corner_ref[owner * CAP + 1])
        meta_ref[owner] = both.astype(jnp.float32)
    copy = pltpu.make_async_copy(
        meta_ref, send_ref.at[:, pl.ds(CAP * SIDE, META)], sems.at[positions]
    )
    copy.start()
    copies.append(copy)
    for copy in copies:
        copy.wait()


def pack(offsets, measured, owners):
    positions = measured.shape[0]
    return pl.pallas_call(
        pack_kernel,
        out_shape=jax.ShapeDtypeStruct((owners, CAP * SIDE + META, SIDE), jnp.float32),
        in_specs=[
            pl.BlockSpec(memory_space=pltpu.SMEM),
            pl.BlockSpec(memory_space=pltpu.VMEM),
        ],
        out_specs=pl.BlockSpec(memory_space=pl.ANY),
        scratch_shapes=[
            pltpu.VMEM((owners, META, SIDE), jnp.float32),
            pltpu.SMEM((owners,), jnp.int32),
            pltpu.SMEM((owners * CAP,), jnp.int32),
            pltpu.SemaphoreType.DMA((positions + 1,)),
        ],
        cost_estimate=pl.CostEstimate(
            flops=0, bytes_accessed=40 * 1024 * 1024, transcendentals=0
        ),
        name="pack_measured",
    )(offsets, measured)


def pair_places(rows, cols):
    row_blocks = rows // BLOCK
    last = cols - SIDE
    rim = [(row_blocks - 1, col) for col in range(0, cols, SIDE)]
    rim += [(row, last) for row in range(row_blocks - 1)]
    inner = [(row, col) for row in range(row_blocks - 1) for col in range(0, last, SIDE)]
    return rim, inner


def forward_pairs(places, ext_ref, probe_ref, tables, far_ref, enter_ref):
    probe_re = probe_ref[0]
    probe_im = probe_ref[1]
    rows = []
    for row, col in places:
        trans = [cut_pair(ext_ref, comp, row * BLOCK, col) for comp in range(2)]
        rows.append(
            stacked([times(probe_re, probe_im, trans[0][n], trans[1][n]) for n in range(2)])
        )
    enters = two_sided(rows, tables, 0, 2)
    rows = []
    for pair, (row, col) in enumerate(places):
        enter = enters[pair]
        enter_ref[pair] = enter
        trans = [cut_pair(ext_ref, comp, row * BLOCK, col) for comp in range(2, 4)]
        rows.append(
            stacked([times(*halves(enter, n), trans[0][n], trans[1][n]) for n in range(2)])
        )
    fars = two_sided(rows, tables, 4, 6)
    for pair in range(len(places)):
        far_ref[pair] = fars[pair]


def extended_parts(tile_ref, below_ref, right_ref, diag_ref, ext_ref, first):
    rows, cols = tile_ref.shape[1:]
    comps = pl.ds(first, tile_ref.shape[0] - first)
    return [
        (tile_ref.at[comps], ext_ref.at[:, pl.ds(0, rows), pl.ds(0, cols)]),
        (below_ref.at[comps], ext_ref.at[:, pl.ds(rows, BLOCK), pl.ds(0, cols)]),
        (right_ref.at[comps], ext_ref.at[:, pl.ds(0, rows), pl.ds(cols, SIDE)]),
        (diag_ref.at[comps], ext_ref.at[:, pl.ds(rows, BLOCK), pl.ds(cols, SIDE)]),
    ]


def start_copies(parts, sems):
    copies = [
        pltpu.make_async_copy(source, target, sems.at[n])
        for n, (source, target) in enumerate(parts)
    ]
    for copy in copies:
        copy.start()
    return copies


def wait_copies(copies):
    for copy in copies:
        copy.wait()


def forward_inner_kernel(places, tile_ref, probe_ref, tables, far_ref, enter_ref):
    forward_pairs(places, tile_ref, probe_ref, tables, far_ref, enter_ref)


def forward_rim_kernel(
    places,
    tile_ref,
    below_ref,
    right_ref,
    diag_ref,
    probe_ref,
    tables,
    far_ref,
    enter_ref,
    ext_ref,
    sems,
):
    wait_copies(
        start_copies(
            extended_parts(tile_ref, below_ref, right_ref, diag_ref, ext_ref, 0), sems
        )
    )
    forward_pairs(places, ext_ref, probe_ref, tables, far_ref, enter_ref)


def stage_cost(pairs):
    return pl.CostEstimate(
        flops=pairs * 4 * 3 * 2 * 256**3, bytes_accessed=1024 * 1024, transcendentals=0
    )


def fields(places):
    field = jax.ShapeDtypeStruct((len(places), 2 * SIDE, 2 * SIDE), jnp.float32)
    return field, field


def in_vmem(count):
    return [pl.BlockSpec(memory_space=pltpu.VMEM)] * count


def anywhere(count):
    return [pl.BlockSpec(memory_space=pl.ANY)] * count


def forward_inner(places, tile, probe, tables):
    return pl.pallas_call(
        functools.partial(forward_inner_kernel, places),
        out_shape=fields(places),
        in_specs=in_vmem(3),
        out_specs=tuple(in_vmem(2)),
        compiler_params=pltpu.CompilerParams(vmem_limit_bytes=VMEM_LIMIT),
        cost_estimate=stage_cost(8 * len(places)),
        name="forward_inner",
    )(tile, probe, tables)


def extended_shape(tile, comps):
    return pltpu.VMEM((comps, tile.shape[1] + BLOCK, tile.shape[2] + SIDE), jnp.float32)


def forward_rim(places, tile, below, right, diag, probe, tables):
    return pl.pallas_call(
        functools.partial(forward_rim_kernel, places),
        out_shape=fields(places),
        in_specs=anywhere(4) + in_vmem(2),
        out_specs=tuple(in_vmem(2)),
        scratch_shapes=[extended_shape(tile, tile.shape[0]), pltpu.SemaphoreType.DMA((4,))],
        compiler_params=pltpu.CompilerParams(vmem_limit_bytes=VMEM_LIMIT),
        cost_estimate=stage_cost(8 * len(places)),
        name="forward_rim",
    )(tile, below, right, diag, probe, tables)


def gather_sums(corner_ref, recv_ref, sum_ref, count_ref):
    sum_ref[...] = jnp.zeros_like(sum_ref)
    for corner in range(sum_ref.shape[0]):
        count_ref[corner] = 0
    for source in range(recv_ref.shape[0]):
        for rank in range(CAP):
            corner = corner_ref[source, rank]

            @pl.when(corner >= 0)
            def _():
                count_ref[corner] = count_ref[corner] + 1
                sum_ref[corner] = (
                    sum_ref[corner] + recv_ref[source, rank * SIDE : (rank + 1) * SIDE]
                )


def backward_pairs(
    places, width, probe_ref, tables, far_ref, enter_ref, ext_ref, sum_ref, count_ref, store
):
    probe_re = probe_ref[0]
    probe_im = probe_ref[1]
    rows = []
    for pair, (row, col) in enumerate(places):
        waves = []
        for n in range(2):
            at = row * width + col // BLOCK + n
            hits = count_ref[at].astype(jnp.float32)
            far_re, far_im = halves(far_ref[pair], n)
            misfit = 2.0 * (hits * (far_re * far_re + far_im * far_im) - sum_ref[at])
            waves.append((misfit * far_re, misfit * far_im))
        rows.append(stacked(waves))
    backs = two_sided(rows, tables, 6, 4)
    rows = []
    for pair, (row, col) in enumerate(places):
        trans = [cut_pair(ext_ref, comp, row * BLOCK, col) for comp in range(2)]
        waves = []
        for n in range(2):
            back = halves(backs[pair], n)
            grad = conj_times(*halves(enter_ref[pair], n), *back)
            store(n, 2, row, col, grad[0])
            store(n, 3, row, col, grad[1])
            waves.append(conj_times(trans[0][n], trans[1][n], *back))
        rows.append(stacked(waves))
    backs = two_sided(rows, tables, 2, 0)
    for pair, (row, col) in enumerate(places):
        for n in range(2):
            grad = conj_times(probe_re, probe_im, *halves(backs[pair], n))
            store(n, 0, row, col, grad[0])
            store(n, 1, row, col, grad[1])


def shifted(low, high):
    if low is None:
        low = jnp.zeros_like(high)
    if high is None:
        high = jnp.zeros_like(low)
    return pltpu.roll(jnp.where(low_lanes(low.shape), high, low), BLOCK, 1)


def backward_rim_kernel(
    places,
    corner_ref,
    recv_ref,
    tile_ref,
    below_ref,
    right_ref,
    diag_ref,
    probe_ref,
    tables,
    far_ref,
    enter_ref,
    row_ref,
    col_ref,
    out_right_ref,
    out_below_ref,
    out_diag_ref,
    ext_ref,
    sum_ref,
    count_ref,
    even_ref,
    odd_ref,
    even_side_ref,
    odd_side_ref,
    sems,
):
    rows, cols = tile_ref.shape[1:]
    last = rows // BLOCK - 1
    copies = start_copies(
        extended_parts(tile_ref, below_ref, right_ref, diag_ref, ext_ref, 2), sems
    )
    gather_sums(corner_ref, recv_ref, sum_ref, count_ref)
    wait_copies(copies)
    bands = (even_ref, odd_ref)
    sides = (even_side_ref, odd_side_ref)

    def store(n, comp, row, col, value):
        if row == last:
            bands[n][comp, :, col : col + SIDE] = value
        else:
            at = row * BLOCK
            top = value[:BLOCK]
            if row > 0:
                top = top + sides[n][comp, at : at + BLOCK]
            sides[n][comp, at : at + BLOCK] = top
            sides[n][comp, at + BLOCK : at + SIDE] = value[BLOCK:]

    backward_pairs(
        places,
        cols // BLOCK,
        probe_ref,
        tables,
        far_ref,
        enter_ref,
        ext_ref,
        sum_ref,
        count_ref,
        store,
    )
    for comp in range(4):
        odd_side = odd_side_ref[comp]
        col_ref[comp] = even_side_ref[comp] + shifted(None, odd_side)
        side = shifted(odd_side, None)
        for out_ref, rim_ref, part in (
            (row_ref, None, slice(0, BLOCK)),
            (out_below_ref, out_diag_ref, slice(BLOCK, SIDE)),
        ):
            before = None
            for col in range(0, cols, SIDE):
                here = odd_ref[comp, part, col : col + SIDE]
                out_ref[comp, :, col : col + SIDE] = even_ref[
                    comp, part, col : col + SIDE
                ] + shifted(before, here)
                before = here
            beyond = shifted(before, None)
            if rim_ref is None:
                out_right_ref[comp, : rows - BLOCK] = side[: rows - BLOCK]
                out_right_ref[comp, rows - BLOCK :] = side[rows - BLOCK :] + beyond
            else:
                rim_ref[comp] = beyond


def backward_inner_kernel(
    places,
    corner_ref,
    recv_ref,
    tile_ref,
    probe_ref,
    tables,
    far_ref,
    enter_ref,
    row_ref,
    col_ref,
    out_ref,
    sum_ref,
    count_ref,
    even_ref,
    odd_ref,
):
    rows, cols = out_ref.shape[1:]
    last = rows - BLOCK
    gather_sums(corner_ref, recv_ref, sum_ref, count_ref)
    acc = (even_ref, odd_ref)

    def store(n, comp, row, col, value):
        at = row * BLOCK
        lanes = slice(col, col + SIDE)
        top = value[:BLOCK]
        if row > 0:
            top = top + acc[n][comp, at : at + BLOCK, lanes]
        acc[n][comp, at : at + BLOCK, lanes] = top
        acc[n][comp, at + BLOCK : at + SIDE, lanes] = value[BLOCK:]

    backward_pairs(
        places,
        cols // BLOCK,
        probe_ref,
        tables,
        far_ref,
        enter_ref,
        tile_ref.at[pl.ds(2, 2)],
        sum_ref,
        count_ref,
        store,
    )
    for comp in range(4):
        before = None
        for col in range(0, cols, SIDE):
            lanes = slice(col, col + SIDE)
            if col < cols - SIDE:
                here = odd_ref[comp, :, lanes]
                value = even_ref[comp, :, lanes] + shifted(before, here)
                before = here
            else:
                value = col_ref[comp] + shifted(before, None)
            out_ref[comp, :last, lanes] = value[:last]
            out_ref[comp, last:, lanes] = value[last:] + row_ref[comp, :, lanes]


def backward_rim(places, corner, recv, tile, below, right, diag, probe, tables, far, enter):
    comps, rows, cols = tile.shape
    corners = (rows // BLOCK) * (cols // BLOCK)
    shapes = (
        (comps, BLOCK, cols),
        (comps, rows, SIDE),
        (comps, rows, SIDE),
        (comps, BLOCK, cols),
        (comps, BLOCK, SIDE),
    )
    return pl.pallas_call(
        functools.partial(backward_rim_kernel, places),
        out_shape=tuple(jax.ShapeDtypeStruct(shape, jnp.float32) for shape in shapes),
        in_specs=[pl.BlockSpec(memory_space=pltpu.SMEM)] + in_vmem(1) + anywhere(4) + in_vmem(4),
        out_specs=tuple(in_vmem(5)),
        scratch_shapes=[
            extended_shape(tile, 2),
            pltpu.VMEM((corners, SIDE, SIDE), jnp.float32),
            pltpu.SMEM((corners,), jnp.int32),
            pltpu.VMEM((comps, SIDE, cols), jnp.float32),
            pltpu.VMEM((comps, SIDE, cols), jnp.float32),
            pltpu.VMEM((comps, rows, SIDE), jnp.float32),
            pltpu.VMEM((comps, rows, SIDE), jnp.float32),
            pltpu.SemaphoreType.DMA((4,)),
        ],
        compiler_params=pltpu.CompilerParams(vmem_limit_bytes=VMEM_LIMIT),
        cost_estimate=stage_cost(len(places)),
        name="backward_rim",
    )(corner, recv, tile, below, right, diag, probe, tables, far, enter)


def backward_inner(places, corner, recv, tile, probe, tables, far, enter, row, col):
    comps, rows, cols = tile.shape
    corners = (rows // BLOCK) * (cols // BLOCK)
    return pl.pallas_call(
        functools.partial(backward_inner_kernel, places),
        out_shape=jax.ShapeDtypeStruct(tile.shape, jnp.float32),
        in_specs=[pl.BlockSpec(memory_space=pltpu.SMEM)] + in_vmem(8),
        out_specs=pl.BlockSpec(memory_space=pltpu.VMEM),
        scratch_shapes=[
            pltpu.VMEM((corners, SIDE, SIDE), jnp.float32),
            pltpu.SMEM((corners,), jnp.int32),
            pltpu.VMEM((comps, rows, cols - SIDE), jnp.float32),
            pltpu.VMEM((comps, rows, cols - SIDE), jnp.float32),
        ],
        compiler_params=pltpu.CompilerParams(vmem_limit_bytes=VMEM_LIMIT),
        cost_estimate=stage_cost(8 * len(places)),
        name="backward_inner",
    )(corner, recv, tile, probe, tables, far, enter, row, col)


def border_kernel(own_ref, above_ref, left_ref, diag_ref, out_ref, top_ref, side_ref, sems):
    comps, rows, cols = out_ref.shape
    top = out_ref.at[:, pl.ds(0, BLOCK)]
    side = out_ref.at[:, pl.ds(BLOCK, rows - BLOCK), pl.ds(0, SIDE)]
    loads = [
        pltpu.make_async_copy(top, top_ref, sems.at[0]),
        pltpu.make_async_copy(side, side_ref, sems.at[1]),
    ]
    for copy in loads:
        copy.start()
    for copy in loads:
        copy.wait()
    top_ref[...] = top_ref[...] + above_ref[...]
    top_ref[:, :, :SIDE] = top_ref[:, :, :SIDE] + left_ref[:, :BLOCK] + diag_ref[...]
    side_ref[...] = side_ref[...] + left_ref[:, BLOCK:]
    stores = [
        pltpu.make_async_copy(top_ref, top, sems.at[0]),
        pltpu.make_async_copy(side_ref, side, sems.at[1]),
    ]
    for copy in stores:
        copy.start()
    for copy in stores:
        copy.wait()


def add_borders(own, above, left, diag):
    comps, rows, cols = own.shape
    vmem = pl.BlockSpec(memory_space=pltpu.VMEM)
    return pl.pallas_call(
        border_kernel,
        out_shape=jax.ShapeDtypeStruct(own.shape, jnp.float32),
        in_specs=[pl.BlockSpec(memory_space=pl.ANY), vmem, vmem, vmem],
        out_specs=pl.BlockSpec(memory_space=pl.ANY),
        scratch_shapes=[
            pltpu.VMEM((comps, BLOCK, cols), jnp.float32),
            pltpu.VMEM((comps, rows - BLOCK, SIDE), jnp.float32),
            pltpu.SemaphoreType.DMA((2,)),
        ],
        input_output_aliases={0: 0},
        compiler_params=pltpu.CompilerParams(vmem_limit_bytes=VMEM_LIMIT),
        name="add_borders",
    )(own, above, left, diag)


def moved(shard, down, across):
    row_total = lax.axis_size("row")
    col_total = lax.axis_size("col")
    if across == 0:
        pairs = [(r, r + down) for r in range(row_total) if 0 <= r + down < row_total]
        return lax.ppermute(shard, "row", pairs)
    if down == 0:
        pairs = [(c, c + across) for c in range(col_total) if 0 <= c + across < col_total]
        return lax.ppermute(shard, "col", pairs)
    pairs = [
        (r * col_total + c, (r + down) * col_total + c + across)
        for r in range(row_total)
        for c in range(col_total)
        if 0 <= r + down < row_total and 0 <= c + across < col_total
    ]
    return lax.ppermute(shard, ("row", "col"), pairs)


def body(object_slices, probe, measured, offsets):
    slices, parts, tile_rows, tile_cols = object_slices.shape
    tile = object_slices.reshape(slices * parts, tile_rows, tile_cols)
    row_total = lax.axis_size("row")
    tables = jnp.asarray(TABLES)
    send = pack(offsets, measured, row_total)
    recv = lax.all_to_all(send, "row", split_axis=0, concat_axis=0, tiled=True)
    below = moved(tile[:, :BLOCK, :], -1, 0)
    right = moved(tile[:, :, :SIDE], 0, -1)
    diag = moved(tile[:, :BLOCK, :SIDE], -1, -1)
    rim, inner = pair_places(tile_rows, tile_cols)
    far_inner, enter_inner = forward_inner(inner, tile, probe, tables)
    far_rim, enter_rim = forward_rim(rim, tile, below, right, diag, probe, tables)
    corner = recv[:, CAP * SIDE : CAP * SIDE + CAP, 0].astype(jnp.int32)
    row, col, to_right, to_below, to_diag = backward_rim(
        rim, corner, recv, tile, below, right, diag, probe, tables, far_rim, enter_rim
    )
    above = moved(to_below, 1, 0)
    left = moved(to_right, 0, 1)
    corner_part = moved(to_diag, 1, 1)
    own = backward_inner(
        inner, corner, recv, tile, probe, tables, far_inner, enter_inner, row, col
    )
    result = add_borders(own, above, left, corner_part)
    return result.reshape(object_slices.shape)


def solution(mesh):
    placed = (
        P(None, None, "row", "col"),
        P(),
        P(("row", "col"), None, None),
        P(None, ("row", "col")),
    )
    return jax.shard_map(
        body, mesh=mesh, in_specs=placed, out_specs=P(None, None, "row", "col"), check_vma=False
    )
```

```python
import functools
import math

import jax
import jax.numpy as jnp
import ml_dtypes
import numpy as np
from jax import lax
from jax.experimental import pallas as pl
from jax.experimental.pallas import tpu as pltpu
from jax.sharding import PartitionSpec as P

PHASE = 40.0
SIDE = 128
BLOCK = 64
CAP = 2
META = 8
VMEM_LIMIT = 28 * 1024 * 1024


def dft_matrix():
    index = np.arange(SIDE)
    angle = (index[:, None] * index[None, :] % SIDE) * (-2.0 * math.pi / SIDE)
    return np.exp(1j * angle) / math.sqrt(SIDE)


def propagation_matrix():
    index = np.arange(SIDE)
    freq = np.where(index < SIDE // 2, index, index - SIDE) / SIDE
    dft = dft_matrix()
    return np.conj(dft) @ (np.exp(-1j * PHASE * freq * freq)[:, None] * dft)


def real_forms(matrix):
    right = np.block([[matrix.real, matrix.imag], [-matrix.imag, matrix.real]])
    out = []
    for form in (right, right.T):
        form = form.astype(np.float32)
        high = form.astype(ml_dtypes.bfloat16)
        out.append(high)
        out.append((form - high.astype(np.float32)).astype(ml_dtypes.bfloat16))
    return np.stack(out)


TABLES = np.concatenate([real_forms(propagation_matrix()), real_forms(dft_matrix())])


def split(field):
    high = field.astype(jnp.bfloat16)
    low = (field - high.astype(jnp.float32)).astype(jnp.bfloat16)
    return high, low


def from_right(rows, tables, at):
    high, low = split(rows)
    left = jnp.concatenate([high, low, high], axis=1)
    right = jnp.concatenate([tables[at], tables[at], tables[at + 1]], axis=0)
    return jnp.dot(left, right, preferred_element_type=jnp.float32)


def from_left(columns, tables, at):
    high, low = split(columns)
    left = jnp.concatenate([tables[at], tables[at], tables[at + 1]], axis=1)
    right = jnp.concatenate([high, low, high], axis=0)
    return jnp.dot(left, right, preferred_element_type=jnp.float32)


def swap(pair):
    top = jnp.concatenate([pair[:SIDE, :SIDE], pair[SIDE:, :SIDE]], axis=1)
    bottom = jnp.concatenate([pair[:SIDE, SIDE:], pair[SIDE:, SIDE:]], axis=1)
    return jnp.concatenate([top, bottom], axis=0)


def two_sided(pairs, tables, right_at, left_at):
    pairs = [from_right(rows, tables, right_at) for rows in pairs]
    return [from_left(swap(rows), tables, left_at) for rows in pairs]


def stacked(fields):
    return jnp.concatenate([jnp.concatenate(field, axis=1) for field in fields], axis=0)


def halves(pair, n):
    return pair[:SIDE, n * SIDE : (n + 1) * SIDE], pair[SIDE:, n * SIDE : (n + 1) * SIDE]


def low_lanes(shape):
    return lax.broadcasted_iota(jnp.int32, shape, len(shape) - 1) < BLOCK


def cut_pair(ext_ref, comp, row, col):
    first = ext_ref[comp, row : row + SIDE, col : col + SIDE]
    second = ext_ref[comp, row : row + SIDE, col + SIDE : col + 2 * SIDE]
    mixed = jnp.where(low_lanes(first.shape), second, first)
    return first, pltpu.roll(mixed, BLOCK, 1)


def times(left_re, left_im, right_re, right_im):
    return (left_re * right_re - left_im * right_im, left_re * right_im + left_im * right_re)


def conj_times(left_re, left_im, right_re, right_im):
    return (left_re * right_re + left_im * right_im, left_re * right_im - left_im * right_re)


def pack_kernel(off_ref, meas_ref, send_ref, meta_ref, count_ref, corner_ref, sems):
    owners = send_ref.shape[0]
    positions = meas_ref.shape[0]
    for owner in range(owners):
        count_ref[owner] = 0
        for rank in range(CAP):
            corner_ref[owner * CAP + rank] = -1
    copies = []
    for pos in range(positions):
        y = off_ref[0, pos]
        x = off_ref[1, pos]
        owner = lax.shift_right_logical(y, 8)
        rank = jnp.minimum(count_ref[owner], CAP - 1)
        count_ref[owner] = rank + 1
        corner = (lax.shift_right_logical(y, 6) & 3) * 8 + (lax.shift_right_logical(x, 6) & 7)
        corner_ref[owner * CAP + rank] = corner
        copy = pltpu.make_async_copy(
            meas_ref.at[pos],
            send_ref.at[owner, pl.ds(pl.multiple_of(rank * SIDE, SIDE), SIDE)],
            sems.at[pos],
        )
        copy.start()
        copies.append(copy)
    first = low_lanes((META, SIDE))
    for owner in range(owners):
        both = jnp.where(first, corner_ref[owner * CAP], corner_ref[owner * CAP + 1])
        meta_ref[owner] = both.astype(jnp.float32)
    copy = pltpu.make_async_copy(
        meta_ref, send_ref.at[:, pl.ds(CAP * SIDE, META)], sems.at[positions]
    )
    copy.start()
    copies.append(copy)
    for copy in copies:
        copy.wait()


def pack(offsets, measured, owners):
    positions = measured.shape[0]
    return pl.pallas_call(
        pack_kernel,
        out_shape=jax.ShapeDtypeStruct((owners, CAP * SIDE + META, SIDE), jnp.float32),
        in_specs=[
            pl.BlockSpec(memory_space=pltpu.SMEM),
            pl.BlockSpec(memory_space=pltpu.VMEM),
        ],
        out_specs=pl.BlockSpec(memory_space=pl.ANY),
        scratch_shapes=[
            pltpu.VMEM((owners, META, SIDE), jnp.float32),
            pltpu.SMEM((owners,), jnp.int32),
            pltpu.SMEM((owners * CAP,), jnp.int32),
            pltpu.SemaphoreType.DMA((positions + 1,)),
        ],
        cost_estimate=pl.CostEstimate(
            flops=0, bytes_accessed=40 * 1024 * 1024, transcendentals=0
        ),
        name="pack_measured",
    )(offsets, measured)


def pair_places(rows, cols):
    row_blocks = rows // BLOCK
    edge = cols - SIDE
    last = tuple((row_blocks - 1, col) for col in range(0, cols, SIDE))
    side = tuple((row, edge) for row in range(row_blocks - 1))
    inner = tuple((row, col) for row in range(row_blocks - 1) for col in range(0, edge, SIDE))
    return last, side, inner


def forward_pairs(places, ext_ref, probe_ref, tables, far_refs, enter_refs):
    probe_re = probe_ref[0]
    probe_im = probe_ref[1]
    rows = []
    for row, col in places:
        trans = [cut_pair(ext_ref, comp, row * BLOCK, col) for comp in range(2)]
        rows.append(
            stacked([times(probe_re, probe_im, trans[0][n], trans[1][n]) for n in range(2)])
        )
    enters = two_sided(rows, tables, 0, 2)
    rows = []
    for pair, (row, col) in enumerate(places):
        enter = enters[pair]
        enter_refs[pair][...] = enter
        trans = [cut_pair(ext_ref, comp, row * BLOCK, col) for comp in range(2, 4)]
        rows.append(
            stacked([times(*halves(enter, n), trans[0][n], trans[1][n]) for n in range(2)])
        )
    fars = two_sided(rows, tables, 4, 6)
    for far_ref, far in zip(far_refs, fars):
        far_ref[...] = far


def each(ref):
    return [ref.at[pair] for pair in range(ref.shape[0])]


def extended_parts(tile_ref, below_ref, right_ref, diag_ref, ext_ref, first):
    rows, cols = tile_ref.shape[1:]
    comps = pl.ds(first, tile_ref.shape[0] - first)
    return [
        (tile_ref.at[comps], ext_ref.at[:, pl.ds(0, rows), pl.ds(0, cols)]),
        (below_ref.at[comps], ext_ref.at[:, pl.ds(rows, BLOCK), pl.ds(0, cols)]),
        (right_ref.at[comps], ext_ref.at[:, pl.ds(0, rows), pl.ds(cols, SIDE)]),
        (diag_ref.at[comps], ext_ref.at[:, pl.ds(rows, BLOCK), pl.ds(cols, SIDE)]),
    ]


def start_copies(parts, sems):
    copies = [
        pltpu.make_async_copy(source, target, sems.at[n])
        for n, (source, target) in enumerate(parts)
    ]
    for copy in copies:
        copy.start()
    return copies


def wait_copies(copies):
    for copy in copies:
        copy.wait()


def forward_inner_kernel(places, tile_ref, probe_ref, tables, far_ref, enter_ref):
    forward_pairs(places, tile_ref, probe_ref, tables, each(far_ref), each(enter_ref))


def forward_rim_kernel(
    places,
    tile_ref,
    below_ref,
    right_ref,
    diag_ref,
    probe_ref,
    tables,
    far_last_ref,
    enter_last_ref,
    far_side_ref,
    enter_side_ref,
    ext_ref,
    sems,
):
    wait_copies(
        start_copies(
            extended_parts(tile_ref, below_ref, right_ref, diag_ref, ext_ref, 0), sems
        )
    )
    forward_pairs(
        places,
        ext_ref,
        probe_ref,
        tables,
        each(far_last_ref) + each(far_side_ref),
        each(enter_last_ref) + each(enter_side_ref),
    )


def stage_cost(pairs):
    return pl.CostEstimate(
        flops=pairs * 4 * 3 * 2 * 256**3, bytes_accessed=1024 * 1024, transcendentals=0
    )


def fields(places):
    field = jax.ShapeDtypeStruct((len(places), 2 * SIDE, 2 * SIDE), jnp.float32)
    return field, field


def in_vmem(count):
    return [pl.BlockSpec(memory_space=pltpu.VMEM)] * count


def anywhere(count):
    return [pl.BlockSpec(memory_space=pl.ANY)] * count


def forward_inner(places, tile, probe, tables):
    return pl.pallas_call(
        functools.partial(forward_inner_kernel, places),
        out_shape=fields(places),
        in_specs=in_vmem(3),
        out_specs=tuple(in_vmem(2)),
        compiler_params=pltpu.CompilerParams(vmem_limit_bytes=VMEM_LIMIT),
        cost_estimate=stage_cost(8 * len(places)),
        name="forward_inner",
    )(tile, probe, tables)


def extended_shape(tile, comps):
    return pltpu.VMEM((comps, tile.shape[1] + BLOCK, tile.shape[2] + SIDE), jnp.float32)


def forward_rim(last, side, tile, below, right, diag, probe, tables):
    places = last + side
    return pl.pallas_call(
        functools.partial(forward_rim_kernel, places),
        out_shape=fields(last) + fields(side),
        in_specs=anywhere(4) + in_vmem(2),
        out_specs=tuple(in_vmem(4)),
        scratch_shapes=[extended_shape(tile, tile.shape[0]), pltpu.SemaphoreType.DMA((4,))],
        compiler_params=pltpu.CompilerParams(vmem_limit_bytes=VMEM_LIMIT),
        cost_estimate=stage_cost(8 * len(places)),
        name="forward_rim",
    )(tile, below, right, diag, probe, tables)


def gather_sums(corner_ref, recv_ref, sum_ref, count_ref, first):
    corners = sum_ref.shape[0]
    sum_ref[...] = jnp.zeros_like(sum_ref)
    for corner in range(corners):
        count_ref[corner] = 0
    for source in range(recv_ref.shape[0]):
        for rank in range(CAP):
            at = corner_ref[source, rank] - first

            @pl.when(jnp.logical_and(at >= 0, at < corners))
            def _():
                count_ref[at] = count_ref[at] + 1
                sum_ref[at] = sum_ref[at] + recv_ref[source, rank * SIDE : (rank + 1) * SIDE]


def backward_pairs(
    places, corner_of, probe_ref, tables, far_ref, enter_ref, ext_ref, sum_ref, count_ref, store
):
    probe_re = probe_ref[0]
    probe_im = probe_ref[1]
    rows = []
    for pair, (row, col) in enumerate(places):
        waves = []
        for n in range(2):
            at = corner_of(row, col) + n
            hits = count_ref[at].astype(jnp.float32)
            far_re, far_im = halves(far_ref[pair], n)
            misfit = 2.0 * (hits * (far_re * far_re + far_im * far_im) - sum_ref[at])
            waves.append((misfit * far_re, misfit * far_im))
        rows.append(stacked(waves))
    backs = two_sided(rows, tables, 6, 4)
    rows = []
    for pair, (row, col) in enumerate(places):
        trans = [cut_pair(ext_ref, comp, row * BLOCK, col) for comp in range(2)]
        waves = []
        for n in range(2):
            back = halves(backs[pair], n)
            grad = conj_times(*halves(enter_ref[pair], n), *back)
            store(n, 2, row, col, grad[0])
            store(n, 3, row, col, grad[1])
            waves.append(conj_times(trans[0][n], trans[1][n], *back))
        rows.append(stacked(waves))
    backs = two_sided(rows, tables, 2, 0)
    for pair, (row, col) in enumerate(places):
        for n in range(2):
            grad = conj_times(probe_re, probe_im, *halves(backs[pair], n))
            store(n, 0, row, col, grad[0])
            store(n, 1, row, col, grad[1])


def shifted(low, high):
    if low is None:
        low = jnp.zeros_like(high)
    if high is None:
        high = jnp.zeros_like(low)
    return pltpu.roll(jnp.where(low_lanes(low.shape), high, low), BLOCK, 1)


def backward_last_kernel(
    places,
    recv_ref,
    tile_ref,
    below_ref,
    right_ref,
    diag_ref,
    probe_ref,
    tables_ref,
    far_ref,
    enter_ref,
    row_ref,
    right_part_ref,
    out_below_ref,
    out_diag_ref,
    corner_ref,
    items_ref,
    table_buf,
    probe_buf,
    far_buf,
    enter_buf,
    ext_ref,
    sum_ref,
    count_ref,
    meta_ref,
    even_ref,
    odd_ref,
    sems,
):
    rows, cols = tile_ref.shape[1:]
    corners = sum_ref.shape[0]
    start = rows - BLOCK
    two = pl.ds(2, 2)
    above = pl.ds(0, BLOCK)
    under = pl.ds(BLOCK, BLOCK)
    wide = pl.ds(0, cols)
    beyond = pl.ds(cols, SIDE)
    low = pl.ds(start, BLOCK)
    copies = start_copies(
        [
            (recv_ref.at[:, CAP * SIDE], meta_ref),
            (recv_ref.at[:, pl.ds(0, CAP * SIDE)], items_ref),
            (far_ref, far_buf),
            (tables_ref, table_buf),
            (tile_ref.at[two, low], ext_ref.at[:, above, wide]),
            (below_ref.at[two], ext_ref.at[:, under, wide]),
            (right_ref.at[two, low], ext_ref.at[:, above, beyond]),
            (diag_ref.at[two], ext_ref.at[:, under, beyond]),
            (enter_ref, enter_buf),
            (probe_ref, probe_buf),
        ],
        sems,
    )
    wait_copies(copies[:1])
    for source in range(corner_ref.shape[0]):
        for rank in range(CAP):
            corner_ref[source, rank] = meta_ref[source, rank * BLOCK].astype(jnp.int32)
    wait_copies(copies[1:2])
    gather_sums(corner_ref, items_ref, sum_ref, count_ref, start // BLOCK * corners)
    wait_copies(copies[2:])
    bands = (even_ref, odd_ref)

    def store(n, comp, row, col, value):
        bands[n][comp, :, col : col + SIDE] = value

    backward_pairs(
        [(0, col) for _, col in places],
        lambda row, col: col // BLOCK,
        probe_buf,
        table_buf,
        far_buf,
        enter_buf,
        ext_ref,
        sum_ref,
        count_ref,
        store,
    )
    for comp in range(4):
        for out_ref, side_ref, part in (
            (row_ref, right_part_ref, slice(0, BLOCK)),
            (out_below_ref, out_diag_ref, slice(BLOCK, SIDE)),
        ):
            before = None
            for col in range(0, cols, SIDE):
                here = odd_ref[comp, part, col : col + SIDE]
                out_ref[comp, :, col : col + SIDE] = even_ref[
                    comp, part, col : col + SIDE
                ] + shifted(before, here)
                before = here
            side_ref[comp] = shifted(before, None)


def backward_side_kernel(
    places,
    corner_ref,
    recv_ref,
    tile_ref,
    right_ref,
    probe_ref,
    tables,
    far_ref,
    enter_ref,
    right_part_ref,
    col_ref,
    out_right_ref,
    sum_ref,
    count_ref,
    ext_ref,
    even_ref,
    odd_ref,
    sems,
):
    rows, cols = tile_ref.shape[1:]
    edge = cols - SIDE
    last = rows - BLOCK
    width = cols // BLOCK
    two = pl.ds(2, 2)
    copies = start_copies(
        [
            (tile_ref.at[two, :, pl.ds(edge, SIDE)], ext_ref.at[:, :, pl.ds(0, SIDE)]),
            (right_ref.at[two], ext_ref.at[:, :, pl.ds(SIDE, SIDE)]),
        ],
        sems,
    )
    gather_sums(corner_ref, recv_ref, sum_ref, count_ref, 0)
    wait_copies(copies)
    acc = (even_ref, odd_ref)

    def store(n, comp, row, col, value):
        at = row * BLOCK
        top = value[:BLOCK]
        if row > 0:
            top = top + acc[n][comp, at : at + BLOCK]
        acc[n][comp, at : at + BLOCK] = top
        acc[n][comp, at + BLOCK : at + SIDE] = value[BLOCK:]

    backward_pairs(
        [(row, 0) for row, _ in places],
        lambda row, col: row * width + edge // BLOCK,
        probe_ref,
        tables,
        far_ref,
        enter_ref,
        ext_ref,
        sum_ref,
        count_ref,
        store,
    )
    half = rows // 2
    for comp in range(4):
        col_ref[comp] = even_ref[comp] + shifted(None, odd_ref[comp])
        side = shifted(odd_ref[comp], None)
        first = side[:half]
        second = jnp.concatenate(
            [side[half:last], side[last:] + right_part_ref[comp]], axis=0
        )
        out_right_ref[comp] = first + pltpu.roll(second, BLOCK, 1)


def backward_inner_kernel(
    places,
    count_ref,
    sum_ref,
    tile_ref,
    probe_ref,
    tables,
    far_ref,
    enter_ref,
    row_ref,
    col_ref,
    out_ref,
    even_ref,
    odd_ref,
):
    rows, cols = out_ref.shape[1:]
    last = rows - BLOCK
    width = cols // BLOCK
    acc = (even_ref, odd_ref)

    def store(n, comp, row, col, value):
        at = row * BLOCK
        lanes = slice(col, col + SIDE)
        top = value[:BLOCK]
        if row > 0:
            top = top + acc[n][comp, at : at + BLOCK, lanes]
        acc[n][comp, at : at + BLOCK, lanes] = top
        acc[n][comp, at + BLOCK : at + SIDE, lanes] = value[BLOCK:]

    backward_pairs(
        places,
        lambda row, col: row * width + col // BLOCK,
        probe_ref,
        tables,
        far_ref,
        enter_ref,
        tile_ref.at[pl.ds(2, 2)],
        sum_ref,
        count_ref,
        store,
    )
    for comp in range(4):
        before = None
        for col in range(0, cols, SIDE):
            lanes = slice(col, col + SIDE)
            if col < cols - SIDE:
                here = odd_ref[comp, :, lanes]
                value = even_ref[comp, :, lanes] + shifted(before, here)
                before = here
            else:
                value = col_ref[comp] + shifted(before, None)
            out_ref[comp, :last, lanes] = value[:last]
            out_ref[comp, last:, lanes] = value[last:] + row_ref[comp, :, lanes]


def shapes_of(*shapes):
    return tuple(jax.ShapeDtypeStruct(shape, jnp.float32) for shape in shapes)


def backward_last(places, recv, tile, below, right, diag, probe, tables, far, enter):
    comps, rows, cols = tile.shape
    corners = cols // BLOCK
    sources = recv.shape[0]
    edge = (comps, BLOCK, cols)
    side = (comps, BLOCK, SIDE)
    return pl.pallas_call(
        functools.partial(backward_last_kernel, places),
        out_shape=shapes_of(edge, side, edge, side)
        + (jax.ShapeDtypeStruct((sources, CAP), jnp.int32),),
        in_specs=anywhere(9),
        out_specs=tuple(in_vmem(4)) + (pl.BlockSpec(memory_space=pltpu.SMEM),),
        scratch_shapes=[
            pltpu.VMEM((sources, CAP * SIDE, SIDE), jnp.float32),
            pltpu.VMEM(tables.shape, tables.dtype),
            pltpu.VMEM(probe.shape, jnp.float32),
            pltpu.VMEM(far.shape, jnp.float32),
            pltpu.VMEM(enter.shape, jnp.float32),
            pltpu.VMEM((2, SIDE, cols + SIDE), jnp.float32),
            pltpu.VMEM((corners, SIDE, SIDE), jnp.float32),
            pltpu.SMEM((corners,), jnp.int32),
            pltpu.SMEM((sources, SIDE), jnp.float32),
            pltpu.VMEM((comps, SIDE, cols), jnp.float32),
            pltpu.VMEM((comps, SIDE, cols), jnp.float32),
            pltpu.SemaphoreType.DMA((10,)),
        ],
        compiler_params=pltpu.CompilerParams(vmem_limit_bytes=VMEM_LIMIT),
        cost_estimate=stage_cost(len(places)),
        name="backward_last_row",
    )(recv, tile, below, right, diag, probe, tables, far, enter)


def backward_side(places, corner, recv, tile, right, probe, tables, far, enter, right_part):
    comps, rows, cols = tile.shape
    corners = (rows // BLOCK - 1) * (cols // BLOCK)
    return pl.pallas_call(
        functools.partial(backward_side_kernel, places),
        out_shape=shapes_of(
            (comps, rows, SIDE), (comps, rows // 2, SIDE), (corners, SIDE, SIDE)
        )
        + (jax.ShapeDtypeStruct((corners,), jnp.int32),),
        in_specs=[pl.BlockSpec(memory_space=pltpu.SMEM)]
        + in_vmem(1)
        + anywhere(2)
        + in_vmem(5),
        out_specs=tuple(in_vmem(3)) + (pl.BlockSpec(memory_space=pltpu.SMEM),),
        scratch_shapes=[
            pltpu.VMEM((2, rows, 2 * SIDE), jnp.float32),
            pltpu.VMEM((comps, rows, SIDE), jnp.float32),
            pltpu.VMEM((comps, rows, SIDE), jnp.float32),
            pltpu.SemaphoreType.DMA((2,)),
        ],
        compiler_params=pltpu.CompilerParams(vmem_limit_bytes=VMEM_LIMIT),
        cost_estimate=stage_cost(8 * len(places)),
        name="backward_last_column",
    )(corner, recv, tile, right, probe, tables, far, enter, right_part)


def backward_inner(places, count, sums, tile, probe, tables, far, enter, row, col):
    comps, rows, cols = tile.shape
    return pl.pallas_call(
        functools.partial(backward_inner_kernel, places),
        out_shape=jax.ShapeDtypeStruct(tile.shape, jnp.float32),
        in_specs=[pl.BlockSpec(memory_space=pltpu.SMEM)] + in_vmem(8),
        out_specs=pl.BlockSpec(memory_space=pltpu.VMEM),
        scratch_shapes=[
            pltpu.VMEM((comps, rows, cols - SIDE), jnp.float32),
            pltpu.VMEM((comps, rows, cols - SIDE), jnp.float32),
        ],
        compiler_params=pltpu.CompilerParams(vmem_limit_bytes=VMEM_LIMIT),
        cost_estimate=stage_cost(len(places)),
        name="backward_inner",
    )(count, sums, tile, probe, tables, far, enter, row, col)


def border_kernel(
    own_ref, above_ref, left_ref, diag_ref, out_ref, top_ref, side_ref, row_buf, col_buf, diag_buf, sems
):
    rows = out_ref.shape[1]
    half = rows // 2
    top = out_ref.at[:, pl.ds(0, BLOCK)]
    side = out_ref.at[:, pl.ds(BLOCK, rows - BLOCK), pl.ds(0, SIDE)]
    loads = start_copies(
        [
            (above_ref, row_buf),
            (top, top_ref),
            (left_ref, col_buf),
            (diag_ref, diag_buf),
            (side, side_ref),
        ],
        sems,
    )
    wait_copies(loads)
    left = col_buf[...]
    low = low_lanes(left.shape)
    upper = jnp.where(low, left, 0.0)
    lower = pltpu.roll(jnp.where(low, 0.0, left), BLOCK, 2)
    top_ref[...] = top_ref[...] + row_buf[...]
    top_ref[:, :, :SIDE] = top_ref[:, :, :SIDE] + upper[:, :BLOCK] + diag_buf[...]
    stores = start_copies([(top_ref, top)], sems)
    side_ref[:, : half - BLOCK] = side_ref[:, : half - BLOCK] + upper[:, BLOCK:]
    side_ref[:, half - BLOCK :] = side_ref[:, half - BLOCK :] + lower
    stores += start_copies([(side_ref, side)], sems.at[pl.ds(1, 1)])
    wait_copies(stores)


def add_borders(own, above, left, diag):
    comps, rows, cols = own.shape
    return pl.pallas_call(
        border_kernel,
        out_shape=jax.ShapeDtypeStruct(own.shape, jnp.float32),
        in_specs=anywhere(4),
        out_specs=pl.BlockSpec(memory_space=pl.ANY),
        scratch_shapes=[
            pltpu.VMEM((comps, BLOCK, cols), jnp.float32),
            pltpu.VMEM((comps, rows - BLOCK, SIDE), jnp.float32),
            pltpu.VMEM(above.shape, jnp.float32),
            pltpu.VMEM(left.shape, jnp.float32),
            pltpu.VMEM(diag.shape, jnp.float32),
            pltpu.SemaphoreType.DMA((5,)),
        ],
        input_output_aliases={0: 0},
        compiler_params=pltpu.CompilerParams(vmem_limit_bytes=VMEM_LIMIT),
        name="add_borders",
    )(own, above, left, diag)


def strip_kernel(tile_ref, below_ref, right_ref, diag_ref, sems):
    top = pl.ds(0, BLOCK)
    left = pl.ds(0, SIDE)
    wait_copies(
        start_copies(
            [
                (tile_ref.at[:, top], below_ref),
                (tile_ref.at[:, :, left], right_ref),
                (tile_ref.at[:, top, left], diag_ref),
            ],
            sems,
        )
    )


def strips(tile):
    comps, rows, cols = tile.shape
    return pl.pallas_call(
        strip_kernel,
        out_shape=shapes_of((comps, BLOCK, cols), (comps, rows, SIDE), (comps, BLOCK, SIDE)),
        in_specs=anywhere(1),
        out_specs=tuple(in_vmem(3)),
        scratch_shapes=[pltpu.SemaphoreType.DMA((3,))],
        name="halo_strips",
    )(tile)


def moved(shard, down, across):
    row_total = lax.axis_size("row")
    col_total = lax.axis_size("col")
    if across == 0:
        pairs = [(r, r + down) for r in range(row_total) if 0 <= r + down < row_total]
        return lax.ppermute(shard, "row", pairs)
    if down == 0:
        pairs = [(c, c + across) for c in range(col_total) if 0 <= c + across < col_total]
        return lax.ppermute(shard, "col", pairs)
    pairs = [
        (r * col_total + c, (r + down) * col_total + c + across)
        for r in range(row_total)
        for c in range(col_total)
        if 0 <= r + down < row_total and 0 <= c + across < col_total
    ]
    return lax.ppermute(shard, ("row", "col"), pairs)


def body(object_slices, probe, measured, offsets):
    slices, parts, tile_rows, tile_cols = object_slices.shape
    tile = object_slices.reshape(slices * parts, tile_rows, tile_cols)
    row_total = lax.axis_size("row")
    tables = jnp.asarray(TABLES)
    strip_below, strip_right, strip_diag = strips(tile)
    below = moved(strip_below, -1, 0)
    right = moved(strip_right, 0, -1)
    diag = moved(strip_diag, -1, -1)
    send = pack(offsets, measured, row_total)
    recv = lax.all_to_all(send, "row", split_axis=0, concat_axis=0, tiled=True)
    last, side, inner = pair_places(tile_rows, tile_cols)
    far_inner, enter_inner = forward_inner(inner, tile, probe, tables)
    far_last, enter_last, far_side, enter_side = forward_rim(
        last, side, tile, below, right, diag, probe, tables
    )
    row, right_part, to_below, to_diag, corner = backward_last(
        last, recv, tile, below, right, diag, probe, tables, far_last, enter_last
    )
    above = moved(to_below, 1, 0)
    col, to_right, sums, count = backward_side(
        side, corner, recv, tile, right, probe, tables, far_side, enter_side, right_part
    )
    left = moved(to_right, 0, 1)
    corner_part = moved(to_diag, 1, 1)
    own = backward_inner(
        inner, count, sums, tile, probe, tables, far_inner, enter_inner, row, col
    )
    result = add_borders(own, above, left, corner_part)
    return result.reshape(object_slices.shape)


def solution(mesh):
    placed = (
        P(None, None, "row", "col"),
        P(),
        P(("row", "col"), None, None),
        P(None, ("row", "col")),
    )
    return jax.shard_map(
        body, mesh=mesh, in_specs=placed, out_specs=P(None, None, "row", "col"), check_vma=False
    )
```

```python
import functools
import math

import jax
import jax.numpy as jnp
import ml_dtypes
import numpy as np
from jax import lax
from jax.experimental import pallas as pl
from jax.experimental.pallas import tpu as pltpu
from jax.sharding import PartitionSpec as P

PHASE = 40.0
SIDE = 128
BLOCK = 64
CAP = 2
META = 8
VMEM_LIMIT = 28 * 1024 * 1024
VMEM_MOST = 60 * 1024 * 1024


def dft_matrix():
    index = np.arange(SIDE)
    angle = (index[:, None] * index[None, :] % SIDE) * (-2.0 * math.pi / SIDE)
    return np.exp(1j * angle) / math.sqrt(SIDE)


def propagation_matrix():
    index = np.arange(SIDE)
    freq = np.where(index < SIDE // 2, index, index - SIDE) / SIDE
    dft = dft_matrix()
    return np.conj(dft) @ (np.exp(-1j * PHASE * freq * freq)[:, None] * dft)


def real_forms(matrix):
    right = np.block([[matrix.real, matrix.imag], [-matrix.imag, matrix.real]])
    out = []
    for form in (right, right.T):
        form = form.astype(np.float32)
        high = form.astype(ml_dtypes.bfloat16)
        out.append(high)
        out.append((form - high.astype(np.float32)).astype(ml_dtypes.bfloat16))
    return np.stack(out)


TABLES = np.concatenate([real_forms(propagation_matrix()), real_forms(dft_matrix())])


def split(field):
    high = field.astype(jnp.bfloat16)
    low = (field - high.astype(jnp.float32)).astype(jnp.bfloat16)
    return high, low


def from_right(rows, tables, at):
    high, low = split(rows)
    left = jnp.concatenate([high, low, high], axis=1)
    right = jnp.concatenate([tables[at], tables[at], tables[at + 1]], axis=0)
    return jnp.dot(left, right, preferred_element_type=jnp.float32)


def from_left(columns, tables, at):
    high, low = split(columns)
    left = jnp.concatenate([tables[at], tables[at], tables[at + 1]], axis=1)
    right = jnp.concatenate([high, low, high], axis=0)
    return jnp.dot(left, right, preferred_element_type=jnp.float32)


def swap(pair):
    top = jnp.concatenate([pair[:SIDE, :SIDE], pair[SIDE:, :SIDE]], axis=1)
    bottom = jnp.concatenate([pair[:SIDE, SIDE:], pair[SIDE:, SIDE:]], axis=1)
    return jnp.concatenate([top, bottom], axis=0)


def two_sided(pairs, tables, right_at, left_at):
    pairs = [from_right(rows, tables, right_at) for rows in pairs]
    return [from_left(swap(rows), tables, left_at) for rows in pairs]


def stacked(fields):
    return jnp.concatenate([jnp.concatenate(field, axis=1) for field in fields], axis=0)


def halves(pair, n):
    return pair[:SIDE, n * SIDE : (n + 1) * SIDE], pair[SIDE:, n * SIDE : (n + 1) * SIDE]


def low_lanes(shape):
    return lax.broadcasted_iota(jnp.int32, shape, len(shape) - 1) < BLOCK


def cut_pair(ext_ref, comp, row, col):
    first = ext_ref[comp, row : row + SIDE, col : col + SIDE]
    second = ext_ref[comp, row : row + SIDE, col + SIDE : col + 2 * SIDE]
    mixed = jnp.where(low_lanes(first.shape), second, first)
    return first, pltpu.roll(mixed, BLOCK, 1)


def times(left_re, left_im, right_re, right_im):
    return (left_re * right_re - left_im * right_im, left_re * right_im + left_im * right_re)


def conj_times(left_re, left_im, right_re, right_im):
    return (left_re * right_re + left_im * right_im, left_re * right_im - left_im * right_re)


def pack_kernel(
    off_ref, meas_ref, tile_ref, send_ref, right_ref, diag_ref, meta_ref, count_ref, corner_ref, sems
):
    owners = send_ref.shape[0]
    positions = meas_ref.shape[0]
    left = pl.ds(0, SIDE)
    strips = start_copies(
        [
            (tile_ref.at[:, :, left], right_ref),
            (tile_ref.at[:, pl.ds(0, BLOCK), left], diag_ref),
        ],
        sems.at[pl.ds(positions + 1, 2)],
    )
    for owner in range(owners):
        count_ref[owner] = 0
        for rank in range(CAP):
            corner_ref[owner * CAP + rank] = -1
    copies = []
    for pos in range(positions):
        y = off_ref[0, pos]
        x = off_ref[1, pos]
        owner = lax.shift_right_logical(y, 8)
        rank = jnp.minimum(count_ref[owner], CAP - 1)
        count_ref[owner] = rank + 1
        corner = (lax.shift_right_logical(y, 6) & 3) * 8 + (lax.shift_right_logical(x, 6) & 7)
        corner_ref[owner * CAP + rank] = corner
        copy = pltpu.make_async_copy(
            meas_ref.at[pos],
            send_ref.at[owner, pl.ds(pl.multiple_of(rank * SIDE, SIDE), SIDE)],
            sems.at[pos],
        )
        copy.start()
        copies.append(copy)
    first = low_lanes((META, SIDE))
    for owner in range(owners):
        both = jnp.where(first, corner_ref[owner * CAP], corner_ref[owner * CAP + 1])
        meta_ref[owner] = both.astype(jnp.float32)
    copy = pltpu.make_async_copy(
        meta_ref, send_ref.at[:, pl.ds(CAP * SIDE, META)], sems.at[positions]
    )
    copy.start()
    copies.append(copy)
    wait_copies(copies + strips)


def pack(offsets, measured, tile, owners):
    positions = measured.shape[0]
    comps, rows, _ = tile.shape
    return pl.pallas_call(
        pack_kernel,
        out_shape=shapes_of(
            (owners, CAP * SIDE + META, SIDE), (comps, rows, SIDE), (comps, BLOCK, SIDE)
        ),
        in_specs=[pl.BlockSpec(memory_space=pltpu.SMEM)] + in_vmem(1) + anywhere(1),
        out_specs=tuple(anywhere(1) + in_vmem(2)),
        scratch_shapes=[
            pltpu.VMEM((owners, META, SIDE), jnp.float32),
            pltpu.SMEM((owners,), jnp.int32),
            pltpu.SMEM((owners * CAP,), jnp.int32),
            pltpu.SemaphoreType.DMA((positions + 3,)),
        ],
        cost_estimate=pl.CostEstimate(
            flops=0, bytes_accessed=40 * 1024 * 1024, transcendentals=0
        ),
        name="pack_measured",
    )(offsets, measured, tile)


def pair_places(rows, cols):
    row_blocks = rows // BLOCK
    edge = cols - SIDE
    last = tuple((row_blocks - 1, col) for col in range(0, cols, SIDE))
    side = tuple((row, edge) for row in range(row_blocks - 1))
    inner = tuple((row, col) for row in range(row_blocks - 1) for col in range(0, edge, SIDE))
    return last, side, inner


def forward_pairs(places, ext_ref, probe_ref, tables, far_refs, enter_refs):
    probe_re = probe_ref[0]
    probe_im = probe_ref[1]
    rows = []
    for row, col in places:
        trans = [cut_pair(ext_ref, comp, row * BLOCK, col) for comp in range(2)]
        rows.append(
            stacked([times(probe_re, probe_im, trans[0][n], trans[1][n]) for n in range(2)])
        )
    enters = two_sided(rows, tables, 0, 2)
    rows = []
    for pair, (row, col) in enumerate(places):
        enter = enters[pair]
        enter_refs[pair][...] = enter
        trans = [cut_pair(ext_ref, comp, row * BLOCK, col) for comp in range(2, 4)]
        rows.append(
            stacked([times(*halves(enter, n), trans[0][n], trans[1][n]) for n in range(2)])
        )
    fars = two_sided(rows, tables, 4, 6)
    for far_ref, far in zip(far_refs, fars):
        far_ref[...] = far


def each(ref):
    return [ref.at[pair] for pair in range(ref.shape[0])]


def extended_parts(tile_ref, below_ref, right_ref, diag_ref, ext_ref, first):
    rows, cols = tile_ref.shape[1:]
    comps = pl.ds(first, tile_ref.shape[0] - first)
    return [
        (tile_ref.at[comps], ext_ref.at[:, pl.ds(0, rows), pl.ds(0, cols)]),
        (below_ref.at[comps], ext_ref.at[:, pl.ds(rows, BLOCK), pl.ds(0, cols)]),
        (right_ref.at[comps], ext_ref.at[:, pl.ds(0, rows), pl.ds(cols, SIDE)]),
        (diag_ref.at[comps], ext_ref.at[:, pl.ds(rows, BLOCK), pl.ds(cols, SIDE)]),
    ]


def start_copies(parts, sems):
    copies = [
        pltpu.make_async_copy(source, target, sems.at[n])
        for n, (source, target) in enumerate(parts)
    ]
    for copy in copies:
        copy.start()
    return copies


def wait_copies(copies):
    for copy in copies:
        copy.wait()


def forward_inner_kernel(places, tile_ref, probe_ref, tables, far_ref, enter_ref):
    forward_pairs(places, tile_ref, probe_ref, tables, each(far_ref), each(enter_ref))


def forward_rim_kernel(
    places,
    tile_ref,
    below_ref,
    right_ref,
    diag_ref,
    probe_ref,
    tables,
    far_last_ref,
    enter_last_ref,
    far_side_ref,
    enter_side_ref,
    ext_ref,
    sems,
):
    wait_copies(
        start_copies(
            extended_parts(tile_ref, below_ref, right_ref, diag_ref, ext_ref, 0), sems
        )
    )
    forward_pairs(
        places,
        ext_ref,
        probe_ref,
        tables,
        each(far_last_ref) + each(far_side_ref),
        each(enter_last_ref) + each(enter_side_ref),
    )


def stage_cost(pairs):
    return pl.CostEstimate(
        flops=pairs * 4 * 3 * 2 * 256**3, bytes_accessed=1024 * 1024, transcendentals=0
    )


def fields(places):
    field = jax.ShapeDtypeStruct((len(places), 2 * SIDE, 2 * SIDE), jnp.float32)
    return field, field


def in_vmem(count):
    return [pl.BlockSpec(memory_space=pltpu.VMEM)] * count


def anywhere(count):
    return [pl.BlockSpec(memory_space=pl.ANY)] * count


def forward_inner(places, tile, probe, tables):
    return pl.pallas_call(
        functools.partial(forward_inner_kernel, places),
        out_shape=fields(places),
        in_specs=in_vmem(3),
        out_specs=tuple(in_vmem(2)),
        compiler_params=pltpu.CompilerParams(vmem_limit_bytes=VMEM_LIMIT),
        cost_estimate=stage_cost(8 * len(places)),
        name="forward_inner",
    )(tile, probe, tables)


def extended_shape(tile, comps):
    return pltpu.VMEM((comps, tile.shape[1] + BLOCK, tile.shape[2] + SIDE), jnp.float32)


def forward_rim(last, side, tile, below, right, diag, probe, tables):
    places = last + side
    return pl.pallas_call(
        functools.partial(forward_rim_kernel, places),
        out_shape=fields(last) + fields(side),
        in_specs=anywhere(4) + in_vmem(2),
        out_specs=tuple(in_vmem(4)),
        scratch_shapes=[extended_shape(tile, tile.shape[0]), pltpu.SemaphoreType.DMA((4,))],
        compiler_params=pltpu.CompilerParams(vmem_limit_bytes=VMEM_LIMIT),
        cost_estimate=stage_cost(8 * len(places)),
        name="forward_rim",
    )(tile, below, right, diag, probe, tables)


def gather_sums(meta_ref, items_ref, sum_ref, count_ref):
    spare = sum_ref.shape[0] - 1
    for corner in range(spare + 1):
        count_ref[corner] = 0
    for source in range(items_ref.shape[0]):
        for rank in range(CAP):
            corner = meta_ref[source, rank * BLOCK].astype(jnp.int32)
            at = jnp.where(corner < 0, spare, corner)
            hits = count_ref[at]
            count_ref[at] = hits + 1
            item = items_ref[source, rank * SIDE : (rank + 1) * SIDE]
            sum_ref[at] = jnp.where(hits > 0, sum_ref[at], 0.0) + item


def summed(sum_ref, count_ref, at):
    hits = count_ref[at]
    return hits.astype(jnp.float32), jnp.where(hits > 0, sum_ref[at], 0.0)


def backward_pairs(
    places,
    width,
    probe_ref,
    tables,
    far_ref,
    enter_ref,
    ext_ref,
    sum_ref,
    count_ref,
    store,
    before_fields=None,
    before_products=None,
):
    rows = []
    for pair, (row, col) in enumerate(places):
        waves = []
        for n in range(2):
            at = row * width + col // BLOCK + n
            hits, total = summed(sum_ref, count_ref, at)
            far_re, far_im = halves(far_ref[pair], n)
            misfit = 2.0 * (hits * (far_re * far_re + far_im * far_im) - total)
            waves.append((misfit * far_re, misfit * far_im))
        rows.append(stacked(waves))
    if before_products is not None:
        before_products()
    backs = two_sided(rows, tables, 6, 4)
    if before_fields is not None:
        before_fields()
    rows = []
    for pair, (row, col) in enumerate(places):
        trans = [cut_pair(ext_ref, comp, row * BLOCK, col) for comp in range(2)]
        waves = []
        for n in range(2):
            back = halves(backs[pair], n)
            grad = conj_times(*halves(enter_ref[pair], n), *back)
            store(n, 2, row, col, grad[0])
            store(n, 3, row, col, grad[1])
            waves.append(conj_times(trans[0][n], trans[1][n], *back))
        rows.append(stacked(waves))
    backs = two_sided(rows, tables, 2, 0)
    probe_re = probe_ref[0]
    probe_im = probe_ref[1]
    for pair, (row, col) in enumerate(places):
        for n in range(2):
            grad = conj_times(probe_re, probe_im, *halves(backs[pair], n))
            store(n, 0, row, col, grad[0])
            store(n, 1, row, col, grad[1])


def shifted(low, high):
    if low is None:
        low = jnp.zeros_like(high)
    if high is None:
        high = jnp.zeros_like(low)
    return pltpu.roll(jnp.where(low_lanes(low.shape), high, low), BLOCK, 1)


def backward_rim_kernel(
    places,
    recv_ref,
    tile_ref,
    below_ref,
    right_ref,
    diag_ref,
    probe_ref,
    tables_ref,
    far_last_ref,
    enter_last_ref,
    far_side_ref,
    enter_side_ref,
    row_ref,
    col_ref,
    out_below_ref,
    out_right_ref,
    out_diag_ref,
    sum_ref,
    count_ref,
    items_ref,
    meta_ref,
    table_buf,
    probe_buf,
    far_buf,
    enter_buf,
    ext_ref,
    even_ref,
    odd_ref,
    even_side_ref,
    odd_side_ref,
    sems,
):
    rows, cols = tile_ref.shape[1:]
    last = rows // BLOCK - 1
    first = pl.ds(0, far_last_ref.shape[0])
    others = pl.ds(far_last_ref.shape[0], far_side_ref.shape[0])
    copies = start_copies(
        [
            (recv_ref.at[:, CAP * SIDE], meta_ref),
            (recv_ref.at[:, pl.ds(0, CAP * SIDE)], items_ref),
            (far_last_ref, far_buf.at[first]),
            (far_side_ref, far_buf.at[others]),
            (tables_ref, table_buf),
            (enter_last_ref, enter_buf.at[first]),
            (enter_side_ref, enter_buf.at[others]),
            (probe_ref, probe_buf),
        ]
        + extended_parts(tile_ref, below_ref, right_ref, diag_ref, ext_ref, 2),
        sems,
    )
    wait_copies(copies[:2])
    gather_sums(meta_ref, items_ref, sum_ref, count_ref)
    wait_copies(copies[2:4])
    bands = (even_ref, odd_ref)
    sides = (even_side_ref, odd_side_ref)

    def store(n, comp, row, col, value):
        if row == last:
            bands[n][comp, :, col : col + SIDE] = value
        else:
            at = row * BLOCK
            top = value[:BLOCK]
            if row > 0:
                top = top + sides[n][comp, at : at + BLOCK]
            sides[n][comp, at : at + BLOCK] = top
            sides[n][comp, at + BLOCK : at + SIDE] = value[BLOCK:]

    backward_pairs(
        places,
        cols // BLOCK,
        probe_buf,
        table_buf,
        far_buf,
        enter_buf,
        ext_ref,
        sum_ref,
        count_ref,
        store,
        lambda: wait_copies(copies[5:]),
        lambda: wait_copies(copies[4:5]),
    )
    half = rows // 2
    for comp in range(4):
        beyond = []
        for out_ref, part in (
            (row_ref, slice(0, BLOCK)),
            (out_below_ref, slice(BLOCK, SIDE)),
        ):
            before = None
            for col in range(0, cols, SIDE):
                here = odd_ref[comp, part, col : col + SIDE]
                out_ref[comp, :, col : col + SIDE] = even_ref[
                    comp, part, col : col + SIDE
                ] + shifted(before, here)
                before = here
            beyond.append(shifted(before, None))
        out_diag_ref[comp] = beyond[1]
        odd_side = odd_side_ref[comp]
        col_ref[comp] = even_side_ref[comp] + shifted(None, odd_side)
        side = shifted(odd_side, None)
        second = jnp.concatenate(
            [side[half : rows - BLOCK], side[rows - BLOCK :] + beyond[0]], axis=0
        )
        out_right_ref[comp] = side[:half] + pltpu.roll(second, BLOCK, 1)


def backward_inner_kernel(
    places,
    count_ref,
    sum_ref,
    tile_ref,
    probe_ref,
    tables,
    far_ref,
    enter_ref,
    row_ref,
    col_ref,
    out_ref,
    even_ref,
    odd_ref,
):
    rows, cols = out_ref.shape[1:]
    last = rows - BLOCK
    acc = (even_ref, odd_ref)

    def store(n, comp, row, col, value):
        at = row * BLOCK
        lanes = slice(col, col + SIDE)
        top = value[:BLOCK]
        if row > 0:
            top = top + acc[n][comp, at : at + BLOCK, lanes]
        acc[n][comp, at : at + BLOCK, lanes] = top
        acc[n][comp, at + BLOCK : at + SIDE, lanes] = value[BLOCK:]

    backward_pairs(
        places,
        cols // BLOCK,
        probe_ref,
        tables,
        far_ref,
        enter_ref,
        tile_ref.at[pl.ds(2, 2)],
        sum_ref,
        count_ref,
        store,
    )
    for comp in range(4):
        before = None
        for col in range(0, cols, SIDE):
            lanes = slice(col, col + SIDE)
            if col < cols - SIDE:
                here = odd_ref[comp, :, lanes]
                value = even_ref[comp, :, lanes] + shifted(before, here)
                before = here
            else:
                value = col_ref[comp] + shifted(before, None)
            out_ref[comp, :last, lanes] = value[:last]
            out_ref[comp, last:, lanes] = value[last:] + row_ref[comp, :, lanes]


def shapes_of(*shapes):
    return tuple(jax.ShapeDtypeStruct(shape, jnp.float32) for shape in shapes)


def backward_rim(recv, tile, below, right, diag, probe, tables, fields_last, fields_side, places):
    comps, rows, cols = tile.shape
    corners = (rows // BLOCK) * (cols // BLOCK) + 1
    sources = recv.shape[0]
    field = (len(places), 2 * SIDE, 2 * SIDE)
    return pl.pallas_call(
        functools.partial(backward_rim_kernel, places),
        out_shape=shapes_of(
            (comps, BLOCK, cols),
            (comps, rows, SIDE),
            (comps, BLOCK, cols),
            (comps, rows // 2, SIDE),
            (comps, BLOCK, SIDE),
            (corners, SIDE, SIDE),
        )
        + (jax.ShapeDtypeStruct((corners,), jnp.int32),),
        in_specs=anywhere(11),
        out_specs=tuple(in_vmem(6)) + (pl.BlockSpec(memory_space=pltpu.SMEM),),
        scratch_shapes=[
            pltpu.VMEM((sources, CAP * SIDE, SIDE), jnp.float32),
            pltpu.SMEM((sources, SIDE), jnp.float32),
            pltpu.VMEM(tables.shape, tables.dtype),
            pltpu.VMEM(probe.shape, jnp.float32),
            pltpu.VMEM(field, jnp.float32),
            pltpu.VMEM(field, jnp.float32),
            extended_shape(tile, 2),
            pltpu.VMEM((comps, SIDE, cols), jnp.float32),
            pltpu.VMEM((comps, SIDE, cols), jnp.float32),
            pltpu.VMEM((comps, rows, SIDE), jnp.float32),
            pltpu.VMEM((comps, rows, SIDE), jnp.float32),
            pltpu.SemaphoreType.DMA((12,)),
        ],
        compiler_params=pltpu.CompilerParams(vmem_limit_bytes=VMEM_MOST),
        cost_estimate=stage_cost(len(places)),
        name="backward_rim",
    )(recv, tile, below, right, diag, probe, tables, *fields_last, *fields_side)


def backward_inner(places, count, sums, tile, probe, tables, far, enter, row, col):
    comps, rows, cols = tile.shape
    return pl.pallas_call(
        functools.partial(backward_inner_kernel, places),
        out_shape=jax.ShapeDtypeStruct(tile.shape, jnp.float32),
        in_specs=[pl.BlockSpec(memory_space=pltpu.SMEM)] + in_vmem(8),
        out_specs=pl.BlockSpec(memory_space=pltpu.VMEM),
        scratch_shapes=[
            pltpu.VMEM((comps, rows, cols - SIDE), jnp.float32),
            pltpu.VMEM((comps, rows, cols - SIDE), jnp.float32),
        ],
        compiler_params=pltpu.CompilerParams(vmem_limit_bytes=VMEM_LIMIT),
        cost_estimate=stage_cost(len(places)),
        name="backward_inner",
    )(count, sums, tile, probe, tables, far, enter, row, col)


def border_kernel(
    own_ref, above_ref, left_ref, diag_ref, out_ref, top_ref, side_ref, row_buf, col_buf, diag_buf, sems
):
    rows = out_ref.shape[1]
    half = rows // 2
    top = out_ref.at[:, pl.ds(0, BLOCK)]
    side = out_ref.at[:, pl.ds(BLOCK, rows - BLOCK), pl.ds(0, SIDE)]
    loads = start_copies(
        [
            (above_ref, row_buf),
            (top, top_ref),
            (left_ref, col_buf),
            (diag_ref, diag_buf),
            (side, side_ref),
        ],
        sems,
    )
    wait_copies(loads)
    left = col_buf[...]
    low = low_lanes(left.shape)
    upper = jnp.where(low, left, 0.0)
    lower = pltpu.roll(jnp.where(low, 0.0, left), BLOCK, 2)
    top_ref[...] = top_ref[...] + row_buf[...]
    top_ref[:, :, :SIDE] = top_ref[:, :, :SIDE] + upper[:, :BLOCK] + diag_buf[...]
    stores = start_copies([(top_ref, top)], sems)
    side_ref[:, : half - BLOCK] = side_ref[:, : half - BLOCK] + upper[:, BLOCK:]
    side_ref[:, half - BLOCK :] = side_ref[:, half - BLOCK :] + lower
    stores += start_copies([(side_ref, side)], sems.at[pl.ds(1, 1)])
    wait_copies(stores)


def add_borders(own, above, left, diag):
    comps, rows, cols = own.shape
    return pl.pallas_call(
        border_kernel,
        out_shape=jax.ShapeDtypeStruct(own.shape, jnp.float32),
        in_specs=anywhere(4),
        out_specs=pl.BlockSpec(memory_space=pl.ANY),
        scratch_shapes=[
            pltpu.VMEM((comps, BLOCK, cols), jnp.float32),
            pltpu.VMEM((comps, rows - BLOCK, SIDE), jnp.float32),
            pltpu.VMEM(above.shape, jnp.float32),
            pltpu.VMEM(left.shape, jnp.float32),
            pltpu.VMEM(diag.shape, jnp.float32),
            pltpu.SemaphoreType.DMA((5,)),
        ],
        input_output_aliases={0: 0},
        compiler_params=pltpu.CompilerParams(vmem_limit_bytes=VMEM_LIMIT),
        name="add_borders",
    )(own, above, left, diag)


def strip_kernel(tile_ref, below_ref, sems):
    wait_copies(start_copies([(tile_ref.at[:, pl.ds(0, BLOCK)], below_ref)], sems))


def row_strip(tile):
    comps, rows, cols = tile.shape
    return pl.pallas_call(
        strip_kernel,
        out_shape=jax.ShapeDtypeStruct((comps, BLOCK, cols), jnp.float32),
        in_specs=anywhere(1),
        out_specs=pl.BlockSpec(memory_space=pltpu.VMEM),
        scratch_shapes=[pltpu.SemaphoreType.DMA((1,))],
        compiler_params=pltpu.CompilerParams(vmem_limit_bytes=VMEM_MOST),
        name="row_strip",
    )(tile)


def moved(shard, down, across):
    row_total = lax.axis_size("row")
    col_total = lax.axis_size("col")
    if across == 0:
        pairs = [(r, r + down) for r in range(row_total) if 0 <= r + down < row_total]
        return lax.ppermute(shard, "row", pairs)
    if down == 0:
        pairs = [(c, c + across) for c in range(col_total) if 0 <= c + across < col_total]
        return lax.ppermute(shard, "col", pairs)
    pairs = [
        (r * col_total + c, (r + down) * col_total + c + across)
        for r in range(row_total)
        for c in range(col_total)
        if 0 <= r + down < row_total and 0 <= c + across < col_total
    ]
    return lax.ppermute(shard, ("row", "col"), pairs)


def body(object_slices, probe, measured, offsets):
    slices, parts, tile_rows, tile_cols = object_slices.shape
    tile = object_slices.reshape(slices * parts, tile_rows, tile_cols)
    row_total = lax.axis_size("row")
    tables = jnp.asarray(TABLES)
    below = moved(row_strip(tile), -1, 0)
    send, strip_right, strip_diag = pack(offsets, measured, tile, row_total)
    right = moved(strip_right, 0, -1)
    diag = moved(strip_diag, -1, -1)
    recv = lax.all_to_all(send, "row", split_axis=0, concat_axis=0, tiled=True)
    last, side, inner = pair_places(tile_rows, tile_cols)
    far_inner, enter_inner = forward_inner(inner, tile, probe, tables)
    far_inner, enter_inner, right = lax.optimization_barrier((far_inner, enter_inner, right))
    far_last, enter_last, far_side, enter_side = forward_rim(
        last, side, tile, below, right, diag, probe, tables
    )
    row, col, to_below, to_right, to_diag, sums, count = backward_rim(
        recv,
        tile,
        below,
        right,
        diag,
        probe,
        tables,
        (far_last, enter_last),
        (far_side, enter_side),
        last + side,
    )
    above = moved(to_below, 1, 0)
    left = moved(to_right, 0, 1)
    corner_part = moved(to_diag, 1, 1)
    own = backward_inner(
        inner, count, sums, tile, probe, tables, far_inner, enter_inner, row, col
    )
    result = add_borders(own, above, left, corner_part)
    return result.reshape(object_slices.shape)


def solution(mesh):
    placed = (
        P(None, None, "row", "col"),
        P(),
        P(("row", "col"), None, None),
        P(None, ("row", "col")),
    )
    return jax.shard_map(
        body, mesh=mesh, in_specs=placed, out_specs=P(None, None, "row", "col"), check_vma=False
    )
```

```python
import functools
import math

import jax
import jax.numpy as jnp
import ml_dtypes
import numpy as np
from jax import lax
from jax.experimental import pallas as pl
from jax.experimental.pallas import tpu as pltpu
from jax.sharding import PartitionSpec as P

PHASE = 40.0
SIDE = 128
BLOCK = 64
CAP = 2
META = 8
CHUNKS = 4
VMEM_LIMIT = 64 * 1024 * 1024


def dft_matrix():
    index = np.arange(SIDE)
    angle = (index[:, None] * index[None, :] % SIDE) * (-2.0 * math.pi / SIDE)
    return np.exp(1j * angle) / math.sqrt(SIDE)


def propagation_matrix():
    index = np.arange(SIDE)
    freq = np.where(index < SIDE // 2, index, index - SIDE) / SIDE
    dft = dft_matrix()
    return np.conj(dft) @ (np.exp(-1j * PHASE * freq * freq)[:, None] * dft)


def real_forms(matrix):
    right = np.block([[matrix.real, matrix.imag], [-matrix.imag, matrix.real]])
    out = []
    for form in (right, right.T):
        form = form.astype(np.float32)
        high = form.astype(ml_dtypes.bfloat16)
        out.append(high)
        out.append((form - high.astype(np.float32)).astype(ml_dtypes.bfloat16))
    return np.stack(out)


TABLES = np.concatenate([real_forms(propagation_matrix()), real_forms(dft_matrix())])


def split(field):
    high = field.astype(jnp.bfloat16)
    low = (field - high.astype(jnp.float32)).astype(jnp.bfloat16)
    return high, low


def from_right(rows, tables, at):
    high, low = split(rows)
    left = jnp.concatenate([high, low, high], axis=1)
    right = jnp.concatenate([tables[at], tables[at], tables[at + 1]], axis=0)
    return jnp.dot(left, right, preferred_element_type=jnp.float32)


def from_left(columns, tables, at):
    high, low = split(columns)
    left = jnp.concatenate([tables[at], tables[at], tables[at + 1]], axis=1)
    right = jnp.concatenate([high, low, high], axis=0)
    return jnp.dot(left, right, preferred_element_type=jnp.float32)


def swap(pair):
    top = jnp.concatenate([pair[:SIDE, :SIDE], pair[SIDE:, :SIDE]], axis=1)
    bottom = jnp.concatenate([pair[:SIDE, SIDE:], pair[SIDE:, SIDE:]], axis=1)
    return jnp.concatenate([top, bottom], axis=0)


def two_sided(pairs, tables, right_at, left_at):
    pairs = [from_right(rows, tables, right_at) for rows in pairs]
    return [from_left(swap(rows), tables, left_at) for rows in pairs]


def stacked(fields):
    return jnp.concatenate([jnp.concatenate(field, axis=1) for field in fields], axis=0)


def halves(pair, n):
    return pair[:SIDE, n * SIDE : (n + 1) * SIDE], pair[SIDE:, n * SIDE : (n + 1) * SIDE]


def low_lanes(shape):
    return lax.broadcasted_iota(jnp.int32, shape, len(shape) - 1) < BLOCK


def cut_pair(ext_ref, comp, row, col):
    first = ext_ref[comp, row : row + SIDE, col : col + SIDE]
    second = ext_ref[comp, row : row + SIDE, col + SIDE : col + 2 * SIDE]
    mixed = jnp.where(low_lanes(first.shape), second, first)
    return first, pltpu.roll(mixed, BLOCK, 1)


def times(left_re, left_im, right_re, right_im):
    return (left_re * right_re - left_im * right_im, left_re * right_im + left_im * right_re)


def conj_times(left_re, left_im, right_re, right_im):
    return (left_re * right_re + left_im * right_im, left_re * right_im - left_im * right_re)


def pack_kernel(off_ref, meas_ref, send_ref, meta_ref, count_ref, corner_ref, sems):
    owners = send_ref.shape[0]
    positions = meas_ref.shape[0]
    for owner in range(owners):
        count_ref[owner] = 0
        for rank in range(CAP):
            corner_ref[owner * CAP + rank] = -1
    copies = []
    for pos in range(positions):
        y = off_ref[0, pos]
        x = off_ref[1, pos]
        owner = lax.shift_right_logical(y, 8)
        rank = jnp.minimum(count_ref[owner], CAP - 1)
        count_ref[owner] = rank + 1
        corner = (lax.shift_right_logical(y, 6) & 3) * 8 + (lax.shift_right_logical(x, 6) & 7)
        corner_ref[owner * CAP + rank] = corner
        copy = pltpu.make_async_copy(
            meas_ref.at[pos],
            send_ref.at[owner, pl.ds(pl.multiple_of(rank * SIDE, SIDE), SIDE)],
            sems.at[pos],
        )
        copy.start()
        copies.append(copy)
    first = low_lanes((META, SIDE))
    for owner in range(owners):
        both = jnp.where(first, corner_ref[owner * CAP], corner_ref[owner * CAP + 1])
        meta_ref[owner] = both.astype(jnp.float32)
    copy = pltpu.make_async_copy(
        meta_ref, send_ref.at[:, pl.ds(CAP * SIDE, META)], sems.at[positions]
    )
    copy.start()
    copies.append(copy)
    for copy in copies:
        copy.wait()


def pack(offsets, measured, owners):
    positions = measured.shape[0]
    return pl.pallas_call(
        pack_kernel,
        out_shape=jax.ShapeDtypeStruct((owners, CAP * SIDE + META, SIDE), jnp.float32),
        in_specs=[
            pl.BlockSpec(memory_space=pltpu.SMEM),
            pl.BlockSpec(memory_space=pltpu.VMEM),
        ],
        out_specs=pl.BlockSpec(memory_space=pl.ANY),
        scratch_shapes=[
            pltpu.VMEM((owners, META, SIDE), jnp.float32),
            pltpu.SMEM((owners,), jnp.int32),
            pltpu.SMEM((owners * CAP,), jnp.int32),
            pltpu.SemaphoreType.DMA((positions + 1,)),
        ],
        compiler_params=pltpu.CompilerParams(vmem_limit_bytes=VMEM_LIMIT),
        cost_estimate=pl.CostEstimate(
            flops=0, bytes_accessed=40 * 1024 * 1024, transcendentals=0
        ),
        name="pack_measured",
    )(offsets, measured)


def pair_places(rows, cols):
    row_blocks = rows // BLOCK
    edge = cols - SIDE
    last = tuple((row_blocks - 1, col) for col in range(0, cols, SIDE))
    side = tuple((row, edge) for row in range(row_blocks - 1))
    inner = tuple((row, col) for row in range(row_blocks - 1) for col in range(0, edge, SIDE))
    return last, side, inner


def forward_pairs(places, ext_ref, probe_ref, tables, far_refs, enter_refs):
    probe_re = probe_ref[0]
    probe_im = probe_ref[1]
    rows = []
    for row, col in places:
        trans = [cut_pair(ext_ref, comp, row * BLOCK, col) for comp in range(2)]
        rows.append(
            stacked([times(probe_re, probe_im, trans[0][n], trans[1][n]) for n in range(2)])
        )
    enters = two_sided(rows, tables, 0, 2)
    rows = []
    for pair, (row, col) in enumerate(places):
        enter = enters[pair]
        enter_refs[pair][...] = enter
        trans = [cut_pair(ext_ref, comp, row * BLOCK, col) for comp in range(2, 4)]
        rows.append(
            stacked([times(*halves(enter, n), trans[0][n], trans[1][n]) for n in range(2)])
        )
    fars = two_sided(rows, tables, 4, 6)
    for far_ref, far in zip(far_refs, fars):
        far_ref[...] = far


def each(ref):
    return [ref.at[pair] for pair in range(ref.shape[0])]


def start_copies(parts, sems):
    copies = [
        pltpu.make_async_copy(source, target, sems.at[n])
        for n, (source, target) in enumerate(parts)
    ]
    for copy in copies:
        copy.start()
    return copies


def wait_copies(copies):
    for copy in copies:
        copy.wait()


def forward_inner_kernel(places, tile_ref, probe_ref, tables, far_ref, enter_ref):
    forward_pairs(places, tile_ref, probe_ref, tables, each(far_ref), each(enter_ref))


def forward_rim_kernel(
    places,
    tile_ref,
    below_ref,
    right_ref,
    diag_ref,
    probe_ref,
    tables,
    far_last_ref,
    enter_last_ref,
    far_side_ref,
    enter_side_ref,
    ext_ref,
    sems,
):
    rows, cols = tile_ref.shape[1:]
    wait_copies(
        start_copies(
            [
                (tile_ref, ext_ref.at[:, pl.ds(0, rows), pl.ds(0, cols)]),
                (below_ref, ext_ref.at[:, pl.ds(rows, BLOCK), pl.ds(0, cols)]),
                (right_ref, ext_ref.at[:, pl.ds(0, rows), pl.ds(cols, SIDE)]),
                (diag_ref, ext_ref.at[:, pl.ds(rows, BLOCK), pl.ds(cols, SIDE)]),
            ],
            sems,
        )
    )
    forward_pairs(
        places,
        ext_ref,
        probe_ref,
        tables,
        each(far_last_ref) + each(far_side_ref),
        each(enter_last_ref) + each(enter_side_ref),
    )


def stage_cost(pairs):
    return pl.CostEstimate(
        flops=pairs * 4 * 3 * 2 * 256**3, bytes_accessed=1024 * 1024, transcendentals=0
    )


def fields(places):
    field = jax.ShapeDtypeStruct((len(places), 2 * SIDE, 2 * SIDE), jnp.float32)
    return field, field


def in_vmem(count):
    return [pl.BlockSpec(memory_space=pltpu.VMEM)] * count


def anywhere(count):
    return [pl.BlockSpec(memory_space=pl.ANY)] * count


def in_hbm(count):
    return [pl.BlockSpec(memory_space=pltpu.HBM)] * count


def forward_inner(places, tile, probe, tables):
    return pl.pallas_call(
        functools.partial(forward_inner_kernel, places),
        out_shape=fields(places),
        in_specs=in_vmem(3),
        out_specs=tuple(in_vmem(2)),
        compiler_params=pltpu.CompilerParams(vmem_limit_bytes=VMEM_LIMIT),
        cost_estimate=stage_cost(8 * len(places)),
        name="forward_inner",
    )(tile, probe, tables)


def extended_shape(tile, comps):
    return pltpu.VMEM((comps, tile.shape[1] + BLOCK, tile.shape[2] + SIDE), jnp.float32)


def forward_rim(last, side, tile, below, right, diag, probe, tables):
    places = last + side
    return pl.pallas_call(
        functools.partial(forward_rim_kernel, places),
        out_shape=fields(last) + fields(side),
        in_specs=in_hbm(4) + in_vmem(2),
        out_specs=tuple(in_vmem(4)),
        scratch_shapes=[extended_shape(tile, tile.shape[0]), pltpu.SemaphoreType.DMA((4,))],
        compiler_params=pltpu.CompilerParams(vmem_limit_bytes=VMEM_LIMIT),
        cost_estimate=stage_cost(8 * len(places)),
        name="forward_rim",
    )(tile, below, right, diag, probe, tables)


def gather_sums(meta_ref, items_ref, sum_ref, count_ref, arrivals):
    spare = sum_ref.shape[0] - 1
    sources = items_ref.shape[0]
    for corner in range(spare + 1):
        count_ref[corner] = 0
    for source in range(sources):
        if source % (sources // len(arrivals)) == 0:
            arrivals[source * len(arrivals) // sources].wait()
        for rank in range(CAP):
            corner = meta_ref[source, rank * BLOCK].astype(jnp.int32)
            at = jnp.where(corner < 0, spare, corner)
            hits = count_ref[at]
            count_ref[at] = hits + 1
            item = items_ref[source, rank * SIDE : (rank + 1) * SIDE]
            sum_ref[at] = jnp.where(hits > 0, sum_ref[at], 0.0) + item


def summed(sum_ref, count_ref, at):
    hits = count_ref[at]
    return hits.astype(jnp.float32), jnp.where(hits > 0, sum_ref[at], 0.0)


def backward_pairs(
    places,
    width,
    probe_ref,
    tables,
    far_ref,
    enter_ref,
    ext_ref,
    sum_ref,
    count_ref,
    store,
    before_pair,
    before_products,
    before_fields,
    after_fields,
):
    rows = []
    for pair, (row, col) in enumerate(places):
        before_pair(pair)
        waves = []
        for n in range(2):
            at = row * width + col // BLOCK + n
            hits, total = summed(sum_ref, count_ref, at)
            far_re, far_im = halves(far_ref[pair], n)
            misfit = 2.0 * (hits * (far_re * far_re + far_im * far_im) - total)
            waves.append((misfit * far_re, misfit * far_im))
        rows.append(stacked(waves))
    before_products()
    backs = two_sided(rows, tables, 6, 4)
    before_fields()
    rows = []
    for pair, (row, col) in enumerate(places):
        trans = [cut_pair(ext_ref, comp, row * BLOCK, col) for comp in range(2)]
        waves = []
        for n in range(2):
            back = halves(backs[pair], n)
            grad = conj_times(*halves(enter_ref[pair], n), *back)
            store(n, 2, row, col, grad[0])
            store(n, 3, row, col, grad[1])
            waves.append(conj_times(trans[0][n], trans[1][n], *back))
        rows.append(stacked(waves))
    after_fields()
    backs = two_sided(rows, tables, 2, 0)
    probe_re = probe_ref[0]
    probe_im = probe_ref[1]
    for pair, (row, col) in enumerate(places):
        for n in range(2):
            grad = conj_times(probe_re, probe_im, *halves(backs[pair], n))
            store(n, 0, row, col, grad[0])
            store(n, 1, row, col, grad[1])


def shifted(low, high):
    if low is None:
        low = jnp.zeros_like(high)
    if high is None:
        high = jnp.zeros_like(low)
    return pltpu.roll(jnp.where(low_lanes(low.shape), high, low), BLOCK, 1)


def backward_rim_kernel(
    places,
    recv_ref,
    tile_ref,
    below_ref,
    right_ref,
    diag_ref,
    probe_ref,
    tables_ref,
    far_last_ref,
    enter_last_ref,
    far_side_ref,
    enter_side_ref,
    row_ref,
    col_ref,
    out_below_ref,
    out_right_ref,
    out_diag_ref,
    out_sum_ref,
    count_ref,
    items_ref,
    meta_ref,
    table_buf,
    probe_buf,
    far_buf,
    enter_buf,
    ext_ref,
    sum_ref,
    even_ref,
    odd_ref,
    even_side_ref,
    odd_side_ref,
    row_buf,
    col_buf,
    below_buf,
    right_buf,
    diag_buf,
    sems,
    out_sems,
):
    rows, cols = tile_ref.shape[1:]
    last = rows // BLOCK - 1
    corners = sum_ref.shape[0] - 1
    near = far_last_ref.shape[0]
    first = pl.ds(0, near)
    others = pl.ds(near, far_side_ref.shape[0])
    two = pl.ds(2, 2)
    chunk = recv_ref.shape[0] // CHUNKS
    wide = pl.ds(0, cols)
    beyond = pl.ds(cols, SIDE)
    copies = start_copies(
        [(recv_ref.at[:, CAP * SIDE], meta_ref)]
        + [
            (recv_ref.at[part, pl.ds(0, CAP * SIDE)], items_ref.at[part])
            for part in (pl.ds(n * chunk, chunk) for n in range(CHUNKS))
        ]
        + [
            (far_last_ref, far_buf.at[first]),
            (tables_ref, table_buf),
            (far_side_ref, far_buf.at[others]),
            (enter_last_ref, enter_buf.at[first]),
            (enter_side_ref, enter_buf.at[others]),
            (tile_ref.at[two], ext_ref.at[:, pl.ds(0, rows), wide]),
            (below_ref.at[two], ext_ref.at[:, pl.ds(rows, BLOCK), wide]),
            (right_ref.at[two], ext_ref.at[:, pl.ds(0, rows), beyond]),
            (diag_ref.at[two], ext_ref.at[:, pl.ds(rows, BLOCK), beyond]),
            (probe_ref, probe_buf),
        ],
        sems,
    )
    wait_copies(copies[:1])
    rest = copies[1 + CHUNKS :]
    gather_sums(meta_ref, items_ref, sum_ref, count_ref, copies[1 : 1 + CHUNKS])
    bands = (even_ref, odd_ref)
    sides = (even_side_ref, odd_side_ref)
    stores = start_copies(
        [(sum_ref.at[pl.ds(0, corners)], out_sum_ref)], out_sems.at[pl.ds(20, 1)]
    )

    def store(n, comp, row, col, value):
        if row == last:
            bands[n][comp, :, col : col + SIDE] = value
        else:
            at = row * BLOCK
            top = value[:BLOCK]
            if row > 0:
                top = top + sides[n][comp, at : at + BLOCK]
            sides[n][comp, at : at + BLOCK] = top
            sides[n][comp, at + BLOCK : at + SIDE] = value[BLOCK:]

    half = rows // 2

    def finish(comp):
        beyond_cols = []
        for buf, part in ((row_buf, slice(0, BLOCK)), (below_buf, slice(BLOCK, SIDE))):
            before = None
            for col in range(0, cols, SIDE):
                here = odd_ref[comp, part, col : col + SIDE]
                buf[comp, :, col : col + SIDE] = even_ref[
                    comp, part, col : col + SIDE
                ] + shifted(before, here)
                before = here
            beyond_cols.append(shifted(before, None))
        corner = beyond_cols[1]
        diag_buf[comp] = corner[: BLOCK // 2] + pltpu.roll(corner[BLOCK // 2 :], BLOCK, 1)
        odd_side = odd_side_ref[comp]
        col_buf[comp] = even_side_ref[comp] + shifted(None, odd_side)
        side = shifted(odd_side, None)
        second = jnp.concatenate(
            [side[half : rows - BLOCK], side[rows - BLOCK :] + beyond_cols[0]], axis=0
        )
        right_buf[comp] = side[:half] + pltpu.roll(second, BLOCK, 1)
        stores.extend(
            start_copies(
                [
                    (below_buf.at[comp], out_below_ref.at[comp]),
                    (diag_buf.at[comp], out_diag_ref.at[comp]),
                    (right_buf.at[comp], out_right_ref.at[comp]),
                    (row_buf.at[comp], row_ref.at[comp]),
                    (col_buf.at[comp], col_ref.at[comp]),
                ],
                out_sems.at[pl.ds(5 * comp, 5)],
            )
        )

    def before_pair(pair):
        if pair == 0:
            rest[0].wait()
        if pair == near:
            rest[2].wait()

    def after_fields():
        finish(2)
        finish(3)

    backward_pairs(
        places,
        cols // BLOCK,
        probe_buf,
        table_buf,
        far_buf,
        enter_buf,
        ext_ref,
        sum_ref,
        count_ref,
        store,
        before_pair,
        lambda: wait_copies(rest[1:2]),
        lambda: wait_copies(rest[3:]),
        after_fields,
    )
    finish(0)
    finish(1)
    wait_copies(stores)


def backward_inner_kernel(
    places,
    count_ref,
    sum_ref,
    tile_ref,
    probe_ref,
    tables_ref,
    far_ref,
    enter_ref,
    row_ref,
    col_ref,
    out_ref,
    sum_buf,
    trans_buf,
    probe_buf,
    table_buf,
    far_buf,
    enter_buf,
    row_buf,
    col_buf,
    out_buf,
    even_ref,
    odd_ref,
    sems,
    out_sems,
):
    comps, rows, cols = out_buf.shape
    last = rows - BLOCK
    width = cols // BLOCK
    acc = (even_ref, odd_ref)
    row_blocks = last // BLOCK
    group = len(places) // row_blocks
    parts = []
    for n in range(row_blocks):
        here = pl.ds(n * width, width)
        parts.append((sum_ref.at[here], sum_buf.at[here]))
        here = pl.ds(n * group, group)
        parts.append((far_ref.at[here], far_buf.at[here]))
        if n == 0:
            parts.append((tables_ref, table_buf))
    copies = start_copies(
        parts
        + [
            (enter_ref, enter_buf),
            (tile_ref.at[pl.ds(2, 2)], trans_buf),
            (probe_ref, probe_buf),
            (row_ref, row_buf),
            (col_ref, col_buf),
        ],
        sems,
    )
    table_copy = copies.pop(2)
    rest = copies[2 * row_blocks :]
    stores = []

    def store(n, comp, row, col, value):
        at = row * BLOCK
        lanes = slice(col, col + SIDE)
        top = value[:BLOCK]
        if row > 0:
            top = top + acc[n][comp, at : at + BLOCK, lanes]
        acc[n][comp, at : at + BLOCK, lanes] = top
        acc[n][comp, at + BLOCK : at + SIDE, lanes] = value[BLOCK:]

    def finish(comp):
        before = None
        for col in range(0, cols, SIDE):
            lanes = slice(col, col + SIDE)
            if col < cols - SIDE:
                here = odd_ref[comp, :, lanes]
                value = even_ref[comp, :, lanes] + shifted(before, here)
                before = here
            else:
                value = col_buf[comp] + shifted(before, None)
            out_buf[comp, :last, lanes] = value[:last]
            out_buf[comp, last:, lanes] = value[last:] + row_buf[comp, :, lanes]
        stores.extend(
            start_copies(
                [(out_buf.at[comp], out_ref.at[comp])], out_sems.at[pl.ds(comp, 1)]
            )
        )

    def before_pair(pair):
        if pair % group == 0:
            at = 2 * (pair // group)
            wait_copies(copies[at : at + 2])

    def after_fields():
        finish(2)
        finish(3)

    backward_pairs(
        places,
        width,
        probe_buf,
        table_buf,
        far_buf,
        enter_buf,
        trans_buf,
        sum_buf,
        count_ref,
        store,
        before_pair,
        table_copy.wait,
        lambda: wait_copies(rest),
        after_fields,
    )
    finish(0)
    finish(1)
    wait_copies(stores)


def shapes_of(*shapes):
    return tuple(jax.ShapeDtypeStruct(shape, jnp.float32) for shape in shapes)


def backward_rim(places, recv, tile, below, right, diag, probe, tables, fields_last, fields_side):
    comps, rows, cols = tile.shape
    corners = (rows // BLOCK) * (cols // BLOCK)
    sources = recv.shape[0]
    field = (len(places), 2 * SIDE, 2 * SIDE)
    outs = (
        (comps, BLOCK, cols),
        (comps, rows, SIDE),
        (comps, BLOCK, cols),
        (comps, rows // 2, SIDE),
        (comps, BLOCK // 2, SIDE),
    )
    return pl.pallas_call(
        functools.partial(backward_rim_kernel, places),
        out_shape=shapes_of(*outs, (corners, SIDE, SIDE))
        + (jax.ShapeDtypeStruct((corners + 1,), jnp.int32),),
        in_specs=in_hbm(11),
        out_specs=tuple(in_hbm(6)) + (pl.BlockSpec(memory_space=pltpu.SMEM),),
        scratch_shapes=[
            pltpu.VMEM((sources, CAP * SIDE, SIDE), jnp.float32),
            pltpu.SMEM((sources, SIDE), jnp.float32),
            pltpu.VMEM(tables.shape, tables.dtype),
            pltpu.VMEM(probe.shape, jnp.float32),
            pltpu.VMEM(field, jnp.float32),
            pltpu.VMEM(field, jnp.float32),
            extended_shape(tile, 2),
            pltpu.VMEM((corners + 1, SIDE, SIDE), jnp.float32),
            pltpu.VMEM((comps, SIDE, cols), jnp.float32),
            pltpu.VMEM((comps, SIDE, cols), jnp.float32),
            pltpu.VMEM((comps, rows, SIDE), jnp.float32),
            pltpu.VMEM((comps, rows, SIDE), jnp.float32),
        ]
        + [pltpu.VMEM(shape, jnp.float32) for shape in outs]
        + [pltpu.SemaphoreType.DMA((CHUNKS + 11,)), pltpu.SemaphoreType.DMA((21,))],
        compiler_params=pltpu.CompilerParams(vmem_limit_bytes=VMEM_LIMIT),
        cost_estimate=stage_cost(len(places)),
        name="backward_rim",
    )(recv, tile, below, right, diag, probe, tables, *fields_last, *fields_side)


def backward_inner(places, count, sums, tile, probe, tables, far, enter, row, col):
    comps, rows, cols = tile.shape
    return pl.pallas_call(
        functools.partial(backward_inner_kernel, places),
        out_shape=jax.ShapeDtypeStruct(tile.shape, jnp.float32),
        in_specs=[pl.BlockSpec(memory_space=pltpu.SMEM)] + in_hbm(8),
        out_specs=in_hbm(1)[0],
        scratch_shapes=[
            pltpu.VMEM(sums.shape, jnp.float32),
            pltpu.VMEM((2, rows, cols), jnp.float32),
            pltpu.VMEM(probe.shape, jnp.float32),
            pltpu.VMEM(tables.shape, tables.dtype),
            pltpu.VMEM(far.shape, jnp.float32),
            pltpu.VMEM(enter.shape, jnp.float32),
            pltpu.VMEM(row.shape, jnp.float32),
            pltpu.VMEM(col.shape, jnp.float32),
            pltpu.VMEM(tile.shape, jnp.float32),
            pltpu.VMEM((comps, rows, cols - SIDE), jnp.float32),
            pltpu.VMEM((comps, rows, cols - SIDE), jnp.float32),
            pltpu.SemaphoreType.DMA((2 * (rows // BLOCK - 1) + 6,)),
            pltpu.SemaphoreType.DMA((comps,)),
        ],
        compiler_params=pltpu.CompilerParams(vmem_limit_bytes=VMEM_LIMIT),
        cost_estimate=stage_cost(len(places)),
        name="backward_inner",
    )(count, sums, tile, probe, tables, far, enter, row, col)


def border_kernel(
    own_ref, above_ref, left_ref, diag_ref, out_ref, top_ref, side_ref, row_buf, col_buf, diag_buf, sems
):
    rows = out_ref.shape[1]
    half = rows // 2
    top = out_ref.at[:, pl.ds(0, BLOCK)]
    side = out_ref.at[:, pl.ds(BLOCK, rows - BLOCK), pl.ds(0, SIDE)]
    loads = start_copies(
        [
            (above_ref, row_buf),
            (top, top_ref),
            (left_ref, col_buf),
            (diag_ref, diag_buf),
            (side, side_ref),
        ],
        sems,
    )
    def unpacked(packed):
        low = low_lanes(packed.shape)
        upper = jnp.where(low, packed, 0.0)
        return upper, pltpu.roll(jnp.where(low, 0.0, packed), BLOCK, 2)

    wait_copies(loads[:2])
    top_ref[...] = top_ref[...] + row_buf[...]
    wait_copies(loads[2:4])
    upper, lower = unpacked(col_buf[...])
    corner = jnp.concatenate(unpacked(diag_buf[...]), axis=1)
    top_ref[:, :, :SIDE] = top_ref[:, :, :SIDE] + upper[:, :BLOCK] + corner
    stores = start_copies([(top_ref, top)], sems.at[pl.ds(5, 1)])
    wait_copies(loads[4:])
    side_ref[:, : half - BLOCK] = side_ref[:, : half - BLOCK] + upper[:, BLOCK:]
    side_ref[:, half - BLOCK :] = side_ref[:, half - BLOCK :] + lower
    stores += start_copies([(side_ref, side)], sems.at[pl.ds(6, 1)])
    wait_copies(stores)


def add_borders(own, above, left, diag):
    comps, rows, cols = own.shape
    return pl.pallas_call(
        border_kernel,
        out_shape=jax.ShapeDtypeStruct(own.shape, jnp.float32),
        in_specs=anywhere(4),
        out_specs=pl.BlockSpec(memory_space=pl.ANY),
        scratch_shapes=[
            pltpu.VMEM((comps, BLOCK, cols), jnp.float32),
            pltpu.VMEM((comps, rows - BLOCK, SIDE), jnp.float32),
            pltpu.VMEM(above.shape, jnp.float32),
            pltpu.VMEM(left.shape, jnp.float32),
            pltpu.VMEM(diag.shape, jnp.float32),
            pltpu.SemaphoreType.DMA((7,)),
        ],
        input_output_aliases={0: 0},
        compiler_params=pltpu.CompilerParams(vmem_limit_bytes=VMEM_LIMIT),
        name="add_borders",
    )(own, above, left, diag)


def row_strip_kernel(tile_ref, row_ref, corner_ref, sems):
    top = pl.ds(0, BLOCK)
    wait_copies(
        start_copies(
            [
                (tile_ref.at[:, top], row_ref),
                (tile_ref.at[:, top, pl.ds(0, SIDE)], corner_ref),
            ],
            sems,
        )
    )


def row_strip(tile):
    comps, rows, cols = tile.shape
    return pl.pallas_call(
        row_strip_kernel,
        out_shape=shapes_of((comps, BLOCK, cols), (comps, BLOCK, SIDE)),
        in_specs=in_hbm(1),
        out_specs=tuple(in_vmem(2)),
        scratch_shapes=[pltpu.SemaphoreType.DMA((2,))],
        compiler_params=pltpu.CompilerParams(vmem_limit_bytes=VMEM_LIMIT),
        name="row_strip",
    )(tile)


def column_strip_kernel(tile_ref, send_ref, out_ref, sems):
    wait_copies(start_copies([(tile_ref.at[:, :, pl.ds(0, SIDE)], out_ref)], sems))


def column_strip(tile, send):
    comps, rows, cols = tile.shape
    return pl.pallas_call(
        column_strip_kernel,
        out_shape=jax.ShapeDtypeStruct((comps, rows, SIDE), jnp.float32),
        in_specs=in_hbm(2),
        out_specs=pl.BlockSpec(memory_space=pltpu.VMEM),
        scratch_shapes=[pltpu.SemaphoreType.DMA((1,))],
        compiler_params=pltpu.CompilerParams(vmem_limit_bytes=VMEM_LIMIT),
        name="column_strip",
    )(tile, send)


def moved(shard, down, across):
    row_total = lax.axis_size("row")
    col_total = lax.axis_size("col")
    if across == 0:
        pairs = [(r, r + down) for r in range(row_total) if 0 <= r + down < row_total]
        return lax.ppermute(shard, "row", pairs)
    if down == 0:
        pairs = [(c, c + across) for c in range(col_total) if 0 <= c + across < col_total]
        return lax.ppermute(shard, "col", pairs)
    pairs = [
        (r * col_total + c, (r + down) * col_total + c + across)
        for r in range(row_total)
        for c in range(col_total)
        if 0 <= r + down < row_total and 0 <= c + across < col_total
    ]
    return lax.ppermute(shard, ("row", "col"), pairs)


def body(object_slices, probe, measured, offsets):
    slices, parts, tile_rows, tile_cols = object_slices.shape
    tile = object_slices.reshape(slices * parts, tile_rows, tile_cols)
    row_total = lax.axis_size("row")
    tables = jnp.asarray(TABLES)
    strip_below, strip_diag = row_strip(tile)
    below = moved(strip_below, -1, 0)
    diag = moved(strip_diag, -1, -1)
    send = pack(offsets, measured, row_total)
    recv = lax.all_to_all(send, "row", split_axis=0, concat_axis=0, tiled=True)
    right = moved(column_strip(tile, send), 0, -1)
    last, side, inner = pair_places(tile_rows, tile_cols)
    far_inner, enter_inner = forward_inner(inner, tile, probe, tables)
    far_inner, enter_inner, right = lax.optimization_barrier((far_inner, enter_inner, right))
    far_last, enter_last, far_side, enter_side = forward_rim(
        last, side, tile, below, right, diag, probe, tables
    )
    row, col, to_below, to_right, to_diag, sums, count = backward_rim(
        last + side,
        recv,
        tile,
        below,
        right,
        diag,
        probe,
        tables,
        (far_last, enter_last),
        (far_side, enter_side),
    )
    above = moved(to_below, 1, 0)
    left = moved(to_right, 0, 1)
    corner_part = moved(to_diag, 1, 1)
    own = backward_inner(
        inner, count, sums, tile, probe, tables, far_inner, enter_inner, row, col
    )
    result = add_borders(own, above, left, corner_part)
    return result.reshape(object_slices.shape)


def solution(mesh):
    placed = (
        P(None, None, "row", "col"),
        P(),
        P(("row", "col"), None, None),
        P(None, ("row", "col")),
    )
    return jax.shard_map(
        body, mesh=mesh, in_specs=placed, out_specs=P(None, None, "row", "col"), check_vma=False
    )
```

```python
import functools
import math

import jax
import jax.numpy as jnp
import ml_dtypes
import numpy as np
from jax import lax
from jax.experimental import pallas as pl
from jax.experimental.pallas import tpu as pltpu
from jax.sharding import PartitionSpec as P

PHASE = 40.0
SIDE = 128
BLOCK = 64
CAP = 2
META = 8
CHUNKS = 4
VMEM_LIMIT = 64 * 1024 * 1024


def dft_matrix():
    index = np.arange(SIDE)
    angle = (index[:, None] * index[None, :] % SIDE) * (-2.0 * math.pi / SIDE)
    return np.exp(1j * angle) / math.sqrt(SIDE)


def propagation_matrix():
    index = np.arange(SIDE)
    freq = np.where(index < SIDE // 2, index, index - SIDE) / SIDE
    dft = dft_matrix()
    return np.conj(dft) @ (np.exp(-1j * PHASE * freq * freq)[:, None] * dft)


def real_forms(matrix):
    right = np.block([[matrix.real, matrix.imag], [-matrix.imag, matrix.real]])
    out = []
    for form in (right, right.T):
        form = form.astype(np.float32)
        high = form.astype(ml_dtypes.bfloat16)
        out.append(high)
        out.append((form - high.astype(np.float32)).astype(ml_dtypes.bfloat16))
    return np.stack(out)


TABLES = np.concatenate([real_forms(propagation_matrix()), real_forms(dft_matrix())])


def split(field):
    high = field.astype(jnp.bfloat16)
    low = (field - high.astype(jnp.float32)).astype(jnp.bfloat16)
    return high, low


def from_right(rows, tables, at):
    high, low = split(rows)
    left = jnp.concatenate([high, low, high], axis=1)
    right = jnp.concatenate([tables[at], tables[at], tables[at + 1]], axis=0)
    return jnp.dot(left, right, preferred_element_type=jnp.float32)


def from_left(columns, tables, at):
    high, low = split(columns)
    left = jnp.concatenate([tables[at], tables[at], tables[at + 1]], axis=1)
    right = jnp.concatenate([high, low, high], axis=0)
    return jnp.dot(left, right, preferred_element_type=jnp.float32)


def swap(pair):
    top = jnp.concatenate([pair[:SIDE, :SIDE], pair[SIDE:, :SIDE]], axis=1)
    bottom = jnp.concatenate([pair[:SIDE, SIDE:], pair[SIDE:, SIDE:]], axis=1)
    return jnp.concatenate([top, bottom], axis=0)


def two_sided(pairs, tables, right_at, left_at):
    pairs = [from_right(rows, tables, right_at) for rows in pairs]
    return [from_left(swap(rows), tables, left_at) for rows in pairs]


def stacked(fields):
    return jnp.concatenate([jnp.concatenate(field, axis=1) for field in fields], axis=0)


def halves(pair, n):
    return pair[:SIDE, n * SIDE : (n + 1) * SIDE], pair[SIDE:, n * SIDE : (n + 1) * SIDE]


def low_lanes(shape):
    return lax.broadcasted_iota(jnp.int32, shape, len(shape) - 1) < BLOCK


def cut_pair(ext_ref, comp, row, col):
    first = ext_ref[comp, row : row + SIDE, col : col + SIDE]
    second = ext_ref[comp, row : row + SIDE, col + SIDE : col + 2 * SIDE]
    mixed = jnp.where(low_lanes(first.shape), second, first)
    return first, pltpu.roll(mixed, BLOCK, 1)


def times(left_re, left_im, right_re, right_im):
    return (left_re * right_re - left_im * right_im, left_re * right_im + left_im * right_re)


def conj_times(left_re, left_im, right_re, right_im):
    return (left_re * right_re + left_im * right_im, left_re * right_im - left_im * right_re)


def pack_kernel(off_ref, meas_ref, send_ref, meta_ref, count_ref, corner_ref, sems):
    owners = send_ref.shape[0]
    positions = meas_ref.shape[0]
    for owner in range(owners):
        count_ref[owner] = 0
        for rank in range(CAP):
            corner_ref[owner * CAP + rank] = -1
    copies = []
    for pos in range(positions):
        y = off_ref[0, pos]
        x = off_ref[1, pos]
        owner = lax.shift_right_logical(y, 8)
        rank = jnp.minimum(count_ref[owner], CAP - 1)
        count_ref[owner] = rank + 1
        corner = (lax.shift_right_logical(y, 6) & 3) * 8 + (lax.shift_right_logical(x, 6) & 7)
        corner_ref[owner * CAP + rank] = corner
        copy = pltpu.make_async_copy(
            meas_ref.at[pos],
            send_ref.at[owner, pl.ds(pl.multiple_of(rank * SIDE, SIDE), SIDE)],
            sems.at[pos],
        )
        copy.start()
        copies.append(copy)
    first = low_lanes((META, SIDE))
    for owner in range(owners):
        both = jnp.where(first, corner_ref[owner * CAP], corner_ref[owner * CAP + 1])
        meta_ref[owner] = both.astype(jnp.float32)
    copy = pltpu.make_async_copy(
        meta_ref, send_ref.at[:, pl.ds(CAP * SIDE, META)], sems.at[positions]
    )
    copy.start()
    copies.append(copy)
    for copy in copies:
        copy.wait()


def pack(offsets, measured, owners):
    positions = measured.shape[0]
    return pl.pallas_call(
        pack_kernel,
        out_shape=jax.ShapeDtypeStruct((owners, CAP * SIDE + META, SIDE), jnp.float32),
        in_specs=[
            pl.BlockSpec(memory_space=pltpu.SMEM),
            pl.BlockSpec(memory_space=pltpu.VMEM),
        ],
        out_specs=pl.BlockSpec(memory_space=pl.ANY),
        scratch_shapes=[
            pltpu.VMEM((owners, META, SIDE), jnp.float32),
            pltpu.SMEM((owners,), jnp.int32),
            pltpu.SMEM((owners * CAP,), jnp.int32),
            pltpu.SemaphoreType.DMA((positions + 1,)),
        ],
        compiler_params=pltpu.CompilerParams(vmem_limit_bytes=VMEM_LIMIT),
        cost_estimate=pl.CostEstimate(
            flops=0, bytes_accessed=40 * 1024 * 1024, transcendentals=0
        ),
        name="pack_measured",
    )(offsets, measured)


def pair_places(rows, cols):
    row_blocks = rows // BLOCK
    edge = cols - SIDE
    last = tuple((row_blocks - 1, col) for col in range(0, cols, SIDE))
    side = tuple((row, edge) for row in range(row_blocks - 1))
    inner = tuple((row, col) for row in range(row_blocks - 1) for col in range(0, edge, SIDE))
    return last, side, inner


def forward_pairs(places, ext_ref, probe_ref, tables, far_refs, enter_refs):
    probe_re = probe_ref[0]
    probe_im = probe_ref[1]
    rows = []
    for row, col in places:
        trans = [cut_pair(ext_ref, comp, row * BLOCK, col) for comp in range(2)]
        rows.append(
            stacked([times(probe_re, probe_im, trans[0][n], trans[1][n]) for n in range(2)])
        )
    enters = two_sided(rows, tables, 0, 2)
    rows = []
    for pair, (row, col) in enumerate(places):
        enter = enters[pair]
        enter_refs[pair][...] = enter
        trans = [cut_pair(ext_ref, comp, row * BLOCK, col) for comp in range(2, 4)]
        rows.append(
            stacked([times(*halves(enter, n), trans[0][n], trans[1][n]) for n in range(2)])
        )
    fars = two_sided(rows, tables, 4, 6)
    for far_ref, far in zip(far_refs, fars):
        far_ref[...] = far


def each(ref):
    return [ref.at[pair] for pair in range(ref.shape[0])]


def start_copies(parts, sems):
    copies = [
        pltpu.make_async_copy(source, target, sems.at[n])
        for n, (source, target) in enumerate(parts)
    ]
    for copy in copies:
        copy.start()
    return copies


def wait_copies(copies):
    for copy in copies:
        copy.wait()


def forward_inner_kernel(places, tile_ref, probe_ref, tables, far_ref, enter_ref):
    forward_pairs(places, tile_ref, probe_ref, tables, each(far_ref), each(enter_ref))


def forward_side_kernel(
    places, tile_ref, right_ref, probe_ref, tables, far_ref, enter_ref, ext_ref, sems
):
    cols = tile_ref.shape[2]
    wait_copies(
        start_copies(
            [
                (tile_ref.at[:, :, pl.ds(cols - SIDE, SIDE)], ext_ref.at[:, :, pl.ds(0, SIDE)]),
                (right_ref, ext_ref.at[:, :, pl.ds(SIDE, SIDE)]),
            ],
            sems,
        )
    )
    forward_pairs(
        [(row, 0) for row, _ in places], ext_ref, probe_ref, tables, each(far_ref), each(enter_ref)
    )


def forward_last_kernel(
    places,
    tile_ref,
    below_ref,
    right_ref,
    diag_ref,
    probe_ref,
    tables,
    far_ref,
    enter_ref,
    ext_ref,
    sems,
):
    rows, cols = tile_ref.shape[1:]
    low = pl.ds(rows - BLOCK, BLOCK)
    upper, lower = pl.ds(0, BLOCK), pl.ds(BLOCK, BLOCK)
    wide, beyond = pl.ds(0, cols), pl.ds(cols, SIDE)
    wait_copies(
        start_copies(
            [
                (tile_ref.at[:, low], ext_ref.at[:, upper, wide]),
                (below_ref, ext_ref.at[:, lower, wide]),
                (right_ref.at[:, low], ext_ref.at[:, upper, beyond]),
                (diag_ref, ext_ref.at[:, lower, beyond]),
            ],
            sems,
        )
    )
    forward_pairs(
        [(0, col) for _, col in places], ext_ref, probe_ref, tables, each(far_ref), each(enter_ref)
    )


def stage_cost(pairs):
    return pl.CostEstimate(
        flops=pairs * 4 * 3 * 2 * 256**3, bytes_accessed=1024 * 1024, transcendentals=0
    )


def fields(places):
    field = jax.ShapeDtypeStruct((len(places), 2 * SIDE, 2 * SIDE), jnp.float32)
    return field, field


def in_vmem(count):
    return [pl.BlockSpec(memory_space=pltpu.VMEM)] * count


def anywhere(count):
    return [pl.BlockSpec(memory_space=pl.ANY)] * count


def in_hbm(count):
    return [pl.BlockSpec(memory_space=pltpu.HBM)] * count


def forward_inner(places, tile, probe, tables):
    return pl.pallas_call(
        functools.partial(forward_inner_kernel, places),
        out_shape=fields(places),
        in_specs=in_vmem(3),
        out_specs=tuple(in_vmem(2)),
        compiler_params=pltpu.CompilerParams(vmem_limit_bytes=VMEM_LIMIT),
        cost_estimate=stage_cost(8 * len(places)),
        name="forward_inner",
    )(tile, probe, tables)


def extended_shape(tile, comps):
    return pltpu.VMEM((comps, tile.shape[1] + BLOCK, tile.shape[2] + SIDE), jnp.float32)


def forward_side(places, tile, right, probe, tables):
    comps, rows, _ = tile.shape
    return pl.pallas_call(
        functools.partial(forward_side_kernel, places),
        out_shape=fields(places),
        in_specs=in_hbm(2) + in_vmem(2),
        out_specs=tuple(in_vmem(2)),
        scratch_shapes=[
            pltpu.VMEM((comps, rows, 2 * SIDE), jnp.float32),
            pltpu.SemaphoreType.DMA((2,)),
        ],
        compiler_params=pltpu.CompilerParams(vmem_limit_bytes=VMEM_LIMIT),
        cost_estimate=stage_cost(8 * len(places)),
        name="forward_last_column",
    )(tile, right, probe, tables)


def forward_last(places, tile, below, right, diag, probe, tables):
    comps, _, cols = tile.shape
    return pl.pallas_call(
        functools.partial(forward_last_kernel, places),
        out_shape=fields(places),
        in_specs=in_hbm(4) + in_vmem(2),
        out_specs=tuple(in_vmem(2)),
        scratch_shapes=[
            pltpu.VMEM((comps, SIDE, cols + SIDE), jnp.float32),
            pltpu.SemaphoreType.DMA((4,)),
        ],
        compiler_params=pltpu.CompilerParams(vmem_limit_bytes=VMEM_LIMIT),
        cost_estimate=stage_cost(8 * len(places)),
        name="forward_last_row",
    )(tile, below, right, diag, probe, tables)


def gather_sums(meta_ref, items_ref, sum_ref, count_ref, arrivals):
    spare = sum_ref.shape[0] - 1
    sources = items_ref.shape[0]
    for corner in range(spare + 1):
        count_ref[corner] = 0
    for source in range(sources):
        if source % (sources // len(arrivals)) == 0:
            arrivals[source * len(arrivals) // sources].wait()
        for rank in range(CAP):
            corner = meta_ref[source, rank * BLOCK].astype(jnp.int32)
            at = jnp.where(corner < 0, spare, corner)
            hits = count_ref[at]
            count_ref[at] = hits + 1
            item = items_ref[source, rank * SIDE : (rank + 1) * SIDE]
            sum_ref[at] = jnp.where(hits > 0, sum_ref[at], 0.0) + item


def summed(sum_ref, count_ref, at):
    hits = count_ref[at]
    return hits.astype(jnp.float32), jnp.where(hits > 0, sum_ref[at], 0.0)


def backward_pairs(
    places,
    width,
    probe_ref,
    tables,
    far_ref,
    enter_ref,
    ext_ref,
    sum_ref,
    count_ref,
    store,
    before_pair,
    before_products,
    before_fields,
    after_fields,
):
    rows = []
    for pair, (row, col) in enumerate(places):
        before_pair(pair)
        waves = []
        for n in range(2):
            at = row * width + col // BLOCK + n
            hits, total = summed(sum_ref, count_ref, at)
            far_re, far_im = halves(far_ref[pair], n)
            misfit = 2.0 * (hits * (far_re * far_re + far_im * far_im) - total)
            waves.append((misfit * far_re, misfit * far_im))
        rows.append(stacked(waves))
    before_products()
    backs = two_sided(rows, tables, 6, 4)
    before_fields()
    rows = []
    for pair, (row, col) in enumerate(places):
        trans = [cut_pair(ext_ref, comp, row * BLOCK, col) for comp in range(2)]
        waves = []
        for n in range(2):
            back = halves(backs[pair], n)
            grad = conj_times(*halves(enter_ref[pair], n), *back)
            store(n, 2, row, col, grad[0])
            store(n, 3, row, col, grad[1])
            waves.append(conj_times(trans[0][n], trans[1][n], *back))
        rows.append(stacked(waves))
    after_fields()
    backs = two_sided(rows, tables, 2, 0)
    probe_re = probe_ref[0]
    probe_im = probe_ref[1]
    for pair, (row, col) in enumerate(places):
        for n in range(2):
            grad = conj_times(probe_re, probe_im, *halves(backs[pair], n))
            store(n, 0, row, col, grad[0])
            store(n, 1, row, col, grad[1])


def shifted(low, high):
    if low is None:
        low = jnp.zeros_like(high)
    if high is None:
        high = jnp.zeros_like(low)
    return pltpu.roll(jnp.where(low_lanes(low.shape), high, low), BLOCK, 1)


def backward_rim_kernel(
    places,
    recv_ref,
    tile_ref,
    below_ref,
    right_ref,
    diag_ref,
    probe_ref,
    tables_ref,
    far_last_ref,
    enter_last_ref,
    far_side_ref,
    enter_side_ref,
    row_ref,
    col_ref,
    out_below_ref,
    out_right_ref,
    out_diag_ref,
    out_sum_ref,
    count_ref,
    items_ref,
    meta_ref,
    table_buf,
    probe_buf,
    far_buf,
    enter_buf,
    ext_ref,
    sum_ref,
    even_ref,
    odd_ref,
    even_side_ref,
    odd_side_ref,
    row_buf,
    col_buf,
    below_buf,
    right_buf,
    diag_buf,
    sems,
    out_sems,
):
    rows, cols = tile_ref.shape[1:]
    last = rows // BLOCK - 1
    corners = sum_ref.shape[0] - 1
    near = far_last_ref.shape[0]
    first = pl.ds(0, near)
    others = pl.ds(near, far_side_ref.shape[0])
    two = pl.ds(2, 2)
    chunk = recv_ref.shape[0] // CHUNKS
    wide = pl.ds(0, cols)
    beyond = pl.ds(cols, SIDE)
    copies = start_copies(
        [(recv_ref.at[:, CAP * SIDE], meta_ref)]
        + [
            (recv_ref.at[part, pl.ds(0, CAP * SIDE)], items_ref.at[part])
            for part in (pl.ds(n * chunk, chunk) for n in range(CHUNKS))
        ]
        + [
            (far_last_ref, far_buf.at[first]),
            (tables_ref, table_buf),
            (far_side_ref, far_buf.at[others]),
            (enter_last_ref, enter_buf.at[first]),
            (enter_side_ref, enter_buf.at[others]),
            (tile_ref.at[two], ext_ref.at[:, pl.ds(0, rows), wide]),
            (below_ref.at[two], ext_ref.at[:, pl.ds(rows, BLOCK), wide]),
            (right_ref.at[two], ext_ref.at[:, pl.ds(0, rows), beyond]),
            (diag_ref.at[two], ext_ref.at[:, pl.ds(rows, BLOCK), beyond]),
            (probe_ref, probe_buf),
        ],
        sems,
    )
    wait_copies(copies[:1])
    rest = copies[1 + CHUNKS :]
    gather_sums(meta_ref, items_ref, sum_ref, count_ref, copies[1 : 1 + CHUNKS])
    bands = (even_ref, odd_ref)
    sides = (even_side_ref, odd_side_ref)
    stores = start_copies(
        [(sum_ref.at[pl.ds(0, corners)], out_sum_ref)], out_sems.at[pl.ds(20, 1)]
    )

    def store(n, comp, row, col, value):
        if row == last:
            bands[n][comp, :, col : col + SIDE] = value
        else:
            at = row * BLOCK
            top = value[:BLOCK]
            if row > 0:
                top = top + sides[n][comp, at : at + BLOCK]
            sides[n][comp, at : at + BLOCK] = top
            sides[n][comp, at + BLOCK : at + SIDE] = value[BLOCK:]

    half = rows // 2

    def finish(comp):
        beyond_cols = []
        for buf, part in ((row_buf, slice(0, BLOCK)), (below_buf, slice(BLOCK, SIDE))):
            before = None
            for col in range(0, cols, SIDE):
                here = odd_ref[comp, part, col : col + SIDE]
                buf[comp, :, col : col + SIDE] = even_ref[
                    comp, part, col : col + SIDE
                ] + shifted(before, here)
                before = here
            beyond_cols.append(shifted(before, None))
        corner = beyond_cols[1]
        diag_buf[comp] = corner[: BLOCK // 2] + pltpu.roll(corner[BLOCK // 2 :], BLOCK, 1)
        odd_side = odd_side_ref[comp]
        col_buf[comp] = even_side_ref[comp] + shifted(None, odd_side)
        side = shifted(odd_side, None)
        second = jnp.concatenate(
            [side[half : rows - BLOCK], side[rows - BLOCK :] + beyond_cols[0]], axis=0
        )
        right_buf[comp] = side[:half] + pltpu.roll(second, BLOCK, 1)
        stores.extend(
            start_copies(
                [
                    (below_buf.at[comp], out_below_ref.at[comp]),
                    (diag_buf.at[comp], out_diag_ref.at[comp]),
                    (right_buf.at[comp], out_right_ref.at[comp]),
                    (row_buf.at[comp], row_ref.at[comp]),
                    (col_buf.at[comp], col_ref.at[comp]),
                ],
                out_sems.at[pl.ds(5 * comp, 5)],
            )
        )

    def before_pair(pair):
        if pair == 0:
            rest[0].wait()
        if pair == near:
            rest[2].wait()

    def after_fields():
        finish(2)
        finish(3)

    backward_pairs(
        places,
        cols // BLOCK,
        probe_buf,
        table_buf,
        far_buf,
        enter_buf,
        ext_ref,
        sum_ref,
        count_ref,
        store,
        before_pair,
        lambda: wait_copies(rest[1:2]),
        lambda: wait_copies(rest[3:]),
        after_fields,
    )
    finish(0)
    finish(1)
    wait_copies(stores)


def backward_inner_kernel(
    places,
    count_ref,
    sum_ref,
    tile_ref,
    probe_ref,
    tables_ref,
    far_ref,
    enter_ref,
    row_ref,
    col_ref,
    out_ref,
    sum_buf,
    trans_buf,
    probe_buf,
    table_buf,
    far_buf,
    enter_buf,
    row_buf,
    col_buf,
    out_buf,
    even_ref,
    odd_ref,
    sems,
    out_sems,
):
    comps, rows, cols = out_buf.shape
    last = rows - BLOCK
    width = cols // BLOCK
    acc = (even_ref, odd_ref)
    row_blocks = last // BLOCK
    group = len(places) // row_blocks
    parts = []
    for n in range(row_blocks):
        here = pl.ds(n * width, width)
        parts.append((sum_ref.at[here], sum_buf.at[here]))
        here = pl.ds(n * group, group)
        parts.append((far_ref.at[here], far_buf.at[here]))
        if n == 0:
            parts.append((tables_ref, table_buf))
    copies = start_copies(
        parts
        + [
            (enter_ref, enter_buf),
            (tile_ref.at[pl.ds(2, 2)], trans_buf),
            (probe_ref, probe_buf),
            (row_ref, row_buf),
            (col_ref, col_buf),
        ],
        sems,
    )
    table_copy = copies.pop(2)
    rest = copies[2 * row_blocks :]
    stores = []

    def store(n, comp, row, col, value):
        at = row * BLOCK
        lanes = slice(col, col + SIDE)
        top = value[:BLOCK]
        if row > 0:
            top = top + acc[n][comp, at : at + BLOCK, lanes]
        acc[n][comp, at : at + BLOCK, lanes] = top
        acc[n][comp, at + BLOCK : at + SIDE, lanes] = value[BLOCK:]

    def finish(comp):
        before = None
        for col in range(0, cols, SIDE):
            lanes = slice(col, col + SIDE)
            if col < cols - SIDE:
                here = odd_ref[comp, :, lanes]
                value = even_ref[comp, :, lanes] + shifted(before, here)
                before = here
            else:
                value = col_buf[comp] + shifted(before, None)
            out_buf[comp, :last, lanes] = value[:last]
            out_buf[comp, last:, lanes] = value[last:] + row_buf[comp, :, lanes]
        stores.extend(
            start_copies(
                [(out_buf.at[comp], out_ref.at[comp])], out_sems.at[pl.ds(comp, 1)]
            )
        )

    def before_pair(pair):
        if pair % group == 0:
            at = 2 * (pair // group)
            wait_copies(copies[at : at + 2])

    def after_fields():
        finish(2)
        finish(3)

    backward_pairs(
        places,
        width,
        probe_buf,
        table_buf,
        far_buf,
        enter_buf,
        trans_buf,
        sum_buf,
        count_ref,
        store,
        before_pair,
        table_copy.wait,
        lambda: wait_copies(rest),
        after_fields,
    )
    finish(0)
    finish(1)
    wait_copies(stores)


def shapes_of(*shapes):
    return tuple(jax.ShapeDtypeStruct(shape, jnp.float32) for shape in shapes)


def backward_rim(places, recv, tile, below, right, diag, probe, tables, fields_last, fields_side):
    comps, rows, cols = tile.shape
    corners = (rows // BLOCK) * (cols // BLOCK)
    sources = recv.shape[0]
    field = (len(places), 2 * SIDE, 2 * SIDE)
    outs = (
        (comps, BLOCK, cols),
        (comps, rows, SIDE),
        (comps, BLOCK, cols),
        (comps, rows // 2, SIDE),
        (comps, BLOCK // 2, SIDE),
    )
    return pl.pallas_call(
        functools.partial(backward_rim_kernel, places),
        out_shape=shapes_of(*outs, (corners, SIDE, SIDE))
        + (jax.ShapeDtypeStruct((corners + 1,), jnp.int32),),
        in_specs=in_hbm(11),
        out_specs=tuple(in_hbm(6)) + (pl.BlockSpec(memory_space=pltpu.SMEM),),
        scratch_shapes=[
            pltpu.VMEM((sources, CAP * SIDE, SIDE), jnp.float32),
            pltpu.SMEM((sources, SIDE), jnp.float32),
            pltpu.VMEM(tables.shape, tables.dtype),
            pltpu.VMEM(probe.shape, jnp.float32),
            pltpu.VMEM(field, jnp.float32),
            pltpu.VMEM(field, jnp.float32),
            extended_shape(tile, 2),
            pltpu.VMEM((corners + 1, SIDE, SIDE), jnp.float32),
            pltpu.VMEM((comps, SIDE, cols), jnp.float32),
            pltpu.VMEM((comps, SIDE, cols), jnp.float32),
            pltpu.VMEM((comps, rows, SIDE), jnp.float32),
            pltpu.VMEM((comps, rows, SIDE), jnp.float32),
        ]
        + [pltpu.VMEM(shape, jnp.float32) for shape in outs]
        + [pltpu.SemaphoreType.DMA((CHUNKS + 11,)), pltpu.SemaphoreType.DMA((21,))],
        compiler_params=pltpu.CompilerParams(vmem_limit_bytes=VMEM_LIMIT),
        cost_estimate=stage_cost(len(places)),
        name="backward_rim",
    )(recv, tile, below, right, diag, probe, tables, *fields_last, *fields_side)


def backward_inner(places, count, sums, tile, probe, tables, far, enter, row, col):
    comps, rows, cols = tile.shape
    return pl.pallas_call(
        functools.partial(backward_inner_kernel, places),
        out_shape=jax.ShapeDtypeStruct(tile.shape, jnp.float32),
        in_specs=[pl.BlockSpec(memory_space=pltpu.SMEM)] + in_hbm(8),
        out_specs=in_hbm(1)[0],
        scratch_shapes=[
            pltpu.VMEM(sums.shape, jnp.float32),
            pltpu.VMEM((2, rows, cols), jnp.float32),
            pltpu.VMEM(probe.shape, jnp.float32),
            pltpu.VMEM(tables.shape, tables.dtype),
            pltpu.VMEM(far.shape, jnp.float32),
            pltpu.VMEM(enter.shape, jnp.float32),
            pltpu.VMEM(row.shape, jnp.float32),
            pltpu.VMEM(col.shape, jnp.float32),
            pltpu.VMEM(tile.shape, jnp.float32),
            pltpu.VMEM((comps, rows, cols - SIDE), jnp.float32),
            pltpu.VMEM((comps, rows, cols - SIDE), jnp.float32),
            pltpu.SemaphoreType.DMA((2 * (rows // BLOCK - 1) + 6,)),
            pltpu.SemaphoreType.DMA((comps,)),
        ],
        compiler_params=pltpu.CompilerParams(vmem_limit_bytes=VMEM_LIMIT),
        cost_estimate=stage_cost(len(places)),
        name="backward_inner",
    )(count, sums, tile, probe, tables, far, enter, row, col)


def border_kernel(
    own_ref, above_ref, left_ref, diag_ref, out_ref, top_ref, side_ref, row_buf, col_buf, diag_buf, sems
):
    rows = out_ref.shape[1]
    half = rows // 2
    top = out_ref.at[:, pl.ds(0, BLOCK)]
    side = out_ref.at[:, pl.ds(BLOCK, rows - BLOCK), pl.ds(0, SIDE)]
    loads = start_copies(
        [
            (above_ref, row_buf),
            (top, top_ref),
            (left_ref, col_buf),
            (diag_ref, diag_buf),
            (side, side_ref),
        ],
        sems,
    )
    def unpacked(packed):
        low = low_lanes(packed.shape)
        upper = jnp.where(low, packed, 0.0)
        return upper, pltpu.roll(jnp.where(low, 0.0, packed), BLOCK, 2)

    wait_copies(loads[:2])
    top_ref[...] = top_ref[...] + row_buf[...]
    wait_copies(loads[2:4])
    upper, lower = unpacked(col_buf[...])
    corner = jnp.concatenate(unpacked(diag_buf[...]), axis=1)
    top_ref[:, :, :SIDE] = top_ref[:, :, :SIDE] + upper[:, :BLOCK] + corner
    stores = start_copies([(top_ref, top)], sems.at[pl.ds(5, 1)])
    wait_copies(loads[4:])
    side_ref[:, : half - BLOCK] = side_ref[:, : half - BLOCK] + upper[:, BLOCK:]
    side_ref[:, half - BLOCK :] = side_ref[:, half - BLOCK :] + lower
    stores += start_copies([(side_ref, side)], sems.at[pl.ds(6, 1)])
    wait_copies(stores)


def add_borders(own, above, left, diag):
    comps, rows, cols = own.shape
    return pl.pallas_call(
        border_kernel,
        out_shape=jax.ShapeDtypeStruct(own.shape, jnp.float32),
        in_specs=anywhere(4),
        out_specs=pl.BlockSpec(memory_space=pl.ANY),
        scratch_shapes=[
            pltpu.VMEM((comps, BLOCK, cols), jnp.float32),
            pltpu.VMEM((comps, rows - BLOCK, SIDE), jnp.float32),
            pltpu.VMEM(above.shape, jnp.float32),
            pltpu.VMEM(left.shape, jnp.float32),
            pltpu.VMEM(diag.shape, jnp.float32),
            pltpu.SemaphoreType.DMA((7,)),
        ],
        input_output_aliases={0: 0},
        compiler_params=pltpu.CompilerParams(vmem_limit_bytes=VMEM_LIMIT),
        name="add_borders",
    )(own, above, left, diag)


def row_strip_kernel(tile_ref, row_ref, sems):
    wait_copies(start_copies([(tile_ref.at[:, pl.ds(0, BLOCK)], row_ref)], sems))


def row_strip(tile):
    comps, rows, cols = tile.shape
    return pl.pallas_call(
        row_strip_kernel,
        out_shape=jax.ShapeDtypeStruct((comps, BLOCK, cols), jnp.float32),
        in_specs=in_hbm(1),
        out_specs=in_vmem(1)[0],
        scratch_shapes=[pltpu.SemaphoreType.DMA((1,))],
        compiler_params=pltpu.CompilerParams(vmem_limit_bytes=VMEM_LIMIT),
        name="row_strip",
    )(tile)


def column_strip_kernel(tile_ref, send_ref, out_ref, sems):
    wait_copies(start_copies([(tile_ref.at[:, :, pl.ds(0, SIDE)], out_ref)], sems))


def column_strip(tile, send):
    comps, rows, cols = tile.shape
    return pl.pallas_call(
        column_strip_kernel,
        out_shape=jax.ShapeDtypeStruct((comps, rows, SIDE), jnp.float32),
        in_specs=in_hbm(2),
        out_specs=pl.BlockSpec(memory_space=pltpu.VMEM),
        scratch_shapes=[pltpu.SemaphoreType.DMA((1,))],
        compiler_params=pltpu.CompilerParams(vmem_limit_bytes=VMEM_LIMIT),
        name="column_strip",
    )(tile, send)


def moved(shard, down, across):
    row_total = lax.axis_size("row")
    col_total = lax.axis_size("col")
    if across == 0:
        pairs = [(r, r + down) for r in range(row_total) if 0 <= r + down < row_total]
        return lax.ppermute(shard, "row", pairs)
    if down == 0:
        pairs = [(c, c + across) for c in range(col_total) if 0 <= c + across < col_total]
        return lax.ppermute(shard, "col", pairs)
    pairs = [
        (r * col_total + c, (r + down) * col_total + c + across)
        for r in range(row_total)
        for c in range(col_total)
        if 0 <= r + down < row_total and 0 <= c + across < col_total
    ]
    return lax.ppermute(shard, ("row", "col"), pairs)


def body(object_slices, probe, measured, offsets):
    slices, parts, tile_rows, tile_cols = object_slices.shape
    tile = object_slices.reshape(slices * parts, tile_rows, tile_cols)
    row_total = lax.axis_size("row")
    tables = jnp.asarray(TABLES)
    below = moved(row_strip(tile), -1, 0)
    send = pack(offsets, measured, row_total)
    recv = lax.all_to_all(send, "row", split_axis=0, concat_axis=0, tiled=True)
    right = moved(column_strip(tile, send), 0, -1)
    last, side, inner = pair_places(tile_rows, tile_cols)
    far_inner, enter_inner = forward_inner(inner, tile, probe, tables)
    below, right, far_inner = lax.optimization_barrier((below, right, far_inner))
    diag = moved(below[:, :, :SIDE], 0, -1)
    far_side, enter_side = forward_side(side, tile, right, probe, tables)
    diag, far_side = lax.optimization_barrier((diag, far_side))
    far_last, enter_last = forward_last(last, tile, below, right, diag, probe, tables)
    row, col, to_below, to_right, to_diag, sums, count = backward_rim(
        last + side,
        recv,
        tile,
        below,
        right,
        diag,
        probe,
        tables,
        (far_last, enter_last),
        (far_side, enter_side),
    )
    above = moved(to_below, 1, 0)
    left = moved(to_right, 0, 1)
    corner_part = moved(to_diag, 1, 1)
    own = backward_inner(
        inner, count, sums, tile, probe, tables, far_inner, enter_inner, row, col
    )
    result = add_borders(own, above, left, corner_part)
    return result.reshape(object_slices.shape)


def solution(mesh):
    placed = (
        P(None, None, "row", "col"),
        P(),
        P(("row", "col"), None, None),
        P(None, ("row", "col")),
    )
    return jax.shard_map(
        body, mesh=mesh, in_specs=placed, out_specs=P(None, None, "row", "col"), check_vma=False
    )
```

```python
import functools
import math

import jax
import jax.numpy as jnp
import ml_dtypes
import numpy as np
from jax import lax
from jax.experimental import pallas as pl
from jax.experimental.pallas import tpu as pltpu
from jax.sharding import PartitionSpec as P

PHASE = 40.0
SIDE = 128
BLOCK = 64
CAP = 2
META = 8
CHUNKS = 4
VMEM_LIMIT = 64 * 1024 * 1024


def dft_matrix():
    index = np.arange(SIDE)
    angle = (index[:, None] * index[None, :] % SIDE) * (-2.0 * math.pi / SIDE)
    return np.exp(1j * angle) / math.sqrt(SIDE)


def propagation_matrix():
    index = np.arange(SIDE)
    freq = np.where(index < SIDE // 2, index, index - SIDE) / SIDE
    dft = dft_matrix()
    return np.conj(dft) @ (np.exp(-1j * PHASE * freq * freq)[:, None] * dft)


def real_forms(matrix):
    right = np.block([[matrix.real, matrix.imag], [-matrix.imag, matrix.real]])
    out = []
    for form in (right, right.T):
        form = form.astype(np.float32)
        high = form.astype(ml_dtypes.bfloat16)
        out.append(high)
        out.append((form - high.astype(np.float32)).astype(ml_dtypes.bfloat16))
    return np.stack(out)


TABLES = np.concatenate([real_forms(propagation_matrix()), real_forms(dft_matrix())])


def split(field):
    high = field.astype(jnp.bfloat16)
    low = (field - high.astype(jnp.float32)).astype(jnp.bfloat16)
    return high, low


def from_right(rows, tables, at):
    high, low = split(rows)
    left = jnp.concatenate([high, low, high], axis=1)
    right = jnp.concatenate([tables[at], tables[at], tables[at + 1]], axis=0)
    return jnp.dot(left, right, preferred_element_type=jnp.float32)


def from_left(columns, tables, at):
    high, low = split(columns)
    left = jnp.concatenate([tables[at], tables[at], tables[at + 1]], axis=1)
    right = jnp.concatenate([high, low, high], axis=0)
    return jnp.dot(left, right, preferred_element_type=jnp.float32)


def swap(pair):
    top = jnp.concatenate([pair[:SIDE, :SIDE], pair[SIDE:, :SIDE]], axis=1)
    bottom = jnp.concatenate([pair[:SIDE, SIDE:], pair[SIDE:, SIDE:]], axis=1)
    return jnp.concatenate([top, bottom], axis=0)


def two_sided(pairs, tables, right_at, left_at):
    pairs = [from_right(rows, tables, right_at) for rows in pairs]
    return [from_left(swap(rows), tables, left_at) for rows in pairs]


def stacked(fields):
    return jnp.concatenate([jnp.concatenate(field, axis=1) for field in fields], axis=0)


def halves(pair, n):
    return pair[:SIDE, n * SIDE : (n + 1) * SIDE], pair[SIDE:, n * SIDE : (n + 1) * SIDE]


def low_lanes(shape):
    return lax.broadcasted_iota(jnp.int32, shape, len(shape) - 1) < BLOCK


def cut_pair(ext_ref, comp, row, col):
    first = ext_ref[comp, row : row + SIDE, col : col + SIDE]
    second = ext_ref[comp, row : row + SIDE, col + SIDE : col + 2 * SIDE]
    mixed = jnp.where(low_lanes(first.shape), second, first)
    return first, pltpu.roll(mixed, BLOCK, 1)


def times(left_re, left_im, right_re, right_im):
    return (left_re * right_re - left_im * right_im, left_re * right_im + left_im * right_re)


def conj_times(left_re, left_im, right_re, right_im):
    return (left_re * right_re + left_im * right_im, left_re * right_im - left_im * right_re)


def pack_kernel(off_ref, meas_ref, send_ref, meta_ref, count_ref, corner_ref, sems):
    owners = send_ref.shape[0]
    positions = meas_ref.shape[0]
    for owner in range(owners):
        count_ref[owner] = 0
        for rank in range(CAP):
            corner_ref[owner * CAP + rank] = -1
    copies = []
    for pos in range(positions):
        y = off_ref[0, pos]
        x = off_ref[1, pos]
        owner = lax.shift_right_logical(y, 8)
        rank = jnp.minimum(count_ref[owner], CAP - 1)
        count_ref[owner] = rank + 1
        corner = (lax.shift_right_logical(y, 6) & 3) * 8 + (lax.shift_right_logical(x, 6) & 7)
        corner_ref[owner * CAP + rank] = corner
        copy = pltpu.make_async_copy(
            meas_ref.at[pos],
            send_ref.at[owner, pl.ds(pl.multiple_of(rank * SIDE, SIDE), SIDE)],
            sems.at[pos],
        )
        copy.start()
        copies.append(copy)
    first = low_lanes((META, SIDE))
    for owner in range(owners):
        both = jnp.where(first, corner_ref[owner * CAP], corner_ref[owner * CAP + 1])
        meta_ref[owner] = both.astype(jnp.float32)
    copy = pltpu.make_async_copy(
        meta_ref, send_ref.at[:, pl.ds(CAP * SIDE, META)], sems.at[positions]
    )
    copy.start()
    copies.append(copy)
    for copy in copies:
        copy.wait()


def pack(offsets, measured, owners):
    positions = measured.shape[0]
    return pl.pallas_call(
        pack_kernel,
        out_shape=jax.ShapeDtypeStruct((owners, CAP * SIDE + META, SIDE), jnp.float32),
        in_specs=[
            pl.BlockSpec(memory_space=pltpu.SMEM),
            pl.BlockSpec(memory_space=pltpu.VMEM),
        ],
        out_specs=pl.BlockSpec(memory_space=pl.ANY),
        scratch_shapes=[
            pltpu.VMEM((owners, META, SIDE), jnp.float32),
            pltpu.SMEM((owners,), jnp.int32),
            pltpu.SMEM((owners * CAP,), jnp.int32),
            pltpu.SemaphoreType.DMA((positions + 1,)),
        ],
        compiler_params=pltpu.CompilerParams(vmem_limit_bytes=VMEM_LIMIT),
        cost_estimate=pl.CostEstimate(
            flops=0, bytes_accessed=40 * 1024 * 1024, transcendentals=0
        ),
        name="pack_measured",
    )(offsets, measured)


def pair_places(rows, cols):
    row_blocks = rows // BLOCK
    edge = cols - SIDE
    last = tuple((row_blocks - 1, col) for col in range(0, cols, SIDE))
    side = tuple((row, edge) for row in range(row_blocks - 1))
    inner = tuple((row, col) for row in range(row_blocks - 1) for col in range(0, edge, SIDE))
    return last, side, inner


def forward_pairs(places, ext_ref, probe_ref, tables, far_refs, enter_refs):
    probe_re = probe_ref[0]
    probe_im = probe_ref[1]
    rows = []
    for row, col in places:
        trans = [cut_pair(ext_ref, comp, row * BLOCK, col) for comp in range(2)]
        rows.append(
            stacked([times(probe_re, probe_im, trans[0][n], trans[1][n]) for n in range(2)])
        )
    enters = two_sided(rows, tables, 0, 2)
    rows = []
    for pair, (row, col) in enumerate(places):
        enter = enters[pair]
        enter_refs[pair][...] = enter
        trans = [cut_pair(ext_ref, comp, row * BLOCK, col) for comp in range(2, 4)]
        rows.append(
            stacked([times(*halves(enter, n), trans[0][n], trans[1][n]) for n in range(2)])
        )
    fars = two_sided(rows, tables, 4, 6)
    for far_ref, far in zip(far_refs, fars):
        far_ref[...] = far


def each(ref):
    return [ref.at[pair] for pair in range(ref.shape[0])]


def start_copies(parts, sems):
    copies = [
        pltpu.make_async_copy(source, target, sems.at[n])
        for n, (source, target) in enumerate(parts)
    ]
    for copy in copies:
        copy.start()
    return copies


def wait_copies(copies):
    for copy in copies:
        copy.wait()


def forward_inner_kernel(places, tile_ref, probe_ref, tables, far_ref, enter_ref):
    forward_pairs(places, tile_ref, probe_ref, tables, each(far_ref), each(enter_ref))


def forward_side_kernel(
    places, tile_ref, right_ref, probe_ref, tables, far_ref, enter_ref, ext_ref, sems
):
    cols = tile_ref.shape[2]
    wait_copies(
        start_copies(
            [
                (tile_ref.at[:, :, pl.ds(cols - SIDE, SIDE)], ext_ref.at[:, :, pl.ds(0, SIDE)]),
                (right_ref, ext_ref.at[:, :, pl.ds(SIDE, SIDE)]),
            ],
            sems,
        )
    )
    forward_pairs(
        [(row, 0) for row, _ in places], ext_ref, probe_ref, tables, each(far_ref), each(enter_ref)
    )


def forward_last_kernel(
    places,
    tile_ref,
    below_ref,
    right_ref,
    diag_ref,
    probe_ref,
    tables,
    far_ref,
    enter_ref,
    ext_ref,
    sems,
):
    rows, cols = tile_ref.shape[1:]
    low = pl.ds(rows - BLOCK, BLOCK)
    upper, lower = pl.ds(0, BLOCK), pl.ds(BLOCK, BLOCK)
    wide, beyond = pl.ds(0, cols), pl.ds(cols, SIDE)
    wait_copies(
        start_copies(
            [
                (tile_ref.at[:, low], ext_ref.at[:, upper, wide]),
                (below_ref, ext_ref.at[:, lower, wide]),
                (right_ref.at[:, low], ext_ref.at[:, upper, beyond]),
                (diag_ref, ext_ref.at[:, lower, beyond]),
            ],
            sems,
        )
    )
    forward_pairs(
        [(0, col) for _, col in places], ext_ref, probe_ref, tables, each(far_ref), each(enter_ref)
    )


def stage_cost(pairs):
    return pl.CostEstimate(
        flops=pairs * 4 * 3 * 2 * 256**3, bytes_accessed=1024 * 1024, transcendentals=0
    )


def fields(places):
    field = jax.ShapeDtypeStruct((len(places), 2 * SIDE, 2 * SIDE), jnp.float32)
    return field, field


def in_vmem(count):
    return [pl.BlockSpec(memory_space=pltpu.VMEM)] * count


def anywhere(count):
    return [pl.BlockSpec(memory_space=pl.ANY)] * count


def in_hbm(count):
    return [pl.BlockSpec(memory_space=pltpu.HBM)] * count


def forward_inner(places, tile, probe, tables):
    return pl.pallas_call(
        functools.partial(forward_inner_kernel, places),
        out_shape=fields(places),
        in_specs=in_vmem(3),
        out_specs=tuple(in_vmem(2)),
        compiler_params=pltpu.CompilerParams(vmem_limit_bytes=VMEM_LIMIT),
        cost_estimate=stage_cost(8 * len(places)),
        name="forward_inner",
    )(tile, probe, tables)


def extended_shape(tile, comps):
    return pltpu.VMEM((comps, tile.shape[1] + BLOCK, tile.shape[2] + SIDE), jnp.float32)


def forward_side(places, tile, right, probe, tables):
    comps, rows, _ = tile.shape
    return pl.pallas_call(
        functools.partial(forward_side_kernel, places),
        out_shape=fields(places),
        in_specs=in_hbm(2) + in_vmem(2),
        out_specs=tuple(in_vmem(2)),
        scratch_shapes=[
            pltpu.VMEM((comps, rows, 2 * SIDE), jnp.float32),
            pltpu.SemaphoreType.DMA((2,)),
        ],
        compiler_params=pltpu.CompilerParams(vmem_limit_bytes=VMEM_LIMIT),
        cost_estimate=stage_cost(8 * len(places)),
        name="forward_last_column",
    )(tile, right, probe, tables)


def forward_last(places, tile, below, right, diag, probe, tables):
    comps, _, cols = tile.shape
    return pl.pallas_call(
        functools.partial(forward_last_kernel, places),
        out_shape=fields(places),
        in_specs=in_hbm(4) + in_vmem(2),
        out_specs=tuple(in_vmem(2)),
        scratch_shapes=[
            pltpu.VMEM((comps, SIDE, cols + SIDE), jnp.float32),
            pltpu.SemaphoreType.DMA((4,)),
        ],
        compiler_params=pltpu.CompilerParams(vmem_limit_bytes=VMEM_LIMIT),
        cost_estimate=stage_cost(8 * len(places)),
        name="forward_last_row",
    )(tile, below, right, diag, probe, tables)


def gather_sums(meta_ref, items_ref, sum_ref, count_ref, arrivals):
    spare = sum_ref.shape[0] - 1
    sources = items_ref.shape[0]
    for corner in range(spare + 1):
        count_ref[corner] = 0
    for source in range(sources):
        if source % (sources // len(arrivals)) == 0:
            arrivals[source * len(arrivals) // sources].wait()
        for rank in range(CAP):
            corner = meta_ref[source, rank * BLOCK].astype(jnp.int32)
            at = jnp.where(corner < 0, spare, corner)
            hits = count_ref[at]
            count_ref[at] = hits + 1
            item = items_ref[source, rank * SIDE : (rank + 1) * SIDE]
            sum_ref[at] = jnp.where(hits > 0, sum_ref[at], 0.0) + item


def summed(sum_ref, count_ref, at):
    hits = count_ref[at]
    return hits.astype(jnp.float32), jnp.where(hits > 0, sum_ref[at], 0.0)


def backward_pairs(
    places,
    width,
    probe_ref,
    tables,
    far_ref,
    enter_ref,
    ext_ref,
    sum_ref,
    count_ref,
    store,
    before_pair,
    before_products,
    before_fields,
    after_fields,
):
    rows = []
    for pair, (row, col) in enumerate(places):
        before_pair(pair)
        waves = []
        for n in range(2):
            at = row * width + col // BLOCK + n
            hits, total = summed(sum_ref, count_ref, at)
            far_re, far_im = halves(far_ref[pair], n)
            misfit = 2.0 * (hits * (far_re * far_re + far_im * far_im) - total)
            waves.append((misfit * far_re, misfit * far_im))
        rows.append(stacked(waves))
    before_products()
    backs = two_sided(rows, tables, 6, 4)
    before_fields()
    rows = []
    for pair, (row, col) in enumerate(places):
        trans = [cut_pair(ext_ref, comp, row * BLOCK, col) for comp in range(2)]
        waves = []
        for n in range(2):
            back = halves(backs[pair], n)
            grad = conj_times(*halves(enter_ref[pair], n), *back)
            store(n, 2, row, col, grad[0])
            store(n, 3, row, col, grad[1])
            waves.append(conj_times(trans[0][n], trans[1][n], *back))
        rows.append(stacked(waves))
    after_fields()
    backs = two_sided(rows, tables, 2, 0)
    probe_re = probe_ref[0]
    probe_im = probe_ref[1]
    for pair, (row, col) in enumerate(places):
        for n in range(2):
            grad = conj_times(probe_re, probe_im, *halves(backs[pair], n))
            store(n, 0, row, col, grad[0])
            store(n, 1, row, col, grad[1])


def shifted(low, high):
    if low is None:
        low = jnp.zeros_like(high)
    if high is None:
        high = jnp.zeros_like(low)
    return pltpu.roll(jnp.where(low_lanes(low.shape), high, low), BLOCK, 1)


def backward_rim_kernel(
    places,
    recv_ref,
    tile_ref,
    below_ref,
    right_ref,
    diag_ref,
    probe_ref,
    tables_ref,
    far_last_ref,
    enter_last_ref,
    far_side_ref,
    enter_side_ref,
    row_ref,
    col_ref,
    out_below_ref,
    out_right_ref,
    out_diag_ref,
    out_sum_ref,
    count_ref,
    items_ref,
    meta_ref,
    table_buf,
    probe_buf,
    far_buf,
    enter_buf,
    ext_ref,
    sum_ref,
    even_ref,
    odd_ref,
    even_side_ref,
    odd_side_ref,
    row_buf,
    col_buf,
    below_buf,
    right_buf,
    diag_buf,
    sems,
    out_sems,
):
    rows, cols = tile_ref.shape[1:]
    last = rows // BLOCK - 1
    corners = sum_ref.shape[0] - 1
    near = far_last_ref.shape[0]
    first = pl.ds(0, near)
    others = pl.ds(near, far_side_ref.shape[0])
    two = pl.ds(2, 2)
    chunk = recv_ref.shape[0] // CHUNKS
    wide = pl.ds(0, cols)
    beyond = pl.ds(cols, SIDE)
    copies = start_copies(
        [(recv_ref.at[:, CAP * SIDE], meta_ref)]
        + [
            (recv_ref.at[part, pl.ds(0, CAP * SIDE)], items_ref.at[part])
            for part in (pl.ds(n * chunk, chunk) for n in range(CHUNKS))
        ]
        + [
            (far_last_ref, far_buf.at[first]),
            (tables_ref, table_buf),
            (far_side_ref, far_buf.at[others]),
            (enter_last_ref, enter_buf.at[first]),
            (enter_side_ref, enter_buf.at[others]),
            (tile_ref.at[two], ext_ref.at[:, pl.ds(0, rows), wide]),
            (below_ref.at[two], ext_ref.at[:, pl.ds(rows, BLOCK), wide]),
            (right_ref.at[two], ext_ref.at[:, pl.ds(0, rows), beyond]),
            (diag_ref.at[two], ext_ref.at[:, pl.ds(rows, BLOCK), beyond]),
            (probe_ref, probe_buf),
        ],
        sems,
    )
    wait_copies(copies[:1])
    rest = copies[1 + CHUNKS :]
    gather_sums(meta_ref, items_ref, sum_ref, count_ref, copies[1 : 1 + CHUNKS])
    bands = (even_ref, odd_ref)
    sides = (even_side_ref, odd_side_ref)
    stores = start_copies(
        [(sum_ref.at[pl.ds(0, corners)], out_sum_ref)], out_sems.at[pl.ds(20, 1)]
    )

    def store(n, comp, row, col, value):
        if row == last:
            bands[n][comp, :, col : col + SIDE] = value
        else:
            at = row * BLOCK
            top = value[:BLOCK]
            if row > 0:
                top = top + sides[n][comp, at : at + BLOCK]
            sides[n][comp, at : at + BLOCK] = top
            sides[n][comp, at + BLOCK : at + SIDE] = value[BLOCK:]

    half = rows // 2

    def finish(comp):
        beyond_cols = []
        for buf, part in ((row_buf, slice(0, BLOCK)), (below_buf, slice(BLOCK, SIDE))):
            before = None
            for col in range(0, cols, SIDE):
                here = odd_ref[comp, part, col : col + SIDE]
                buf[comp, :, col : col + SIDE] = even_ref[
                    comp, part, col : col + SIDE
                ] + shifted(before, here)
                before = here
            beyond_cols.append(shifted(before, None))
        corner = beyond_cols[1]
        diag_buf[comp] = corner[: BLOCK // 2] + pltpu.roll(corner[BLOCK // 2 :], BLOCK, 1)
        odd_side = odd_side_ref[comp]
        col_buf[comp] = even_side_ref[comp] + shifted(None, odd_side)
        side = shifted(odd_side, None)
        second = jnp.concatenate(
            [side[half : rows - BLOCK], side[rows - BLOCK :] + beyond_cols[0]], axis=0
        )
        right_buf[comp] = side[:half] + pltpu.roll(second, BLOCK, 1)
        stores.extend(
            start_copies(
                [
                    (below_buf.at[comp], out_below_ref.at[comp]),
                    (diag_buf.at[comp], out_diag_ref.at[comp]),
                    (right_buf.at[comp], out_right_ref.at[comp]),
                    (row_buf.at[comp], row_ref.at[comp]),
                    (col_buf.at[comp], col_ref.at[comp]),
                ],
                out_sems.at[pl.ds(5 * comp, 5)],
            )
        )

    def before_pair(pair):
        if pair == 0:
            rest[0].wait()
        if pair == near:
            rest[2].wait()

    def after_fields():
        finish(2)
        finish(3)

    backward_pairs(
        places,
        cols // BLOCK,
        probe_buf,
        table_buf,
        far_buf,
        enter_buf,
        ext_ref,
        sum_ref,
        count_ref,
        store,
        before_pair,
        lambda: wait_copies(rest[1:2]),
        lambda: wait_copies(rest[3:]),
        after_fields,
    )
    finish(0)
    finish(1)
    wait_copies(stores)


def backward_inner_kernel(
    places,
    count_ref,
    sum_ref,
    tile_ref,
    probe_ref,
    tables_ref,
    far_ref,
    enter_ref,
    row_ref,
    col_ref,
    out_ref,
    sum_buf,
    trans_buf,
    probe_buf,
    table_buf,
    far_buf,
    enter_buf,
    row_buf,
    col_buf,
    out_buf,
    even_ref,
    odd_ref,
    sems,
    out_sems,
):
    comps, rows, cols = out_buf.shape
    last = rows - BLOCK
    width = cols // BLOCK
    acc = (even_ref, odd_ref)
    row_blocks = last // BLOCK
    group = len(places) // row_blocks
    parts = []
    for n in range(row_blocks):
        here = pl.ds(n * width, width)
        parts.append((sum_ref.at[here], sum_buf.at[here]))
        here = pl.ds(n * group, group)
        parts.append((far_ref.at[here], far_buf.at[here]))
        if n == 0:
            parts.append((tables_ref, table_buf))
    copies = start_copies(
        parts
        + [
            (enter_ref, enter_buf),
            (tile_ref.at[pl.ds(2, 2)], trans_buf),
            (probe_ref, probe_buf),
            (row_ref, row_buf),
            (col_ref, col_buf),
        ],
        sems,
    )
    table_copy = copies.pop(2)
    rest = copies[2 * row_blocks :]
    stores = []

    def store(n, comp, row, col, value):
        at = row * BLOCK
        lanes = slice(col, col + SIDE)
        top = value[:BLOCK]
        if row > 0:
            top = top + acc[n][comp, at : at + BLOCK, lanes]
        acc[n][comp, at : at + BLOCK, lanes] = top
        acc[n][comp, at + BLOCK : at + SIDE, lanes] = value[BLOCK:]

    def finish(comp):
        before = None
        for col in range(0, cols, SIDE):
            lanes = slice(col, col + SIDE)
            if col < cols - SIDE:
                here = odd_ref[comp, :, lanes]
                value = even_ref[comp, :, lanes] + shifted(before, here)
                before = here
            else:
                value = col_buf[comp] + shifted(before, None)
            out_buf[comp, :last, lanes] = value[:last]
            out_buf[comp, last:, lanes] = value[last:] + row_buf[comp, :, lanes]
        stores.extend(
            start_copies(
                [(out_buf.at[comp], out_ref.at[comp])], out_sems.at[pl.ds(comp, 1)]
            )
        )

    def before_pair(pair):
        if pair % group == 0:
            at = 2 * (pair // group)
            wait_copies(copies[at : at + 2])

    def after_fields():
        finish(2)
        finish(3)

    backward_pairs(
        places,
        width,
        probe_buf,
        table_buf,
        far_buf,
        enter_buf,
        trans_buf,
        sum_buf,
        count_ref,
        store,
        before_pair,
        table_copy.wait,
        lambda: wait_copies(rest),
        after_fields,
    )
    finish(0)
    finish(1)
    wait_copies(stores)


def shapes_of(*shapes):
    return tuple(jax.ShapeDtypeStruct(shape, jnp.float32) for shape in shapes)


def backward_rim(places, recv, tile, below, right, diag, probe, tables, fields_last, fields_side):
    comps, rows, cols = tile.shape
    corners = (rows // BLOCK) * (cols // BLOCK)
    sources = recv.shape[0]
    field = (len(places), 2 * SIDE, 2 * SIDE)
    outs = (
        (comps, BLOCK, cols),
        (comps, rows, SIDE),
        (comps, BLOCK, cols),
        (comps, rows // 2, SIDE),
        (comps, BLOCK // 2, SIDE),
    )
    return pl.pallas_call(
        functools.partial(backward_rim_kernel, places),
        out_shape=shapes_of(*outs, (corners, SIDE, SIDE))
        + (jax.ShapeDtypeStruct((corners + 1,), jnp.int32),),
        in_specs=in_hbm(11),
        out_specs=tuple(in_hbm(6)) + (pl.BlockSpec(memory_space=pltpu.SMEM),),
        scratch_shapes=[
            pltpu.VMEM((sources, CAP * SIDE, SIDE), jnp.float32),
            pltpu.SMEM((sources, SIDE), jnp.float32),
            pltpu.VMEM(tables.shape, tables.dtype),
            pltpu.VMEM(probe.shape, jnp.float32),
            pltpu.VMEM(field, jnp.float32),
            pltpu.VMEM(field, jnp.float32),
            extended_shape(tile, 2),
            pltpu.VMEM((corners + 1, SIDE, SIDE), jnp.float32),
            pltpu.VMEM((comps, SIDE, cols), jnp.float32),
            pltpu.VMEM((comps, SIDE, cols), jnp.float32),
            pltpu.VMEM((comps, rows, SIDE), jnp.float32),
            pltpu.VMEM((comps, rows, SIDE), jnp.float32),
        ]
        + [pltpu.VMEM(shape, jnp.float32) for shape in outs]
        + [pltpu.SemaphoreType.DMA((CHUNKS + 11,)), pltpu.SemaphoreType.DMA((21,))],
        compiler_params=pltpu.CompilerParams(vmem_limit_bytes=VMEM_LIMIT),
        cost_estimate=stage_cost(len(places)),
        name="backward_rim",
    )(recv, tile, below, right, diag, probe, tables, *fields_last, *fields_side)


def backward_inner(places, count, sums, tile, probe, tables, far, enter, row, col):
    comps, rows, cols = tile.shape
    return pl.pallas_call(
        functools.partial(backward_inner_kernel, places),
        out_shape=jax.ShapeDtypeStruct(tile.shape, jnp.float32),
        in_specs=[pl.BlockSpec(memory_space=pltpu.SMEM)] + in_hbm(8),
        out_specs=in_hbm(1)[0],
        scratch_shapes=[
            pltpu.VMEM(sums.shape, jnp.float32),
            pltpu.VMEM((2, rows, cols), jnp.float32),
            pltpu.VMEM(probe.shape, jnp.float32),
            pltpu.VMEM(tables.shape, tables.dtype),
            pltpu.VMEM(far.shape, jnp.float32),
            pltpu.VMEM(enter.shape, jnp.float32),
            pltpu.VMEM(row.shape, jnp.float32),
            pltpu.VMEM(col.shape, jnp.float32),
            pltpu.VMEM(tile.shape, jnp.float32),
            pltpu.VMEM((comps, rows, cols - SIDE), jnp.float32),
            pltpu.VMEM((comps, rows, cols - SIDE), jnp.float32),
            pltpu.SemaphoreType.DMA((2 * (rows // BLOCK - 1) + 6,)),
            pltpu.SemaphoreType.DMA((comps,)),
        ],
        compiler_params=pltpu.CompilerParams(vmem_limit_bytes=VMEM_LIMIT),
        cost_estimate=stage_cost(len(places)),
        name="backward_inner",
    )(count, sums, tile, probe, tables, far, enter, row, col)


def border_kernel(
    own_ref, above_ref, left_ref, diag_ref, out_ref, top_ref, side_ref, row_buf, col_buf, diag_buf, sems
):
    rows = out_ref.shape[1]
    half = rows // 2
    top = out_ref.at[:, pl.ds(0, BLOCK)]
    side = out_ref.at[:, pl.ds(BLOCK, rows - BLOCK), pl.ds(0, SIDE)]
    loads = start_copies(
        [
            (above_ref, row_buf),
            (top, top_ref),
            (left_ref, col_buf),
            (diag_ref, diag_buf),
            (side, side_ref),
        ],
        sems,
    )
    def unpacked(packed):
        low = low_lanes(packed.shape)
        upper = jnp.where(low, packed, 0.0)
        return upper, pltpu.roll(jnp.where(low, 0.0, packed), BLOCK, 2)

    wait_copies(loads[:2])
    top_ref[...] = top_ref[...] + row_buf[...]
    wait_copies(loads[2:4])
    upper, lower = unpacked(col_buf[...])
    corner = jnp.concatenate(unpacked(diag_buf[...]), axis=1)
    top_ref[:, :, :SIDE] = top_ref[:, :, :SIDE] + upper[:, :BLOCK] + corner
    stores = start_copies([(top_ref, top)], sems.at[pl.ds(5, 1)])
    wait_copies(loads[4:])
    side_ref[:, : half - BLOCK] = side_ref[:, : half - BLOCK] + upper[:, BLOCK:]
    side_ref[:, half - BLOCK :] = side_ref[:, half - BLOCK :] + lower
    stores += start_copies([(side_ref, side)], sems.at[pl.ds(6, 1)])
    wait_copies(stores)


def add_borders(own, above, left, diag):
    comps, rows, cols = own.shape
    return pl.pallas_call(
        border_kernel,
        out_shape=jax.ShapeDtypeStruct(own.shape, jnp.float32),
        in_specs=anywhere(4),
        out_specs=pl.BlockSpec(memory_space=pl.ANY),
        scratch_shapes=[
            pltpu.VMEM((comps, BLOCK, cols), jnp.float32),
            pltpu.VMEM((comps, rows - BLOCK, SIDE), jnp.float32),
            pltpu.VMEM(above.shape, jnp.float32),
            pltpu.VMEM(left.shape, jnp.float32),
            pltpu.VMEM(diag.shape, jnp.float32),
            pltpu.SemaphoreType.DMA((7,)),
        ],
        input_output_aliases={0: 0},
        compiler_params=pltpu.CompilerParams(vmem_limit_bytes=VMEM_LIMIT),
        name="add_borders",
    )(own, above, left, diag)


def row_strip_kernel(tile_ref, row_ref, sems):
    wait_copies(start_copies([(tile_ref.at[:, pl.ds(0, BLOCK)], row_ref)], sems))


def row_strip(tile):
    comps, rows, cols = tile.shape
    return pl.pallas_call(
        row_strip_kernel,
        out_shape=jax.ShapeDtypeStruct((comps, BLOCK, cols), jnp.float32),
        in_specs=in_hbm(1),
        out_specs=in_vmem(1)[0],
        scratch_shapes=[pltpu.SemaphoreType.DMA((1,))],
        compiler_params=pltpu.CompilerParams(vmem_limit_bytes=VMEM_LIMIT),
        name="row_strip",
    )(tile)


def column_strip_kernel(tile_ref, send_ref, out_ref, sems):
    wait_copies(start_copies([(tile_ref.at[:, :, pl.ds(0, SIDE)], out_ref)], sems))


def column_strip(tile, send):
    comps, rows, cols = tile.shape
    return pl.pallas_call(
        column_strip_kernel,
        out_shape=jax.ShapeDtypeStruct((comps, rows, SIDE), jnp.float32),
        in_specs=in_hbm(2),
        out_specs=pl.BlockSpec(memory_space=pltpu.VMEM),
        scratch_shapes=[pltpu.SemaphoreType.DMA((1,))],
        compiler_params=pltpu.CompilerParams(vmem_limit_bytes=VMEM_LIMIT),
        name="column_strip",
    )(tile, send)


def moved(shard, down, across):
    row_total = lax.axis_size("row")
    col_total = lax.axis_size("col")
    if across == 0:
        pairs = [(r, r + down) for r in range(row_total) if 0 <= r + down < row_total]
        return lax.ppermute(shard, "row", pairs)
    if down == 0:
        pairs = [(c, c + across) for c in range(col_total) if 0 <= c + across < col_total]
        return lax.ppermute(shard, "col", pairs)
    pairs = [
        (r * col_total + c, (r + down) * col_total + c + across)
        for r in range(row_total)
        for c in range(col_total)
        if 0 <= r + down < row_total and 0 <= c + across < col_total
    ]
    return lax.ppermute(shard, ("row", "col"), pairs)


def body(object_slices, probe, measured, offsets):
    slices, parts, tile_rows, tile_cols = object_slices.shape
    tile = object_slices.reshape(slices * parts, tile_rows, tile_cols)
    row_total = lax.axis_size("row")
    tables = jnp.asarray(TABLES)
    below = moved(row_strip(tile), -1, 0)
    send = pack(offsets, measured, row_total)
    recv = lax.all_to_all(send, "row", split_axis=0, concat_axis=0, tiled=True)
    right = moved(column_strip(tile, send), 0, -1)
    last, side, inner = pair_places(tile_rows, tile_cols)
    far_inner, enter_inner = forward_inner(inner, tile, probe, tables)
    right, far_inner = lax.optimization_barrier((right, far_inner))
    far_side, enter_side = forward_side(side, tile, right, probe, tables)
    below, far_side = lax.optimization_barrier((below, far_side))
    diag = moved(below[:, :, :SIDE], 0, -1)
    far_last, enter_last = forward_last(last, tile, below, right, diag, probe, tables)
    row, col, to_below, to_right, to_diag, sums, count = backward_rim(
        last + side,
        recv,
        tile,
        below,
        right,
        diag,
        probe,
        tables,
        (far_last, enter_last),
        (far_side, enter_side),
    )
    above = moved(to_below, 1, 0)
    left = moved(to_right, 0, 1)
    corner_part = moved(to_diag, 1, 1)
    own = backward_inner(
        inner, count, sums, tile, probe, tables, far_inner, enter_inner, row, col
    )
    result = add_borders(own, above, left, corner_part)
    return result.reshape(object_slices.shape)


def solution(mesh):
    placed = (
        P(None, None, "row", "col"),
        P(),
        P(("row", "col"), None, None),
        P(None, ("row", "col")),
    )
    return jax.shard_map(
        body, mesh=mesh, in_specs=placed, out_specs=P(None, None, "row", "col"), check_vma=False
    )
```

```python
import functools
import math

import jax
import jax.numpy as jnp
import ml_dtypes
import numpy as np
from jax import lax
from jax.experimental import pallas as pl
from jax.experimental.pallas import tpu as pltpu
from jax.sharding import PartitionSpec as P

PHASE = 40.0
SIDE = 128
BLOCK = 64
CAP = 2
META = 8
CHUNKS = 4
VMEM_LIMIT = 64 * 1024 * 1024


def dft_matrix():
    index = np.arange(SIDE)
    angle = (index[:, None] * index[None, :] % SIDE) * (-2.0 * math.pi / SIDE)
    return np.exp(1j * angle) / math.sqrt(SIDE)


def propagation_matrix():
    index = np.arange(SIDE)
    freq = np.where(index < SIDE // 2, index, index - SIDE) / SIDE
    dft = dft_matrix()
    return np.conj(dft) @ (np.exp(-1j * PHASE * freq * freq)[:, None] * dft)


def real_forms(matrix):
    right = np.block([[matrix.real, matrix.imag], [-matrix.imag, matrix.real]])
    out = []
    for form in (right, right.T):
        form = form.astype(np.float32)
        high = form.astype(ml_dtypes.bfloat16)
        out.append(high)
        out.append((form - high.astype(np.float32)).astype(ml_dtypes.bfloat16))
    return np.stack(out)


TABLES = np.concatenate([real_forms(propagation_matrix()), real_forms(dft_matrix())])


def split(field):
    high = field.astype(jnp.bfloat16)
    low = (field - high.astype(jnp.float32)).astype(jnp.bfloat16)
    return high, low


def from_right(rows, tables, at):
    high, low = split(rows)
    left = jnp.concatenate([high, low, high], axis=1)
    right = jnp.concatenate([tables[at], tables[at], tables[at + 1]], axis=0)
    return jnp.dot(left, right, preferred_element_type=jnp.float32)


def from_left(columns, tables, at):
    high, low = split(columns)
    left = jnp.concatenate([tables[at], tables[at], tables[at + 1]], axis=1)
    right = jnp.concatenate([high, low, high], axis=0)
    return jnp.dot(left, right, preferred_element_type=jnp.float32)


def swap(pair):
    top = jnp.concatenate([pair[:SIDE, :SIDE], pair[SIDE:, :SIDE]], axis=1)
    bottom = jnp.concatenate([pair[:SIDE, SIDE:], pair[SIDE:, SIDE:]], axis=1)
    return jnp.concatenate([top, bottom], axis=0)


def two_sided(pairs, tables, right_at, left_at):
    pairs = [from_right(rows, tables, right_at) for rows in pairs]
    return [from_left(swap(rows), tables, left_at) for rows in pairs]


def stacked(fields):
    return jnp.concatenate([jnp.concatenate(field, axis=1) for field in fields], axis=0)


def halves(pair, n):
    return pair[:SIDE, n * SIDE : (n + 1) * SIDE], pair[SIDE:, n * SIDE : (n + 1) * SIDE]


def low_lanes(shape):
    return lax.broadcasted_iota(jnp.int32, shape, len(shape) - 1) < BLOCK


def cut_pair(ext_ref, comp, row, col):
    first = ext_ref[comp, row : row + SIDE, col : col + SIDE]
    second = ext_ref[comp, row : row + SIDE, col + SIDE : col + 2 * SIDE]
    mixed = jnp.where(low_lanes(first.shape), second, first)
    return first, pltpu.roll(mixed, BLOCK, 1)


def times(left_re, left_im, right_re, right_im):
    return (left_re * right_re - left_im * right_im, left_re * right_im + left_im * right_re)


def conj_times(left_re, left_im, right_re, right_im):
    return (left_re * right_re + left_im * right_im, left_re * right_im - left_im * right_re)


def pack_kernel(off_ref, meas_ref, send_ref, meta_ref, count_ref, corner_ref, sems):
    owners = send_ref.shape[0]
    positions = meas_ref.shape[0]
    for owner in range(owners):
        count_ref[owner] = 0
        for rank in range(CAP):
            corner_ref[owner * CAP + rank] = -1
    copies = []
    for pos in range(positions):
        y = off_ref[0, pos]
        x = off_ref[1, pos]
        owner = lax.shift_right_logical(y, 8)
        rank = jnp.minimum(count_ref[owner], CAP - 1)
        count_ref[owner] = rank + 1
        corner = (lax.shift_right_logical(y, 6) & 3) * 8 + (lax.shift_right_logical(x, 6) & 7)
        corner_ref[owner * CAP + rank] = corner
        copy = pltpu.make_async_copy(
            meas_ref.at[pos],
            send_ref.at[owner, pl.ds(pl.multiple_of(rank * SIDE, SIDE), SIDE)],
            sems.at[pos],
        )
        copy.start()
        copies.append(copy)
    first = low_lanes((META, SIDE))
    for owner in range(owners):
        both = jnp.where(first, corner_ref[owner * CAP], corner_ref[owner * CAP + 1])
        meta_ref[owner] = both.astype(jnp.float32)
    copy = pltpu.make_async_copy(
        meta_ref, send_ref.at[:, pl.ds(CAP * SIDE, META)], sems.at[positions]
    )
    copy.start()
    copies.append(copy)
    for copy in copies:
        copy.wait()


def pack(offsets, measured, owners):
    positions = measured.shape[0]
    return pl.pallas_call(
        pack_kernel,
        out_shape=jax.ShapeDtypeStruct((owners, CAP * SIDE + META, SIDE), jnp.float32),
        in_specs=[
            pl.BlockSpec(memory_space=pltpu.SMEM),
            pl.BlockSpec(memory_space=pltpu.VMEM),
        ],
        out_specs=pl.BlockSpec(memory_space=pl.ANY),
        scratch_shapes=[
            pltpu.VMEM((owners, META, SIDE), jnp.float32),
            pltpu.SMEM((owners,), jnp.int32),
            pltpu.SMEM((owners * CAP,), jnp.int32),
            pltpu.SemaphoreType.DMA((positions + 1,)),
        ],
        compiler_params=pltpu.CompilerParams(vmem_limit_bytes=VMEM_LIMIT),
        cost_estimate=pl.CostEstimate(
            flops=0, bytes_accessed=40 * 1024 * 1024, transcendentals=0
        ),
        name="pack_measured",
    )(offsets, measured)


def pair_places(rows, cols):
    row_blocks = rows // BLOCK
    edge = cols - SIDE
    last = tuple((row_blocks - 1, col) for col in range(0, cols, SIDE))
    side = tuple((row, edge) for row in range(row_blocks - 1))
    inner = tuple((row, col) for row in range(row_blocks - 1) for col in range(0, edge, SIDE))
    return last, side, inner


def forward_pairs(places, ext_ref, probe_ref, tables, far_refs, enter_refs, entered):
    probe_re = probe_ref[0]
    probe_im = probe_ref[1]
    rows = []
    for row, col in places:
        trans = [cut_pair(ext_ref, comp, row * BLOCK, col) for comp in range(2)]
        rows.append(
            stacked([times(probe_re, probe_im, trans[0][n], trans[1][n]) for n in range(2)])
        )
    enters = two_sided(rows, tables, 0, 2)
    rows = []
    for pair, (row, col) in enumerate(places):
        enter = enters[pair]
        enter_refs[pair][...] = enter
        trans = [cut_pair(ext_ref, comp, row * BLOCK, col) for comp in range(2, 4)]
        rows.append(
            stacked([times(*halves(enter, n), trans[0][n], trans[1][n]) for n in range(2)])
        )
    entered()
    fars = two_sided(rows, tables, 4, 6)
    for far_ref, far in zip(far_refs, fars):
        far_ref[...] = far


def each(ref):
    return [ref.at[pair] for pair in range(ref.shape[0])]


def start_copies(parts, sems):
    copies = [
        pltpu.make_async_copy(source, target, sems.at[n])
        for n, (source, target) in enumerate(parts)
    ]
    for copy in copies:
        copy.start()
    return copies


def wait_copies(copies):
    for copy in copies:
        copy.wait()


def forward_kernel(places, layout, count, *refs):
    sources = refs[:count]
    probe_ref, tables_ref, far_ref, enter_ref = refs[count : count + 4]
    ext_ref, probe_buf, table_buf, far_buf, enter_buf, sems, out_sems = refs[count + 4 :]
    wait_copies(
        start_copies(
            [(tables_ref, table_buf), (probe_ref, probe_buf)] + layout(ext_ref, *sources), sems
        )
    )
    stores = []

    def entered():
        stores.extend(start_copies([(enter_buf, enter_ref)], out_sems.at[pl.ds(0, 1)]))

    forward_pairs(
        places, ext_ref, probe_buf, table_buf, each(far_buf), each(enter_buf), entered
    )
    stores.extend(start_copies([(far_buf, far_ref)], out_sems.at[pl.ds(1, 1)]))
    wait_copies(stores)


def stage_cost(pairs):
    return pl.CostEstimate(
        flops=pairs * 4 * 3 * 2 * 256**3, bytes_accessed=1024 * 1024, transcendentals=0
    )


def fields(places):
    field = jax.ShapeDtypeStruct((len(places), 2 * SIDE, 2 * SIDE), jnp.float32)
    return field, field


def in_vmem(count):
    return [pl.BlockSpec(memory_space=pltpu.VMEM)] * count


def anywhere(count):
    return [pl.BlockSpec(memory_space=pl.ANY)] * count


def in_hbm(count):
    return [pl.BlockSpec(memory_space=pltpu.HBM)] * count


def forward(name, places, layout, ext, sources, probe, tables):
    field = (len(places), 2 * SIDE, 2 * SIDE)
    return pl.pallas_call(
        functools.partial(forward_kernel, places, layout, len(sources)),
        out_shape=fields(places),
        in_specs=in_hbm(len(sources) + 2),
        out_specs=tuple(in_hbm(2)),
        scratch_shapes=[
            pltpu.VMEM(ext, jnp.float32),
            pltpu.VMEM(probe.shape, jnp.float32),
            pltpu.VMEM(tables.shape, tables.dtype),
            pltpu.VMEM(field, jnp.float32),
            pltpu.VMEM(field, jnp.float32),
            pltpu.SemaphoreType.DMA((len(sources) + 2,)),
            pltpu.SemaphoreType.DMA((2,)),
        ],
        compiler_params=pltpu.CompilerParams(vmem_limit_bytes=VMEM_LIMIT),
        cost_estimate=stage_cost(8 * len(places)),
        name=name,
    )(*sources, probe, tables)


def forward_inner(places, tile, probe, tables):
    def layout(ext_ref, tile_ref):
        return [(tile_ref, ext_ref)]

    return forward("forward_inner", places, layout, tile.shape, (tile,), probe, tables)


def extended_shape(tile, comps):
    return pltpu.VMEM((comps, tile.shape[1] + BLOCK, tile.shape[2] + SIDE), jnp.float32)


def forward_side(places, tile, right, probe, tables):
    comps, rows, cols = tile.shape

    def layout(ext_ref, tile_ref, right_ref):
        return [
            (tile_ref.at[:, :, pl.ds(cols - SIDE, SIDE)], ext_ref.at[:, :, pl.ds(0, SIDE)]),
            (right_ref, ext_ref.at[:, :, pl.ds(SIDE, SIDE)]),
        ]

    here = [(row, 0) for row, _ in places]
    ext = (comps, rows, 2 * SIDE)
    return forward("forward_last_column", here, layout, ext, (tile, right), probe, tables)


def forward_last(places, tile, below, right, diag, probe, tables):
    comps, rows, cols = tile.shape

    def layout(ext_ref, tile_ref, below_ref, right_ref, diag_ref):
        low = pl.ds(rows - BLOCK, BLOCK)
        upper, lower = pl.ds(0, BLOCK), pl.ds(BLOCK, BLOCK)
        wide, beyond = pl.ds(0, cols), pl.ds(cols, SIDE)
        return [
            (tile_ref.at[:, low], ext_ref.at[:, upper, wide]),
            (below_ref, ext_ref.at[:, lower, wide]),
            (right_ref.at[:, low], ext_ref.at[:, upper, beyond]),
            (diag_ref, ext_ref.at[:, lower, beyond]),
        ]

    here = [(0, col) for _, col in places]
    ext = (comps, SIDE, cols + SIDE)
    sources = (tile, below, right, diag)
    return forward("forward_last_row", here, layout, ext, sources, probe, tables)


def gather_sums(meta_ref, items_ref, sum_ref, count_ref, arrivals):
    spare = sum_ref.shape[0] - 1
    sources = items_ref.shape[0]
    for corner in range(spare + 1):
        count_ref[corner] = 0
    for source in range(sources):
        if source % (sources // len(arrivals)) == 0:
            arrivals[source * len(arrivals) // sources].wait()
        for rank in range(CAP):
            corner = meta_ref[source, rank * BLOCK].astype(jnp.int32)
            at = jnp.where(corner < 0, spare, corner)
            hits = count_ref[at]
            count_ref[at] = hits + 1
            item = items_ref[source, rank * SIDE : (rank + 1) * SIDE]
            sum_ref[at] = jnp.where(hits > 0, sum_ref[at], 0.0) + item


def summed(sum_ref, count_ref, at):
    hits = count_ref[at]
    return hits.astype(jnp.float32), jnp.where(hits > 0, sum_ref[at], 0.0)


def backward_pairs(
    places,
    width,
    probe_ref,
    tables,
    far_ref,
    enter_ref,
    ext_ref,
    sum_ref,
    count_ref,
    store,
    before_pair,
    before_products,
    before_fields,
    after_fields,
):
    rows = []
    for pair, (row, col) in enumerate(places):
        before_pair(pair)
        waves = []
        for n in range(2):
            at = row * width + col // BLOCK + n
            hits, total = summed(sum_ref, count_ref, at)
            far_re, far_im = halves(far_ref[pair], n)
            misfit = 2.0 * (hits * (far_re * far_re + far_im * far_im) - total)
            waves.append((misfit * far_re, misfit * far_im))
        rows.append(stacked(waves))
    before_products()
    backs = two_sided(rows, tables, 6, 4)
    before_fields()
    rows = []
    for pair, (row, col) in enumerate(places):
        trans = [cut_pair(ext_ref, comp, row * BLOCK, col) for comp in range(2)]
        waves = []
        for n in range(2):
            back = halves(backs[pair], n)
            grad = conj_times(*halves(enter_ref[pair], n), *back)
            store(n, 2, row, col, grad[0])
            store(n, 3, row, col, grad[1])
            waves.append(conj_times(trans[0][n], trans[1][n], *back))
        rows.append(stacked(waves))
    after_fields()
    backs = two_sided(rows, tables, 2, 0)
    probe_re = probe_ref[0]
    probe_im = probe_ref[1]
    for pair, (row, col) in enumerate(places):
        for n in range(2):
            grad = conj_times(probe_re, probe_im, *halves(backs[pair], n))
            store(n, 0, row, col, grad[0])
            store(n, 1, row, col, grad[1])


def shifted(low, high):
    if low is None:
        low = jnp.zeros_like(high)
    if high is None:
        high = jnp.zeros_like(low)
    return pltpu.roll(jnp.where(low_lanes(low.shape), high, low), BLOCK, 1)


def backward_rim_kernel(
    places,
    recv_ref,
    tile_ref,
    below_ref,
    right_ref,
    diag_ref,
    probe_ref,
    tables_ref,
    far_last_ref,
    enter_last_ref,
    far_side_ref,
    enter_side_ref,
    row_ref,
    col_ref,
    out_below_ref,
    out_right_ref,
    out_diag_ref,
    out_sum_ref,
    count_ref,
    items_ref,
    meta_ref,
    table_buf,
    probe_buf,
    far_buf,
    enter_buf,
    ext_ref,
    sum_ref,
    even_ref,
    odd_ref,
    even_side_ref,
    odd_side_ref,
    row_buf,
    col_buf,
    below_buf,
    right_buf,
    diag_buf,
    sems,
    out_sems,
):
    rows, cols = tile_ref.shape[1:]
    last = rows // BLOCK - 1
    corners = sum_ref.shape[0] - 1
    near = far_last_ref.shape[0]
    first = pl.ds(0, near)
    others = pl.ds(near, far_side_ref.shape[0])
    two = pl.ds(2, 2)
    chunk = recv_ref.shape[0] // CHUNKS
    wide = pl.ds(0, cols)
    beyond = pl.ds(cols, SIDE)
    copies = start_copies(
        [(recv_ref.at[:, CAP * SIDE], meta_ref)]
        + [
            (recv_ref.at[part, pl.ds(0, CAP * SIDE)], items_ref.at[part])
            for part in (pl.ds(n * chunk, chunk) for n in range(CHUNKS))
        ]
        + [
            (far_last_ref, far_buf.at[first]),
            (tables_ref, table_buf),
            (far_side_ref, far_buf.at[others]),
            (enter_last_ref, enter_buf.at[first]),
            (enter_side_ref, enter_buf.at[others]),
            (tile_ref.at[two], ext_ref.at[:, pl.ds(0, rows), wide]),
            (below_ref.at[two], ext_ref.at[:, pl.ds(rows, BLOCK), wide]),
            (right_ref.at[two], ext_ref.at[:, pl.ds(0, rows), beyond]),
            (diag_ref.at[two], ext_ref.at[:, pl.ds(rows, BLOCK), beyond]),
            (probe_ref, probe_buf),
        ],
        sems,
    )
    wait_copies(copies[:1])
    rest = copies[1 + CHUNKS :]
    gather_sums(meta_ref, items_ref, sum_ref, count_ref, copies[1 : 1 + CHUNKS])
    bands = (even_ref, odd_ref)
    sides = (even_side_ref, odd_side_ref)
    stores = start_copies(
        [(sum_ref.at[pl.ds(0, corners)], out_sum_ref)], out_sems.at[pl.ds(20, 1)]
    )

    def store(n, comp, row, col, value):
        if row == last:
            bands[n][comp, :, col : col + SIDE] = value
        else:
            at = row * BLOCK
            top = value[:BLOCK]
            if row > 0:
                top = top + sides[n][comp, at : at + BLOCK]
            sides[n][comp, at : at + BLOCK] = top
            sides[n][comp, at + BLOCK : at + SIDE] = value[BLOCK:]

    half = rows // 2

    def finish(comp):
        beyond_cols = []
        for buf, part in ((row_buf, slice(0, BLOCK)), (below_buf, slice(BLOCK, SIDE))):
            before = None
            for col in range(0, cols, SIDE):
                here = odd_ref[comp, part, col : col + SIDE]
                buf[comp, :, col : col + SIDE] = even_ref[
                    comp, part, col : col + SIDE
                ] + shifted(before, here)
                before = here
            beyond_cols.append(shifted(before, None))
        corner = beyond_cols[1]
        diag_buf[comp] = corner[: BLOCK // 2] + pltpu.roll(corner[BLOCK // 2 :], BLOCK, 1)
        odd_side = odd_side_ref[comp]
        col_buf[comp] = even_side_ref[comp] + shifted(None, odd_side)
        side = shifted(odd_side, None)
        second = jnp.concatenate(
            [side[half : rows - BLOCK], side[rows - BLOCK :] + beyond_cols[0]], axis=0
        )
        right_buf[comp] = side[:half] + pltpu.roll(second, BLOCK, 1)
        stores.extend(
            start_copies(
                [
                    (below_buf.at[comp], out_below_ref.at[comp]),
                    (diag_buf.at[comp], out_diag_ref.at[comp]),
                    (right_buf.at[comp], out_right_ref.at[comp]),
                    (row_buf.at[comp], row_ref.at[comp]),
                    (col_buf.at[comp], col_ref.at[comp]),
                ],
                out_sems.at[pl.ds(5 * comp, 5)],
            )
        )

    def before_pair(pair):
        if pair == 0:
            rest[0].wait()
        if pair == near:
            rest[2].wait()

    def after_fields():
        finish(2)
        finish(3)

    backward_pairs(
        places,
        cols // BLOCK,
        probe_buf,
        table_buf,
        far_buf,
        enter_buf,
        ext_ref,
        sum_ref,
        count_ref,
        store,
        before_pair,
        lambda: wait_copies(rest[1:2]),
        lambda: wait_copies(rest[3:]),
        after_fields,
    )
    finish(0)
    finish(1)
    wait_copies(stores)


def backward_inner_kernel(
    places,
    count_ref,
    sum_ref,
    tile_ref,
    probe_ref,
    tables_ref,
    far_ref,
    enter_ref,
    row_ref,
    col_ref,
    out_ref,
    sum_buf,
    trans_buf,
    probe_buf,
    table_buf,
    far_buf,
    enter_buf,
    row_buf,
    col_buf,
    out_buf,
    even_ref,
    odd_ref,
    sems,
    out_sems,
):
    comps, rows, cols = out_buf.shape
    last = rows - BLOCK
    width = cols // BLOCK
    acc = (even_ref, odd_ref)
    row_blocks = last // BLOCK
    group = len(places) // row_blocks
    parts = []
    for n in range(row_blocks):
        here = pl.ds(n * width, width)
        parts.append((sum_ref.at[here], sum_buf.at[here]))
        here = pl.ds(n * group, group)
        parts.append((far_ref.at[here], far_buf.at[here]))
        if n == 0:
            parts.append((tables_ref, table_buf))
    copies = start_copies(
        parts
        + [
            (enter_ref, enter_buf),
            (tile_ref.at[pl.ds(2, 2)], trans_buf),
            (probe_ref, probe_buf),
            (row_ref, row_buf),
            (col_ref, col_buf),
        ],
        sems,
    )
    table_copy = copies.pop(2)
    rest = copies[2 * row_blocks :]
    stores = []

    def store(n, comp, row, col, value):
        at = row * BLOCK
        lanes = slice(col, col + SIDE)
        top = value[:BLOCK]
        if row > 0:
            top = top + acc[n][comp, at : at + BLOCK, lanes]
        acc[n][comp, at : at + BLOCK, lanes] = top
        acc[n][comp, at + BLOCK : at + SIDE, lanes] = value[BLOCK:]

    def finish(comp):
        before = None
        for col in range(0, cols, SIDE):
            lanes = slice(col, col + SIDE)
            if col < cols - SIDE:
                here = odd_ref[comp, :, lanes]
                value = even_ref[comp, :, lanes] + shifted(before, here)
                before = here
            else:
                value = col_buf[comp] + shifted(before, None)
            out_buf[comp, :last, lanes] = value[:last]
            out_buf[comp, last:, lanes] = value[last:] + row_buf[comp, :, lanes]
        stores.extend(
            start_copies(
                [(out_buf.at[comp], out_ref.at[comp])], out_sems.at[pl.ds(comp, 1)]
            )
        )

    def before_pair(pair):
        if pair % group == 0:
            at = 2 * (pair // group)
            wait_copies(copies[at : at + 2])

    def after_fields():
        finish(2)
        finish(3)

    backward_pairs(
        places,
        width,
        probe_buf,
        table_buf,
        far_buf,
        enter_buf,
        trans_buf,
        sum_buf,
        count_ref,
        store,
        before_pair,
        table_copy.wait,
        lambda: wait_copies(rest),
        after_fields,
    )
    finish(0)
    finish(1)
    wait_copies(stores)


def shapes_of(*shapes):
    return tuple(jax.ShapeDtypeStruct(shape, jnp.float32) for shape in shapes)


def backward_rim(places, recv, tile, below, right, diag, probe, tables, fields_last, fields_side):
    comps, rows, cols = tile.shape
    corners = (rows // BLOCK) * (cols // BLOCK)
    sources = recv.shape[0]
    field = (len(places), 2 * SIDE, 2 * SIDE)
    outs = (
        (comps, BLOCK, cols),
        (comps, rows, SIDE),
        (comps, BLOCK, cols),
        (comps, rows // 2, SIDE),
        (comps, BLOCK // 2, SIDE),
    )
    return pl.pallas_call(
        functools.partial(backward_rim_kernel, places),
        out_shape=shapes_of(*outs, (corners, SIDE, SIDE))
        + (jax.ShapeDtypeStruct((corners + 1,), jnp.int32),),
        in_specs=in_hbm(11),
        out_specs=tuple(in_hbm(6)) + (pl.BlockSpec(memory_space=pltpu.SMEM),),
        scratch_shapes=[
            pltpu.VMEM((sources, CAP * SIDE, SIDE), jnp.float32),
            pltpu.SMEM((sources, SIDE), jnp.float32),
            pltpu.VMEM(tables.shape, tables.dtype),
            pltpu.VMEM(probe.shape, jnp.float32),
            pltpu.VMEM(field, jnp.float32),
            pltpu.VMEM(field, jnp.float32),
            extended_shape(tile, 2),
            pltpu.VMEM((corners + 1, SIDE, SIDE), jnp.float32),
            pltpu.VMEM((comps, SIDE, cols), jnp.float32),
            pltpu.VMEM((comps, SIDE, cols), jnp.float32),
            pltpu.VMEM((comps, rows, SIDE), jnp.float32),
            pltpu.VMEM((comps, rows, SIDE), jnp.float32),
        ]
        + [pltpu.VMEM(shape, jnp.float32) for shape in outs]
        + [pltpu.SemaphoreType.DMA((CHUNKS + 11,)), pltpu.SemaphoreType.DMA((21,))],
        compiler_params=pltpu.CompilerParams(vmem_limit_bytes=VMEM_LIMIT),
        cost_estimate=stage_cost(len(places)),
        name="backward_rim",
    )(recv, tile, below, right, diag, probe, tables, *fields_last, *fields_side)


def backward_inner(places, count, sums, tile, probe, tables, far, enter, row, col):
    comps, rows, cols = tile.shape
    return pl.pallas_call(
        functools.partial(backward_inner_kernel, places),
        out_shape=jax.ShapeDtypeStruct(tile.shape, jnp.float32),
        in_specs=[pl.BlockSpec(memory_space=pltpu.SMEM)] + in_hbm(8),
        out_specs=in_hbm(1)[0],
        scratch_shapes=[
            pltpu.VMEM(sums.shape, jnp.float32),
            pltpu.VMEM((2, rows, cols), jnp.float32),
            pltpu.VMEM(probe.shape, jnp.float32),
            pltpu.VMEM(tables.shape, tables.dtype),
            pltpu.VMEM(far.shape, jnp.float32),
            pltpu.VMEM(enter.shape, jnp.float32),
            pltpu.VMEM(row.shape, jnp.float32),
            pltpu.VMEM(col.shape, jnp.float32),
            pltpu.VMEM(tile.shape, jnp.float32),
            pltpu.VMEM((comps, rows, cols - SIDE), jnp.float32),
            pltpu.VMEM((comps, rows, cols - SIDE), jnp.float32),
            pltpu.SemaphoreType.DMA((2 * (rows // BLOCK - 1) + 6,)),
            pltpu.SemaphoreType.DMA((comps,)),
        ],
        compiler_params=pltpu.CompilerParams(vmem_limit_bytes=VMEM_LIMIT),
        cost_estimate=stage_cost(len(places)),
        name="backward_inner",
    )(count, sums, tile, probe, tables, far, enter, row, col)


def border_kernel(
    own_ref, above_ref, left_ref, diag_ref, out_ref, top_ref, side_ref, row_buf, col_buf, diag_buf, sems
):
    rows = out_ref.shape[1]
    half = rows // 2
    top = out_ref.at[:, pl.ds(0, BLOCK)]
    side = out_ref.at[:, pl.ds(BLOCK, rows - BLOCK), pl.ds(0, SIDE)]
    loads = start_copies(
        [
            (above_ref, row_buf),
            (top, top_ref),
            (left_ref, col_buf),
            (diag_ref, diag_buf),
            (side, side_ref),
        ],
        sems,
    )
    def unpacked(packed):
        low = low_lanes(packed.shape)
        upper = jnp.where(low, packed, 0.0)
        return upper, pltpu.roll(jnp.where(low, 0.0, packed), BLOCK, 2)

    wait_copies(loads[:2])
    top_ref[...] = top_ref[...] + row_buf[...]
    wait_copies(loads[2:4])
    upper, lower = unpacked(col_buf[...])
    corner = jnp.concatenate(unpacked(diag_buf[...]), axis=1)
    top_ref[:, :, :SIDE] = top_ref[:, :, :SIDE] + upper[:, :BLOCK] + corner
    stores = start_copies([(top_ref, top)], sems.at[pl.ds(5, 1)])
    wait_copies(loads[4:])
    side_ref[:, : half - BLOCK] = side_ref[:, : half - BLOCK] + upper[:, BLOCK:]
    side_ref[:, half - BLOCK :] = side_ref[:, half - BLOCK :] + lower
    stores += start_copies([(side_ref, side)], sems.at[pl.ds(6, 1)])
    wait_copies(stores)


def add_borders(own, above, left, diag):
    comps, rows, cols = own.shape
    return pl.pallas_call(
        border_kernel,
        out_shape=jax.ShapeDtypeStruct(own.shape, jnp.float32),
        in_specs=anywhere(4),
        out_specs=pl.BlockSpec(memory_space=pl.ANY),
        scratch_shapes=[
            pltpu.VMEM((comps, BLOCK, cols), jnp.float32),
            pltpu.VMEM((comps, rows - BLOCK, SIDE), jnp.float32),
            pltpu.VMEM(above.shape, jnp.float32),
            pltpu.VMEM(left.shape, jnp.float32),
            pltpu.VMEM(diag.shape, jnp.float32),
            pltpu.SemaphoreType.DMA((7,)),
        ],
        input_output_aliases={0: 0},
        compiler_params=pltpu.CompilerParams(vmem_limit_bytes=VMEM_LIMIT),
        name="add_borders",
    )(own, above, left, diag)


def row_strip_kernel(tile_ref, row_ref, sems):
    wait_copies(start_copies([(tile_ref.at[:, pl.ds(0, BLOCK)], row_ref)], sems))


def row_strip(tile):
    comps, rows, cols = tile.shape
    return pl.pallas_call(
        row_strip_kernel,
        out_shape=jax.ShapeDtypeStruct((comps, BLOCK, cols), jnp.float32),
        in_specs=in_hbm(1),
        out_specs=in_vmem(1)[0],
        scratch_shapes=[pltpu.SemaphoreType.DMA((1,))],
        compiler_params=pltpu.CompilerParams(vmem_limit_bytes=VMEM_LIMIT),
        name="row_strip",
    )(tile)


def column_strip_kernel(tile_ref, send_ref, out_ref, sems):
    wait_copies(start_copies([(tile_ref.at[:, :, pl.ds(0, SIDE)], out_ref)], sems))


def column_strip(tile, send):
    comps, rows, cols = tile.shape
    return pl.pallas_call(
        column_strip_kernel,
        out_shape=jax.ShapeDtypeStruct((comps, rows, SIDE), jnp.float32),
        in_specs=in_hbm(2),
        out_specs=pl.BlockSpec(memory_space=pltpu.VMEM),
        scratch_shapes=[pltpu.SemaphoreType.DMA((1,))],
        compiler_params=pltpu.CompilerParams(vmem_limit_bytes=VMEM_LIMIT),
        name="column_strip",
    )(tile, send)


def moved(shard, down, across):
    row_total = lax.axis_size("row")
    col_total = lax.axis_size("col")
    if across == 0:
        pairs = [(r, r + down) for r in range(row_total) if 0 <= r + down < row_total]
        return lax.ppermute(shard, "row", pairs)
    if down == 0:
        pairs = [(c, c + across) for c in range(col_total) if 0 <= c + across < col_total]
        return lax.ppermute(shard, "col", pairs)
    pairs = [
        (r * col_total + c, (r + down) * col_total + c + across)
        for r in range(row_total)
        for c in range(col_total)
        if 0 <= r + down < row_total and 0 <= c + across < col_total
    ]
    return lax.ppermute(shard, ("row", "col"), pairs)


def body(object_slices, probe, measured, offsets):
    slices, parts, tile_rows, tile_cols = object_slices.shape
    tile = object_slices.reshape(slices * parts, tile_rows, tile_cols)
    row_total = lax.axis_size("row")
    tables = jnp.asarray(TABLES)
    below = moved(row_strip(tile), -1, 0)
    send = pack(offsets, measured, row_total)
    recv = lax.all_to_all(send, "row", split_axis=0, concat_axis=0, tiled=True)
    right = moved(column_strip(tile, send), 0, -1)
    last, side, inner = pair_places(tile_rows, tile_cols)
    far_inner, enter_inner = forward_inner(inner, tile, probe, tables)
    right, far_inner = lax.optimization_barrier((right, far_inner))
    far_side, enter_side = forward_side(side, tile, right, probe, tables)
    below, far_side = lax.optimization_barrier((below, far_side))
    diag = moved(below[:, :, :SIDE], 0, -1)
    far_last, enter_last = forward_last(last, tile, below, right, diag, probe, tables)
    row, col, to_below, to_right, to_diag, sums, count = backward_rim(
        last + side,
        recv,
        tile,
        below,
        right,
        diag,
        probe,
        tables,
        (far_last, enter_last),
        (far_side, enter_side),
    )
    above = moved(to_below, 1, 0)
    left = moved(to_right, 0, 1)
    corner_part = moved(to_diag, 1, 1)
    own = backward_inner(
        inner, count, sums, tile, probe, tables, far_inner, enter_inner, row, col
    )
    result = add_borders(own, above, left, corner_part)
    return result.reshape(object_slices.shape)


def solution(mesh):
    placed = (
        P(None, None, "row", "col"),
        P(),
        P(("row", "col"), None, None),
        P(None, ("row", "col")),
    )
    return jax.shard_map(
        body, mesh=mesh, in_specs=placed, out_specs=P(None, None, "row", "col"), check_vma=False
    )
```

```python
import functools
import math

import jax
import jax.numpy as jnp
import ml_dtypes
import numpy as np
from jax import lax
from jax.experimental import pallas as pl
from jax.experimental.pallas import tpu as pltpu
from jax.sharding import PartitionSpec as P

PHASE = 40.0
SIDE = 128
BLOCK = 64
CAP = 2
META = 8
CHUNKS = 4
VMEM_LIMIT = 64 * 1024 * 1024


def dft_matrix():
    index = np.arange(SIDE)
    angle = (index[:, None] * index[None, :] % SIDE) * (-2.0 * math.pi / SIDE)
    return np.exp(1j * angle) / math.sqrt(SIDE)


def propagation_matrix():
    index = np.arange(SIDE)
    freq = np.where(index < SIDE // 2, index, index - SIDE) / SIDE
    dft = dft_matrix()
    return np.conj(dft) @ (np.exp(-1j * PHASE * freq * freq)[:, None] * dft)


def real_forms(matrix):
    right = np.block([[matrix.real, matrix.imag], [-matrix.imag, matrix.real]])
    out = []
    for form in (right, right.T):
        form = form.astype(np.float32)
        high = form.astype(ml_dtypes.bfloat16)
        out.append(high)
        out.append((form - high.astype(np.float32)).astype(ml_dtypes.bfloat16))
    return np.stack(out)


TABLES = np.concatenate([real_forms(propagation_matrix()), real_forms(dft_matrix())])


def split(field):
    high = field.astype(jnp.bfloat16)
    low = (field - high.astype(jnp.float32)).astype(jnp.bfloat16)
    return high, low


def from_right(rows, tables, at):
    high, low = split(rows)
    left = jnp.concatenate([high, low, high], axis=1)
    right = jnp.concatenate([tables[at], tables[at], tables[at + 1]], axis=0)
    return jnp.dot(left, right, preferred_element_type=jnp.float32)


def from_left(columns, tables, at):
    high, low = split(columns)
    left = jnp.concatenate([tables[at], tables[at], tables[at + 1]], axis=1)
    right = jnp.concatenate([high, low, high], axis=0)
    return jnp.dot(left, right, preferred_element_type=jnp.float32)


def swap(pair):
    top = jnp.concatenate([pair[:SIDE, :SIDE], pair[SIDE:, :SIDE]], axis=1)
    bottom = jnp.concatenate([pair[:SIDE, SIDE:], pair[SIDE:, SIDE:]], axis=1)
    return jnp.concatenate([top, bottom], axis=0)


def two_sided(pairs, tables, right_at, left_at):
    pairs = [from_right(rows, tables, right_at) for rows in pairs]
    return [from_left(swap(rows), tables, left_at) for rows in pairs]


def stacked(fields):
    return jnp.concatenate([jnp.concatenate(field, axis=1) for field in fields], axis=0)


def halves(pair, n):
    return pair[:SIDE, n * SIDE : (n + 1) * SIDE], pair[SIDE:, n * SIDE : (n + 1) * SIDE]


def low_lanes(shape):
    return lax.broadcasted_iota(jnp.int32, shape, len(shape) - 1) < BLOCK


def cut_pair(ext_ref, comp, row, col):
    first = ext_ref[comp, row : row + SIDE, col : col + SIDE]
    second = ext_ref[comp, row : row + SIDE, col + SIDE : col + 2 * SIDE]
    mixed = jnp.where(low_lanes(first.shape), second, first)
    return first, pltpu.roll(mixed, BLOCK, 1)


def times(left_re, left_im, right_re, right_im):
    return (left_re * right_re - left_im * right_im, left_re * right_im + left_im * right_re)


def conj_times(left_re, left_im, right_re, right_im):
    return (left_re * right_re + left_im * right_im, left_re * right_im - left_im * right_re)


def pack_kernel(off_ref, meas_ref, send_ref, meta_ref, count_ref, corner_ref, sems):
    owners = send_ref.shape[0]
    positions = meas_ref.shape[0]
    for owner in range(owners):
        count_ref[owner] = 0
        for rank in range(CAP):
            corner_ref[owner * CAP + rank] = -1
    copies = []
    for pos in range(positions):
        y = off_ref[0, pos]
        x = off_ref[1, pos]
        owner = lax.shift_right_logical(y, 8)
        rank = jnp.minimum(count_ref[owner], CAP - 1)
        count_ref[owner] = rank + 1
        corner = (lax.shift_right_logical(y, 6) & 3) * 8 + (lax.shift_right_logical(x, 6) & 7)
        corner_ref[owner * CAP + rank] = corner
        copy = pltpu.make_async_copy(
            meas_ref.at[pos],
            send_ref.at[owner, pl.ds(pl.multiple_of(rank * SIDE, SIDE), SIDE)],
            sems.at[pos],
        )
        copy.start()
        copies.append(copy)
    first = low_lanes((META, SIDE))
    for owner in range(owners):
        both = jnp.where(first, corner_ref[owner * CAP], corner_ref[owner * CAP + 1])
        meta_ref[owner] = both.astype(jnp.float32)
    copy = pltpu.make_async_copy(
        meta_ref, send_ref.at[:, pl.ds(CAP * SIDE, META)], sems.at[positions]
    )
    copy.start()
    copies.append(copy)
    for copy in copies:
        copy.wait()


def pack(offsets, measured, owners):
    positions = measured.shape[0]
    return pl.pallas_call(
        pack_kernel,
        out_shape=jax.ShapeDtypeStruct((owners, CAP * SIDE + META, SIDE), jnp.float32),
        in_specs=[
            pl.BlockSpec(memory_space=pltpu.SMEM),
            pl.BlockSpec(memory_space=pltpu.VMEM),
        ],
        out_specs=pl.BlockSpec(memory_space=pl.ANY),
        scratch_shapes=[
            pltpu.VMEM((owners, META, SIDE), jnp.float32),
            pltpu.SMEM((owners,), jnp.int32),
            pltpu.SMEM((owners * CAP,), jnp.int32),
            pltpu.SemaphoreType.DMA((positions + 1,)),
        ],
        compiler_params=pltpu.CompilerParams(vmem_limit_bytes=VMEM_LIMIT),
        cost_estimate=pl.CostEstimate(
            flops=0, bytes_accessed=40 * 1024 * 1024, transcendentals=0
        ),
        name="pack_measured",
    )(offsets, measured)


def pair_places(rows, cols):
    row_blocks = rows // BLOCK
    edge = cols - SIDE
    last = tuple((row_blocks - 1, col) for col in range(0, cols, SIDE))
    side = tuple((row, edge) for row in range(row_blocks - 1))
    inner = tuple((row, col) for row in range(row_blocks - 1) for col in range(0, edge, SIDE))
    return last, side, inner


def forward_pairs(places, ext_ref, probe_ref, tables, far_refs, enter_refs, entered, ready):
    probe_re = probe_ref[0]
    probe_im = probe_ref[1]
    rows = []
    for row, col in places:
        trans = [cut_pair(ext_ref, comp, row * BLOCK, col) for comp in range(2)]
        rows.append(
            stacked([times(probe_re, probe_im, trans[0][n], trans[1][n]) for n in range(2)])
        )
    enters = two_sided(rows, tables, 0, 2)
    rows = []
    for pair, (row, col) in enumerate(places):
        enter = enters[pair]
        enter_refs[pair][...] = enter
        trans = [cut_pair(ext_ref, comp, row * BLOCK, col) for comp in range(2, 4)]
        rows.append(
            stacked([times(*halves(enter, n), trans[0][n], trans[1][n]) for n in range(2)])
        )
    entered()
    fars = two_sided(rows, tables, 4, 6)
    for pair, far in enumerate(fars):
        far_refs[pair][...] = far
        ready(pair)


def each(ref):
    return [ref.at[pair] for pair in range(ref.shape[0])]


def start_copies(parts, sems):
    copies = [
        pltpu.make_async_copy(source, target, sems.at[n])
        for n, (source, target) in enumerate(parts)
    ]
    for copy in copies:
        copy.start()
    return copies


def wait_copies(copies):
    for copy in copies:
        copy.wait()


def forward_kernel(places, layout, count, *refs):
    sources = refs[:count]
    probe_ref, tables_ref, far_ref, enter_ref = refs[count : count + 4]
    ext_ref, probe_buf, table_buf, far_buf, enter_buf, sems, out_sems = refs[count + 4 :]
    wait_copies(
        start_copies(
            [(tables_ref, table_buf), (probe_ref, probe_buf)] + layout(ext_ref, *sources), sems
        )
    )
    stores = []

    def entered():
        stores.extend(start_copies([(enter_buf, enter_ref)], out_sems.at[pl.ds(0, 1)]))

    def ready(pair):
        stores.extend(
            start_copies([(far_buf.at[pair], far_ref.at[pair])], out_sems.at[pl.ds(1 + pair, 1)])
        )

    forward_pairs(
        places, ext_ref, probe_buf, table_buf, each(far_buf), each(enter_buf), entered, ready
    )
    wait_copies(stores)


def stage_cost(pairs):
    return pl.CostEstimate(
        flops=pairs * 4 * 3 * 2 * 256**3, bytes_accessed=1024 * 1024, transcendentals=0
    )


def fields(places):
    field = jax.ShapeDtypeStruct((len(places), 2 * SIDE, 2 * SIDE), jnp.float32)
    return field, field


def in_vmem(count):
    return [pl.BlockSpec(memory_space=pltpu.VMEM)] * count


def anywhere(count):
    return [pl.BlockSpec(memory_space=pl.ANY)] * count


def in_hbm(count):
    return [pl.BlockSpec(memory_space=pltpu.HBM)] * count


def forward(name, places, layout, ext, sources, probe, tables):
    field = (len(places), 2 * SIDE, 2 * SIDE)
    return pl.pallas_call(
        functools.partial(forward_kernel, places, layout, len(sources)),
        out_shape=fields(places),
        in_specs=in_hbm(len(sources) + 2),
        out_specs=tuple(in_hbm(2)),
        scratch_shapes=[
            pltpu.VMEM(ext, jnp.float32),
            pltpu.VMEM(probe.shape, jnp.float32),
            pltpu.VMEM(tables.shape, tables.dtype),
            pltpu.VMEM(field, jnp.float32),
            pltpu.VMEM(field, jnp.float32),
            pltpu.SemaphoreType.DMA((len(sources) + 2,)),
            pltpu.SemaphoreType.DMA((1 + len(places),)),
        ],
        compiler_params=pltpu.CompilerParams(vmem_limit_bytes=VMEM_LIMIT),
        cost_estimate=stage_cost(8 * len(places)),
        name=name,
    )(*sources, probe, tables)


def forward_inner(places, tile, probe, tables):
    def layout(ext_ref, tile_ref):
        return [(tile_ref, ext_ref)]

    return forward("forward_inner", places, layout, tile.shape, (tile,), probe, tables)


def extended_shape(tile, comps):
    return pltpu.VMEM((comps, tile.shape[1] + BLOCK, tile.shape[2] + SIDE), jnp.float32)


def forward_side(places, tile, right, probe, tables):
    comps, rows, cols = tile.shape

    def layout(ext_ref, tile_ref, right_ref):
        return [
            (tile_ref.at[:, :, pl.ds(cols - SIDE, SIDE)], ext_ref.at[:, :, pl.ds(0, SIDE)]),
            (right_ref, ext_ref.at[:, :, pl.ds(SIDE, SIDE)]),
        ]

    here = [(row, 0) for row, _ in places]
    ext = (comps, rows, 2 * SIDE)
    return forward("forward_last_column", here, layout, ext, (tile, right), probe, tables)


def forward_last(places, tile, below, right, diag, probe, tables):
    comps, rows, cols = tile.shape

    def layout(ext_ref, tile_ref, below_ref, right_ref, diag_ref):
        low = pl.ds(rows - BLOCK, BLOCK)
        upper, lower = pl.ds(0, BLOCK), pl.ds(BLOCK, BLOCK)
        wide, beyond = pl.ds(0, cols), pl.ds(cols, SIDE)
        return [
            (tile_ref.at[:, low], ext_ref.at[:, upper, wide]),
            (below_ref, ext_ref.at[:, lower, wide]),
            (right_ref.at[:, low], ext_ref.at[:, upper, beyond]),
            (diag_ref, ext_ref.at[:, lower, beyond]),
        ]

    here = [(0, col) for _, col in places]
    ext = (comps, SIDE, cols + SIDE)
    sources = (tile, below, right, diag)
    return forward("forward_last_row", here, layout, ext, sources, probe, tables)


def gather_sums(meta_ref, items_ref, sum_ref, count_ref, arrivals):
    spare = sum_ref.shape[0] - 1
    sources = items_ref.shape[0]
    for corner in range(spare + 1):
        count_ref[corner] = 0
    for source in range(sources):
        if source % (sources // len(arrivals)) == 0:
            arrivals[source * len(arrivals) // sources].wait()
        for rank in range(CAP):
            corner = meta_ref[source, rank * BLOCK].astype(jnp.int32)
            at = jnp.where(corner < 0, spare, corner)
            hits = count_ref[at]
            count_ref[at] = hits + 1
            item = items_ref[source, rank * SIDE : (rank + 1) * SIDE]
            sum_ref[at] = jnp.where(hits > 0, sum_ref[at], 0.0) + item


def summed(sum_ref, count_ref, at):
    hits = count_ref[at]
    return hits.astype(jnp.float32), jnp.where(hits > 0, sum_ref[at], 0.0)


def backward_pairs(
    places,
    width,
    probe_ref,
    tables,
    far_ref,
    enter_ref,
    ext_ref,
    sum_ref,
    count_ref,
    store,
    before_pair,
    before_products,
    before_fields,
    after_fields,
):
    rows = []
    for pair, (row, col) in enumerate(places):
        before_pair(pair)
        waves = []
        for n in range(2):
            at = row * width + col // BLOCK + n
            hits, total = summed(sum_ref, count_ref, at)
            far_re, far_im = halves(far_ref[pair], n)
            misfit = 2.0 * (hits * (far_re * far_re + far_im * far_im) - total)
            waves.append((misfit * far_re, misfit * far_im))
        rows.append(stacked(waves))
    before_products()
    backs = two_sided(rows, tables, 6, 4)
    before_fields()
    rows = []
    for pair, (row, col) in enumerate(places):
        trans = [cut_pair(ext_ref, comp, row * BLOCK, col) for comp in range(2)]
        waves = []
        for n in range(2):
            back = halves(backs[pair], n)
            grad = conj_times(*halves(enter_ref[pair], n), *back)
            store(n, 2, row, col, grad[0])
            store(n, 3, row, col, grad[1])
            waves.append(conj_times(trans[0][n], trans[1][n], *back))
        rows.append(stacked(waves))
    after_fields()
    backs = two_sided(rows, tables, 2, 0)
    probe_re = probe_ref[0]
    probe_im = probe_ref[1]
    for pair, (row, col) in enumerate(places):
        for n in range(2):
            grad = conj_times(probe_re, probe_im, *halves(backs[pair], n))
            store(n, 0, row, col, grad[0])
            store(n, 1, row, col, grad[1])


def shifted(low, high):
    if low is None:
        low = jnp.zeros_like(high)
    if high is None:
        high = jnp.zeros_like(low)
    return pltpu.roll(jnp.where(low_lanes(low.shape), high, low), BLOCK, 1)


def backward_rim_kernel(
    places,
    recv_ref,
    tile_ref,
    below_ref,
    right_ref,
    diag_ref,
    probe_ref,
    tables_ref,
    far_last_ref,
    enter_last_ref,
    far_side_ref,
    enter_side_ref,
    row_ref,
    col_ref,
    out_below_ref,
    out_right_ref,
    out_diag_ref,
    out_sum_ref,
    count_ref,
    items_ref,
    meta_ref,
    table_buf,
    probe_buf,
    far_buf,
    enter_buf,
    ext_ref,
    sum_ref,
    even_ref,
    odd_ref,
    even_side_ref,
    odd_side_ref,
    row_buf,
    col_buf,
    below_buf,
    right_buf,
    diag_buf,
    sems,
    out_sems,
):
    rows, cols = tile_ref.shape[1:]
    last = rows // BLOCK - 1
    corners = sum_ref.shape[0] - 1
    near = far_last_ref.shape[0]
    first = pl.ds(0, near)
    others = pl.ds(near, far_side_ref.shape[0])
    two = pl.ds(2, 2)
    chunk = recv_ref.shape[0] // CHUNKS
    wide = pl.ds(0, cols)
    beyond = pl.ds(cols, SIDE)
    copies = start_copies(
        [(recv_ref.at[:, CAP * SIDE], meta_ref)]
        + [
            (recv_ref.at[part, pl.ds(0, CAP * SIDE)], items_ref.at[part])
            for part in (pl.ds(n * chunk, chunk) for n in range(CHUNKS))
        ]
        + [
            (far_last_ref, far_buf.at[first]),
            (tables_ref, table_buf),
            (far_side_ref, far_buf.at[others]),
            (enter_last_ref, enter_buf.at[first]),
            (enter_side_ref, enter_buf.at[others]),
            (tile_ref.at[two], ext_ref.at[:, pl.ds(0, rows), wide]),
            (below_ref.at[two], ext_ref.at[:, pl.ds(rows, BLOCK), wide]),
            (right_ref.at[two], ext_ref.at[:, pl.ds(0, rows), beyond]),
            (diag_ref.at[two], ext_ref.at[:, pl.ds(rows, BLOCK), beyond]),
            (probe_ref, probe_buf),
        ],
        sems,
    )
    wait_copies(copies[:1])
    rest = copies[1 + CHUNKS :]
    gather_sums(meta_ref, items_ref, sum_ref, count_ref, copies[1 : 1 + CHUNKS])
    bands = (even_ref, odd_ref)
    sides = (even_side_ref, odd_side_ref)
    stores = start_copies(
        [(sum_ref.at[pl.ds(0, corners)], out_sum_ref)], out_sems.at[pl.ds(20, 1)]
    )

    def store(n, comp, row, col, value):
        if row == last:
            bands[n][comp, :, col : col + SIDE] = value
        else:
            at = row * BLOCK
            top = value[:BLOCK]
            if row > 0:
                top = top + sides[n][comp, at : at + BLOCK]
            sides[n][comp, at : at + BLOCK] = top
            sides[n][comp, at + BLOCK : at + SIDE] = value[BLOCK:]

    half = rows // 2

    def finish(comp):
        beyond_cols = []
        for buf, part in ((row_buf, slice(0, BLOCK)), (below_buf, slice(BLOCK, SIDE))):
            before = None
            for col in range(0, cols, SIDE):
                here = odd_ref[comp, part, col : col + SIDE]
                buf[comp, :, col : col + SIDE] = even_ref[
                    comp, part, col : col + SIDE
                ] + shifted(before, here)
                before = here
            beyond_cols.append(shifted(before, None))
        corner = beyond_cols[1]
        diag_buf[comp] = corner[: BLOCK // 2] + pltpu.roll(corner[BLOCK // 2 :], BLOCK, 1)
        odd_side = odd_side_ref[comp]
        col_buf[comp] = even_side_ref[comp] + shifted(None, odd_side)
        side = shifted(odd_side, None)
        second = jnp.concatenate(
            [side[half : rows - BLOCK], side[rows - BLOCK :] + beyond_cols[0]], axis=0
        )
        right_buf[comp] = side[:half] + pltpu.roll(second, BLOCK, 1)
        stores.extend(
            start_copies(
                [
                    (below_buf.at[comp], out_below_ref.at[comp]),
                    (diag_buf.at[comp], out_diag_ref.at[comp]),
                    (right_buf.at[comp], out_right_ref.at[comp]),
                    (row_buf.at[comp], row_ref.at[comp]),
                    (col_buf.at[comp], col_ref.at[comp]),
                ],
                out_sems.at[pl.ds(5 * comp, 5)],
            )
        )

    def before_pair(pair):
        if pair == 0:
            rest[0].wait()
        if pair == near:
            rest[2].wait()

    def after_fields():
        finish(2)
        finish(3)

    backward_pairs(
        places,
        cols // BLOCK,
        probe_buf,
        table_buf,
        far_buf,
        enter_buf,
        ext_ref,
        sum_ref,
        count_ref,
        store,
        before_pair,
        lambda: wait_copies(rest[1:2]),
        lambda: wait_copies(rest[3:]),
        after_fields,
    )
    finish(0)
    finish(1)
    wait_copies(stores)


def backward_inner_kernel(
    places,
    count_ref,
    sum_ref,
    tile_ref,
    probe_ref,
    tables_ref,
    far_ref,
    enter_ref,
    row_ref,
    col_ref,
    out_ref,
    sum_buf,
    trans_buf,
    probe_buf,
    table_buf,
    far_buf,
    enter_buf,
    row_buf,
    col_buf,
    out_buf,
    even_ref,
    odd_ref,
    sems,
    out_sems,
):
    comps, rows, cols = out_buf.shape
    last = rows - BLOCK
    width = cols // BLOCK
    acc = (even_ref, odd_ref)
    row_blocks = last // BLOCK
    group = len(places) // row_blocks
    parts = []
    for n in range(row_blocks):
        here = pl.ds(n * width, width)
        parts.append((sum_ref.at[here], sum_buf.at[here]))
        here = pl.ds(n * group, group)
        parts.append((far_ref.at[here], far_buf.at[here]))
        if n == 0:
            parts.append((tables_ref, table_buf))
    copies = start_copies(
        parts
        + [
            (enter_ref, enter_buf),
            (tile_ref.at[pl.ds(2, 2)], trans_buf),
            (probe_ref, probe_buf),
            (row_ref, row_buf),
            (col_ref, col_buf),
        ],
        sems,
    )
    table_copy = copies.pop(2)
    rest = copies[2 * row_blocks :]
    stores = []

    def store(n, comp, row, col, value):
        at = row * BLOCK
        lanes = slice(col, col + SIDE)
        top = value[:BLOCK]
        if row > 0:
            top = top + acc[n][comp, at : at + BLOCK, lanes]
        acc[n][comp, at : at + BLOCK, lanes] = top
        acc[n][comp, at + BLOCK : at + SIDE, lanes] = value[BLOCK:]

    def finish(comp):
        before = None
        for col in range(0, cols, SIDE):
            lanes = slice(col, col + SIDE)
            if col < cols - SIDE:
                here = odd_ref[comp, :, lanes]
                value = even_ref[comp, :, lanes] + shifted(before, here)
                before = here
            else:
                value = col_buf[comp] + shifted(before, None)
            out_buf[comp, :last, lanes] = value[:last]
            out_buf[comp, last:, lanes] = value[last:] + row_buf[comp, :, lanes]
        stores.extend(
            start_copies(
                [(out_buf.at[comp], out_ref.at[comp])], out_sems.at[pl.ds(comp, 1)]
            )
        )

    def before_pair(pair):
        if pair % group == 0:
            at = 2 * (pair // group)
            wait_copies(copies[at : at + 2])

    def after_fields():
        finish(2)
        finish(3)

    backward_pairs(
        places,
        width,
        probe_buf,
        table_buf,
        far_buf,
        enter_buf,
        trans_buf,
        sum_buf,
        count_ref,
        store,
        before_pair,
        table_copy.wait,
        lambda: wait_copies(rest),
        after_fields,
    )
    finish(0)
    finish(1)
    wait_copies(stores)


def shapes_of(*shapes):
    return tuple(jax.ShapeDtypeStruct(shape, jnp.float32) for shape in shapes)


def backward_rim(places, recv, tile, below, right, diag, probe, tables, fields_last, fields_side):
    comps, rows, cols = tile.shape
    corners = (rows // BLOCK) * (cols // BLOCK)
    sources = recv.shape[0]
    field = (len(places), 2 * SIDE, 2 * SIDE)
    outs = (
        (comps, BLOCK, cols),
        (comps, rows, SIDE),
        (comps, BLOCK, cols),
        (comps, rows // 2, SIDE),
        (comps, BLOCK // 2, SIDE),
    )
    return pl.pallas_call(
        functools.partial(backward_rim_kernel, places),
        out_shape=shapes_of(*outs, (corners, SIDE, SIDE))
        + (jax.ShapeDtypeStruct((corners + 1,), jnp.int32),),
        in_specs=in_hbm(11),
        out_specs=tuple(in_hbm(6)) + (pl.BlockSpec(memory_space=pltpu.SMEM),),
        scratch_shapes=[
            pltpu.VMEM((sources, CAP * SIDE, SIDE), jnp.float32),
            pltpu.SMEM((sources, SIDE), jnp.float32),
            pltpu.VMEM(tables.shape, tables.dtype),
            pltpu.VMEM(probe.shape, jnp.float32),
            pltpu.VMEM(field, jnp.float32),
            pltpu.VMEM(field, jnp.float32),
            extended_shape(tile, 2),
            pltpu.VMEM((corners + 1, SIDE, SIDE), jnp.float32),
            pltpu.VMEM((comps, SIDE, cols), jnp.float32),
            pltpu.VMEM((comps, SIDE, cols), jnp.float32),
            pltpu.VMEM((comps, rows, SIDE), jnp.float32),
            pltpu.VMEM((comps, rows, SIDE), jnp.float32),
        ]
        + [pltpu.VMEM(shape, jnp.float32) for shape in outs]
        + [pltpu.SemaphoreType.DMA((CHUNKS + 11,)), pltpu.SemaphoreType.DMA((21,))],
        compiler_params=pltpu.CompilerParams(vmem_limit_bytes=VMEM_LIMIT),
        cost_estimate=stage_cost(len(places)),
        name="backward_rim",
    )(recv, tile, below, right, diag, probe, tables, *fields_last, *fields_side)


def backward_inner(places, count, sums, tile, probe, tables, far, enter, row, col):
    comps, rows, cols = tile.shape
    return pl.pallas_call(
        functools.partial(backward_inner_kernel, places),
        out_shape=jax.ShapeDtypeStruct(tile.shape, jnp.float32),
        in_specs=[pl.BlockSpec(memory_space=pltpu.SMEM)] + in_hbm(8),
        out_specs=in_hbm(1)[0],
        scratch_shapes=[
            pltpu.VMEM(sums.shape, jnp.float32),
            pltpu.VMEM((2, rows, cols), jnp.float32),
            pltpu.VMEM(probe.shape, jnp.float32),
            pltpu.VMEM(tables.shape, tables.dtype),
            pltpu.VMEM(far.shape, jnp.float32),
            pltpu.VMEM(enter.shape, jnp.float32),
            pltpu.VMEM(row.shape, jnp.float32),
            pltpu.VMEM(col.shape, jnp.float32),
            pltpu.VMEM(tile.shape, jnp.float32),
            pltpu.VMEM((comps, rows, cols - SIDE), jnp.float32),
            pltpu.VMEM((comps, rows, cols - SIDE), jnp.float32),
            pltpu.SemaphoreType.DMA((2 * (rows // BLOCK - 1) + 6,)),
            pltpu.SemaphoreType.DMA((comps,)),
        ],
        compiler_params=pltpu.CompilerParams(vmem_limit_bytes=VMEM_LIMIT),
        cost_estimate=stage_cost(len(places)),
        name="backward_inner",
    )(count, sums, tile, probe, tables, far, enter, row, col)


def border_kernel(
    own_ref, above_ref, left_ref, diag_ref, out_ref, top_ref, side_ref, row_buf, col_buf, diag_buf, sems
):
    rows = out_ref.shape[1]
    half = rows // 2
    top = out_ref.at[:, pl.ds(0, BLOCK)]
    side = out_ref.at[:, pl.ds(BLOCK, rows - BLOCK), pl.ds(0, SIDE)]
    loads = start_copies(
        [
            (above_ref, row_buf),
            (top, top_ref),
            (left_ref, col_buf),
            (diag_ref, diag_buf),
            (side, side_ref),
        ],
        sems,
    )
    def unpacked(packed):
        low = low_lanes(packed.shape)
        upper = jnp.where(low, packed, 0.0)
        return upper, pltpu.roll(jnp.where(low, 0.0, packed), BLOCK, 2)

    wait_copies(loads[:2])
    top_ref[...] = top_ref[...] + row_buf[...]
    wait_copies(loads[2:4])
    upper, lower = unpacked(col_buf[...])
    corner = jnp.concatenate(unpacked(diag_buf[...]), axis=1)
    top_ref[:, :, :SIDE] = top_ref[:, :, :SIDE] + upper[:, :BLOCK] + corner
    stores = start_copies([(top_ref, top)], sems.at[pl.ds(5, 1)])
    wait_copies(loads[4:])
    side_ref[:, : half - BLOCK] = side_ref[:, : half - BLOCK] + upper[:, BLOCK:]
    side_ref[:, half - BLOCK :] = side_ref[:, half - BLOCK :] + lower
    stores += start_copies([(side_ref, side)], sems.at[pl.ds(6, 1)])
    wait_copies(stores)


def add_borders(own, above, left, diag):
    comps, rows, cols = own.shape
    return pl.pallas_call(
        border_kernel,
        out_shape=jax.ShapeDtypeStruct(own.shape, jnp.float32),
        in_specs=anywhere(4),
        out_specs=pl.BlockSpec(memory_space=pl.ANY),
        scratch_shapes=[
            pltpu.VMEM((comps, BLOCK, cols), jnp.float32),
            pltpu.VMEM((comps, rows - BLOCK, SIDE), jnp.float32),
            pltpu.VMEM(above.shape, jnp.float32),
            pltpu.VMEM(left.shape, jnp.float32),
            pltpu.VMEM(diag.shape, jnp.float32),
            pltpu.SemaphoreType.DMA((7,)),
        ],
        input_output_aliases={0: 0},
        compiler_params=pltpu.CompilerParams(vmem_limit_bytes=VMEM_LIMIT),
        name="add_borders",
    )(own, above, left, diag)


def row_strip_kernel(tile_ref, row_ref, sems):
    wait_copies(start_copies([(tile_ref.at[:, pl.ds(0, BLOCK)], row_ref)], sems))


def row_strip(tile):
    comps, rows, cols = tile.shape
    return pl.pallas_call(
        row_strip_kernel,
        out_shape=jax.ShapeDtypeStruct((comps, BLOCK, cols), jnp.float32),
        in_specs=in_hbm(1),
        out_specs=in_vmem(1)[0],
        scratch_shapes=[pltpu.SemaphoreType.DMA((1,))],
        compiler_params=pltpu.CompilerParams(vmem_limit_bytes=VMEM_LIMIT),
        name="row_strip",
    )(tile)


def column_strip_kernel(tile_ref, send_ref, out_ref, sems):
    wait_copies(start_copies([(tile_ref.at[:, :, pl.ds(0, SIDE)], out_ref)], sems))


def column_strip(tile, send):
    comps, rows, cols = tile.shape
    return pl.pallas_call(
        column_strip_kernel,
        out_shape=jax.ShapeDtypeStruct((comps, rows, SIDE), jnp.float32),
        in_specs=in_hbm(2),
        out_specs=pl.BlockSpec(memory_space=pltpu.VMEM),
        scratch_shapes=[pltpu.SemaphoreType.DMA((1,))],
        compiler_params=pltpu.CompilerParams(vmem_limit_bytes=VMEM_LIMIT),
        name="column_strip",
    )(tile, send)


def moved(shard, down, across):
    row_total = lax.axis_size("row")
    col_total = lax.axis_size("col")
    if across == 0:
        pairs = [(r, r + down) for r in range(row_total) if 0 <= r + down < row_total]
        return lax.ppermute(shard, "row", pairs)
    if down == 0:
        pairs = [(c, c + across) for c in range(col_total) if 0 <= c + across < col_total]
        return lax.ppermute(shard, "col", pairs)
    pairs = [
        (r * col_total + c, (r + down) * col_total + c + across)
        for r in range(row_total)
        for c in range(col_total)
        if 0 <= r + down < row_total and 0 <= c + across < col_total
    ]
    return lax.ppermute(shard, ("row", "col"), pairs)


def body(object_slices, probe, measured, offsets):
    slices, parts, tile_rows, tile_cols = object_slices.shape
    tile = object_slices.reshape(slices * parts, tile_rows, tile_cols)
    row_total = lax.axis_size("row")
    tables = jnp.asarray(TABLES)
    below = moved(row_strip(tile), -1, 0)
    send = pack(offsets, measured, row_total)
    recv = lax.all_to_all(send, "row", split_axis=0, concat_axis=0, tiled=True)
    right = moved(column_strip(tile, send), 0, -1)
    last, side, inner = pair_places(tile_rows, tile_cols)
    far_inner, enter_inner = forward_inner(inner, tile, probe, tables)
    right, far_inner = lax.optimization_barrier((right, far_inner))
    far_side, enter_side = forward_side(side, tile, right, probe, tables)
    below, far_side = lax.optimization_barrier((below, far_side))
    diag = moved(below[:, :, :SIDE], 0, -1)
    far_last, enter_last = forward_last(last, tile, below, right, diag, probe, tables)
    row, col, to_below, to_right, to_diag, sums, count = backward_rim(
        last + side,
        recv,
        tile,
        below,
        right,
        diag,
        probe,
        tables,
        (far_last, enter_last),
        (far_side, enter_side),
    )
    above = moved(to_below, 1, 0)
    left = moved(to_right, 0, 1)
    corner_part = moved(to_diag, 1, 1)
    own = backward_inner(
        inner, count, sums, tile, probe, tables, far_inner, enter_inner, row, col
    )
    result = add_borders(own, above, left, corner_part)
    return result.reshape(object_slices.shape)


def solution(mesh):
    placed = (
        P(None, None, "row", "col"),
        P(),
        P(("row", "col"), None, None),
        P(None, ("row", "col")),
    )
    return jax.shard_map(
        body, mesh=mesh, in_specs=placed, out_specs=P(None, None, "row", "col"), check_vma=False
    )
```

```python
import functools
import math

import jax
import jax.numpy as jnp
import ml_dtypes
import numpy as np
from jax import lax
from jax.experimental import pallas as pl
from jax.experimental.pallas import tpu as pltpu
from jax.sharding import PartitionSpec as P

PHASE = 40.0
SIDE = 128
BLOCK = 64
CAP = 2
META = 8
CHUNKS = 4
VMEM_LIMIT = 64 * 1024 * 1024


def dft_matrix():
    index = np.arange(SIDE)
    angle = (index[:, None] * index[None, :] % SIDE) * (-2.0 * math.pi / SIDE)
    return np.exp(1j * angle) / math.sqrt(SIDE)


def propagation_matrix():
    index = np.arange(SIDE)
    freq = np.where(index < SIDE // 2, index, index - SIDE) / SIDE
    dft = dft_matrix()
    return np.conj(dft) @ (np.exp(-1j * PHASE * freq * freq)[:, None] * dft)


def real_forms(matrix):
    right = np.block([[matrix.real, matrix.imag], [-matrix.imag, matrix.real]])
    out = []
    for form in (right, right.T):
        form = form.astype(np.float32)
        high = form.astype(ml_dtypes.bfloat16)
        out.append(high)
        out.append((form - high.astype(np.float32)).astype(ml_dtypes.bfloat16))
    return np.stack(out)


TABLES = np.concatenate([real_forms(propagation_matrix()), real_forms(dft_matrix())])


def split(field):
    high = field.astype(jnp.bfloat16)
    low = (field - high.astype(jnp.float32)).astype(jnp.bfloat16)
    return high, low


def from_right(rows, tables, at):
    high, low = split(rows)
    left = jnp.concatenate([high, low, high], axis=1)
    right = jnp.concatenate([tables[at], tables[at], tables[at + 1]], axis=0)
    return jnp.dot(left, right, preferred_element_type=jnp.float32)


def from_left(columns, tables, at):
    high, low = split(columns)
    left = jnp.concatenate([tables[at], tables[at], tables[at + 1]], axis=1)
    right = jnp.concatenate([high, low, high], axis=0)
    return jnp.dot(left, right, preferred_element_type=jnp.float32)


def swap(pair):
    top = jnp.concatenate([pair[:SIDE, :SIDE], pair[SIDE:, :SIDE]], axis=1)
    bottom = jnp.concatenate([pair[:SIDE, SIDE:], pair[SIDE:, SIDE:]], axis=1)
    return jnp.concatenate([top, bottom], axis=0)


def two_sided(pairs, tables, right_at, left_at):
    pairs = [from_right(rows, tables, right_at) for rows in pairs]
    return [from_left(swap(rows), tables, left_at) for rows in pairs]


def stacked(fields):
    return jnp.concatenate([jnp.concatenate(field, axis=1) for field in fields], axis=0)


def halves(pair, n):
    return pair[:SIDE, n * SIDE : (n + 1) * SIDE], pair[SIDE:, n * SIDE : (n + 1) * SIDE]


def low_lanes(shape):
    return lax.broadcasted_iota(jnp.int32, shape, len(shape) - 1) < BLOCK


def cut_pair(ext_ref, comp, row, col):
    first = ext_ref[comp, row : row + SIDE, col : col + SIDE]
    second = ext_ref[comp, row : row + SIDE, col + SIDE : col + 2 * SIDE]
    mixed = jnp.where(low_lanes(first.shape), second, first)
    return first, pltpu.roll(mixed, BLOCK, 1)


def times(left_re, left_im, right_re, right_im):
    return (left_re * right_re - left_im * right_im, left_re * right_im + left_im * right_re)


def conj_times(left_re, left_im, right_re, right_im):
    return (left_re * right_re + left_im * right_im, left_re * right_im - left_im * right_re)


def pack_kernel(off_ref, meas_ref, send_ref, meta_ref, count_ref, corner_ref, sems):
    owners = send_ref.shape[0]
    positions = meas_ref.shape[0]
    for owner in range(owners):
        count_ref[owner] = 0
        for rank in range(CAP):
            corner_ref[owner * CAP + rank] = -1
    copies = []
    for pos in range(positions):
        y = off_ref[0, pos]
        x = off_ref[1, pos]
        owner = lax.shift_right_logical(y, 8)
        rank = jnp.minimum(count_ref[owner], CAP - 1)
        count_ref[owner] = rank + 1
        corner = (lax.shift_right_logical(y, 6) & 3) * 8 + (lax.shift_right_logical(x, 6) & 7)
        corner_ref[owner * CAP + rank] = corner
        copy = pltpu.make_async_copy(
            meas_ref.at[pos],
            send_ref.at[owner, pl.ds(pl.multiple_of(rank * SIDE, SIDE), SIDE)],
            sems.at[pos],
        )
        copy.start()
        copies.append(copy)
    first = low_lanes((META, SIDE))
    for owner in range(owners):
        both = jnp.where(first, corner_ref[owner * CAP], corner_ref[owner * CAP + 1])
        meta_ref[owner] = both.astype(jnp.float32)
    copy = pltpu.make_async_copy(
        meta_ref, send_ref.at[:, pl.ds(CAP * SIDE, META)], sems.at[positions]
    )
    copy.start()
    copies.append(copy)
    for copy in copies:
        copy.wait()


def pack(offsets, measured, owners):
    positions = measured.shape[0]
    return pl.pallas_call(
        pack_kernel,
        out_shape=jax.ShapeDtypeStruct((owners, CAP * SIDE + META, SIDE), jnp.float32),
        in_specs=[
            pl.BlockSpec(memory_space=pltpu.SMEM),
            pl.BlockSpec(memory_space=pltpu.VMEM),
        ],
        out_specs=pl.BlockSpec(memory_space=pl.ANY),
        scratch_shapes=[
            pltpu.VMEM((owners, META, SIDE), jnp.float32),
            pltpu.SMEM((owners,), jnp.int32),
            pltpu.SMEM((owners * CAP,), jnp.int32),
            pltpu.SemaphoreType.DMA((positions + 1,)),
        ],
        compiler_params=pltpu.CompilerParams(vmem_limit_bytes=VMEM_LIMIT),
        cost_estimate=pl.CostEstimate(
            flops=0, bytes_accessed=40 * 1024 * 1024, transcendentals=0
        ),
        name="pack_measured",
    )(offsets, measured)


def pair_places(rows, cols):
    row_blocks = rows // BLOCK
    edge = cols - SIDE
    last = tuple((row_blocks - 1, col) for col in range(0, cols, SIDE))
    side = tuple((row, edge) for row in range(row_blocks - 1))
    inner = tuple((row, col) for row in range(row_blocks - 1) for col in range(0, edge, SIDE))
    return last, side, inner


def forward_pairs(places, ext_ref, probe_ref, tables, far_refs, enter_refs, entered, ready):
    probe_re = probe_ref[0]
    probe_im = probe_ref[1]
    rows = []
    for row, col in places:
        trans = [cut_pair(ext_ref, comp, row * BLOCK, col) for comp in range(2)]
        rows.append(
            stacked([times(probe_re, probe_im, trans[0][n], trans[1][n]) for n in range(2)])
        )
    enters = two_sided(rows, tables, 0, 2)
    rows = []
    for pair, (row, col) in enumerate(places):
        enter = enters[pair]
        enter_refs[pair][...] = enter
        trans = [cut_pair(ext_ref, comp, row * BLOCK, col) for comp in range(2, 4)]
        rows.append(
            stacked([times(*halves(enter, n), trans[0][n], trans[1][n]) for n in range(2)])
        )
    entered()
    fars = two_sided(rows, tables, 4, 6)
    for pair, far in enumerate(fars):
        far_refs[pair][...] = far
        ready(pair)


def each(ref):
    return [ref.at[pair] for pair in range(ref.shape[0])]


def start_copies(parts, sems):
    copies = [
        pltpu.make_async_copy(source, target, sems.at[n])
        for n, (source, target) in enumerate(parts)
    ]
    for copy in copies:
        copy.start()
    return copies


def wait_copies(copies):
    for copy in copies:
        copy.wait()


def forward_kernel(places, layout, count, *refs):
    sources = refs[:count]
    probe_ref, tables_ref, far_ref, enter_ref = refs[count : count + 4]
    ext_ref, probe_buf, table_buf, far_buf, enter_buf, sems, out_sems = refs[count + 4 :]
    wait_copies(
        start_copies(
            [(tables_ref, table_buf), (probe_ref, probe_buf)] + layout(ext_ref, *sources), sems
        )
    )
    stores = []

    def entered():
        stores.extend(start_copies([(enter_buf, enter_ref)], out_sems.at[pl.ds(0, 1)]))

    def ready(pair):
        stores.extend(
            start_copies([(far_buf.at[pair], far_ref.at[pair])], out_sems.at[pl.ds(1 + pair, 1)])
        )

    forward_pairs(
        places, ext_ref, probe_buf, table_buf, each(far_buf), each(enter_buf), entered, ready
    )
    wait_copies(stores)


def stage_cost(pairs):
    return pl.CostEstimate(
        flops=pairs * 4 * 3 * 2 * 256**3, bytes_accessed=1024 * 1024, transcendentals=0
    )


def fields(places):
    field = jax.ShapeDtypeStruct((len(places), 2 * SIDE, 2 * SIDE), jnp.float32)
    return field, field


def in_vmem(count):
    return [pl.BlockSpec(memory_space=pltpu.VMEM)] * count


def anywhere(count):
    return [pl.BlockSpec(memory_space=pl.ANY)] * count


def in_hbm(count):
    return [pl.BlockSpec(memory_space=pltpu.HBM)] * count


def forward(name, places, layout, ext, sources, probe, tables):
    field = (len(places), 2 * SIDE, 2 * SIDE)
    return pl.pallas_call(
        functools.partial(forward_kernel, places, layout, len(sources)),
        out_shape=fields(places),
        in_specs=in_hbm(len(sources) + 2),
        out_specs=tuple(in_hbm(2)),
        scratch_shapes=[
            pltpu.VMEM(ext, jnp.float32),
            pltpu.VMEM(probe.shape, jnp.float32),
            pltpu.VMEM(tables.shape, tables.dtype),
            pltpu.VMEM(field, jnp.float32),
            pltpu.VMEM(field, jnp.float32),
            pltpu.SemaphoreType.DMA((len(sources) + 2,)),
            pltpu.SemaphoreType.DMA((1 + len(places),)),
        ],
        compiler_params=pltpu.CompilerParams(vmem_limit_bytes=VMEM_LIMIT),
        cost_estimate=stage_cost(8 * len(places)),
        name=name,
    )(*sources, probe, tables)


def forward_inner(places, tile, probe, tables):
    def layout(ext_ref, tile_ref):
        return [(tile_ref, ext_ref)]

    return forward("forward_inner", places, layout, tile.shape, (tile,), probe, tables)


def extended_shape(tile, comps):
    return pltpu.VMEM((comps, tile.shape[1] + BLOCK, tile.shape[2] + SIDE), jnp.float32)


def forward_side(places, tile, right, probe, tables):
    comps, rows, cols = tile.shape

    def layout(ext_ref, tile_ref, right_ref):
        return [
            (tile_ref.at[:, :, pl.ds(cols - SIDE, SIDE)], ext_ref.at[:, :, pl.ds(0, SIDE)]),
            (right_ref, ext_ref.at[:, :, pl.ds(SIDE, SIDE)]),
        ]

    here = [(row, 0) for row, _ in places]
    ext = (comps, rows, 2 * SIDE)
    return forward("forward_last_column", here, layout, ext, (tile, right), probe, tables)


def forward_last(places, tile, below, right, diag, probe, tables):
    comps, rows, cols = tile.shape

    def layout(ext_ref, tile_ref, below_ref, right_ref, diag_ref):
        low = pl.ds(rows - BLOCK, BLOCK)
        upper, lower = pl.ds(0, BLOCK), pl.ds(BLOCK, BLOCK)
        wide, beyond = pl.ds(0, cols), pl.ds(cols, SIDE)
        return [
            (tile_ref.at[:, low], ext_ref.at[:, upper, wide]),
            (below_ref, ext_ref.at[:, lower, wide]),
            (right_ref.at[:, low], ext_ref.at[:, upper, beyond]),
            (diag_ref, ext_ref.at[:, lower, beyond]),
        ]

    here = [(0, col) for _, col in places]
    ext = (comps, SIDE, cols + SIDE)
    sources = (tile, below, right, diag)
    return forward("forward_last_row", here, layout, ext, sources, probe, tables)


def gather_sums(meta_ref, items_ref, sum_ref, count_ref, arrivals):
    spare = sum_ref.shape[0] - 1
    sources = items_ref.shape[0]
    for corner in range(spare + 1):
        count_ref[corner] = 0
    for source in range(sources):
        if source % (sources // len(arrivals)) == 0:
            arrivals[source * len(arrivals) // sources].wait()
        for rank in range(CAP):
            corner = meta_ref[source, rank * BLOCK].astype(jnp.int32)
            at = jnp.where(corner < 0, spare, corner)
            hits = count_ref[at]
            count_ref[at] = hits + 1
            item = items_ref[source, rank * SIDE : (rank + 1) * SIDE]
            sum_ref[at] = jnp.where(hits > 0, sum_ref[at], 0.0) + item


def summed(sum_ref, count_ref, at):
    hits = count_ref[at]
    return hits.astype(jnp.float32), jnp.where(hits > 0, sum_ref[at], 0.0)


def backward_pairs(
    places,
    width,
    probe_ref,
    tables,
    far_ref,
    enter_ref,
    ext_ref,
    sum_ref,
    count_ref,
    store,
    before_pair,
    before_products,
    before_fields,
    after_fields,
):
    rows = []
    for pair, (row, col) in enumerate(places):
        before_pair(pair)
        waves = []
        for n in range(2):
            at = row * width + col // BLOCK + n
            hits, total = summed(sum_ref, count_ref, at)
            far_re, far_im = halves(far_ref[pair], n)
            misfit = 2.0 * (hits * (far_re * far_re + far_im * far_im) - total)
            waves.append((misfit * far_re, misfit * far_im))
        rows.append(stacked(waves))
    before_products()
    backs = two_sided(rows, tables, 6, 4)
    before_fields()
    rows = []
    for pair, (row, col) in enumerate(places):
        trans = [cut_pair(ext_ref, comp, row * BLOCK, col) for comp in range(2)]
        waves = []
        for n in range(2):
            back = halves(backs[pair], n)
            grad = conj_times(*halves(enter_ref[pair], n), *back)
            store(n, 2, row, col, grad[0])
            store(n, 3, row, col, grad[1])
            waves.append(conj_times(trans[0][n], trans[1][n], *back))
        rows.append(stacked(waves))
    backs = two_sided(rows, tables, 2, 0)
    after_fields()
    probe_re = probe_ref[0]
    probe_im = probe_ref[1]
    for pair, (row, col) in enumerate(places):
        for n in range(2):
            grad = conj_times(probe_re, probe_im, *halves(backs[pair], n))
            store(n, 0, row, col, grad[0])
            store(n, 1, row, col, grad[1])


def shifted(low, high):
    if low is None:
        low = jnp.zeros_like(high)
    if high is None:
        high = jnp.zeros_like(low)
    return pltpu.roll(jnp.where(low_lanes(low.shape), high, low), BLOCK, 1)


def backward_rim_kernel(
    places,
    recv_ref,
    tile_ref,
    below_ref,
    right_ref,
    diag_ref,
    probe_ref,
    tables_ref,
    far_last_ref,
    enter_last_ref,
    far_side_ref,
    enter_side_ref,
    row_ref,
    col_ref,
    out_below_ref,
    out_right_ref,
    out_diag_ref,
    out_sum_ref,
    count_ref,
    items_ref,
    meta_ref,
    table_buf,
    probe_buf,
    far_buf,
    enter_buf,
    ext_ref,
    sum_ref,
    even_ref,
    odd_ref,
    even_side_ref,
    odd_side_ref,
    row_buf,
    col_buf,
    below_buf,
    right_buf,
    diag_buf,
    sems,
    out_sems,
):
    rows, cols = tile_ref.shape[1:]
    last = rows // BLOCK - 1
    corners = sum_ref.shape[0] - 1
    near = far_last_ref.shape[0]
    first = pl.ds(0, near)
    others = pl.ds(near, far_side_ref.shape[0])
    two = pl.ds(2, 2)
    chunk = recv_ref.shape[0] // CHUNKS
    wide = pl.ds(0, cols)
    beyond = pl.ds(cols, SIDE)
    copies = start_copies(
        [(recv_ref.at[:, CAP * SIDE], meta_ref)]
        + [
            (recv_ref.at[part, pl.ds(0, CAP * SIDE)], items_ref.at[part])
            for part in (pl.ds(n * chunk, chunk) for n in range(CHUNKS))
        ]
        + [
            (far_last_ref, far_buf.at[first]),
            (tables_ref, table_buf),
            (far_side_ref, far_buf.at[others]),
            (enter_last_ref, enter_buf.at[first]),
            (enter_side_ref, enter_buf.at[others]),
            (tile_ref.at[two], ext_ref.at[:, pl.ds(0, rows), wide]),
            (below_ref.at[two], ext_ref.at[:, pl.ds(rows, BLOCK), wide]),
            (right_ref.at[two], ext_ref.at[:, pl.ds(0, rows), beyond]),
            (diag_ref.at[two], ext_ref.at[:, pl.ds(rows, BLOCK), beyond]),
            (probe_ref, probe_buf),
        ],
        sems,
    )
    wait_copies(copies[:1])
    rest = copies[1 + CHUNKS :]
    gather_sums(meta_ref, items_ref, sum_ref, count_ref, copies[1 : 1 + CHUNKS])
    bands = (even_ref, odd_ref)
    sides = (even_side_ref, odd_side_ref)
    stores = start_copies(
        [(sum_ref.at[pl.ds(0, corners)], out_sum_ref)], out_sems.at[pl.ds(20, 1)]
    )

    def store(n, comp, row, col, value):
        if row == last:
            bands[n][comp, :, col : col + SIDE] = value
        else:
            at = row * BLOCK
            top = value[:BLOCK]
            if row > 0:
                top = top + sides[n][comp, at : at + BLOCK]
            sides[n][comp, at : at + BLOCK] = top
            sides[n][comp, at + BLOCK : at + SIDE] = value[BLOCK:]

    half = rows // 2

    def finish(comp):
        beyond_cols = []
        for buf, part in ((row_buf, slice(0, BLOCK)), (below_buf, slice(BLOCK, SIDE))):
            before = None
            for col in range(0, cols, SIDE):
                here = odd_ref[comp, part, col : col + SIDE]
                buf[comp, :, col : col + SIDE] = even_ref[
                    comp, part, col : col + SIDE
                ] + shifted(before, here)
                before = here
            beyond_cols.append(shifted(before, None))
        corner = beyond_cols[1]
        diag_buf[comp] = corner[: BLOCK // 2] + pltpu.roll(corner[BLOCK // 2 :], BLOCK, 1)
        odd_side = odd_side_ref[comp]
        col_buf[comp] = even_side_ref[comp] + shifted(None, odd_side)
        side = shifted(odd_side, None)
        second = jnp.concatenate(
            [side[half : rows - BLOCK], side[rows - BLOCK :] + beyond_cols[0]], axis=0
        )
        right_buf[comp] = side[:half] + pltpu.roll(second, BLOCK, 1)
        stores.extend(
            start_copies(
                [
                    (below_buf.at[comp], out_below_ref.at[comp]),
                    (diag_buf.at[comp], out_diag_ref.at[comp]),
                    (right_buf.at[comp], out_right_ref.at[comp]),
                    (row_buf.at[comp], row_ref.at[comp]),
                    (col_buf.at[comp], col_ref.at[comp]),
                ],
                out_sems.at[pl.ds(5 * comp, 5)],
            )
        )

    def before_pair(pair):
        if pair == 0:
            rest[0].wait()
        if pair == near:
            rest[2].wait()

    def after_fields():
        finish(2)
        finish(3)

    backward_pairs(
        places,
        cols // BLOCK,
        probe_buf,
        table_buf,
        far_buf,
        enter_buf,
        ext_ref,
        sum_ref,
        count_ref,
        store,
        before_pair,
        lambda: wait_copies(rest[1:2]),
        lambda: wait_copies(rest[3:]),
        after_fields,
    )
    finish(0)
    finish(1)
    wait_copies(stores)


def backward_inner_kernel(
    places,
    count_ref,
    sum_ref,
    tile_ref,
    probe_ref,
    tables_ref,
    far_ref,
    enter_ref,
    row_ref,
    col_ref,
    out_ref,
    sum_buf,
    trans_buf,
    probe_buf,
    table_buf,
    far_buf,
    enter_buf,
    row_buf,
    col_buf,
    out_buf,
    even_ref,
    odd_ref,
    sems,
    out_sems,
):
    comps, rows, cols = out_buf.shape
    last = rows - BLOCK
    width = cols // BLOCK
    acc = (even_ref, odd_ref)
    row_blocks = last // BLOCK
    group = len(places) // row_blocks
    parts = []
    for n in range(row_blocks):
        here = pl.ds(n * width, width)
        parts.append((sum_ref.at[here], sum_buf.at[here]))
        here = pl.ds(n * group, group)
        parts.append((far_ref.at[here], far_buf.at[here]))
        if n == 0:
            parts.append((tables_ref, table_buf))
    copies = start_copies(
        parts
        + [
            (enter_ref, enter_buf),
            (tile_ref.at[pl.ds(2, 2)], trans_buf),
            (probe_ref, probe_buf),
            (row_ref, row_buf),
            (col_ref, col_buf),
        ],
        sems,
    )
    table_copy = copies.pop(2)
    rest = copies[2 * row_blocks :]
    stores = []

    def store(n, comp, row, col, value):
        at = row * BLOCK
        lanes = slice(col, col + SIDE)
        top = value[:BLOCK]
        if row > 0:
            top = top + acc[n][comp, at : at + BLOCK, lanes]
        acc[n][comp, at : at + BLOCK, lanes] = top
        acc[n][comp, at + BLOCK : at + SIDE, lanes] = value[BLOCK:]

    def finish(comp):
        before = None
        for col in range(0, cols, SIDE):
            lanes = slice(col, col + SIDE)
            if col < cols - SIDE:
                here = odd_ref[comp, :, lanes]
                value = even_ref[comp, :, lanes] + shifted(before, here)
                before = here
            else:
                value = col_buf[comp] + shifted(before, None)
            out_buf[comp, :last, lanes] = value[:last]
            out_buf[comp, last:, lanes] = value[last:] + row_buf[comp, :, lanes]
        stores.extend(
            start_copies(
                [(out_buf.at[comp], out_ref.at[comp])], out_sems.at[pl.ds(comp, 1)]
            )
        )

    def before_pair(pair):
        if pair % group == 0:
            at = 2 * (pair // group)
            wait_copies(copies[at : at + 2])

    def after_fields():
        finish(2)
        finish(3)

    backward_pairs(
        places,
        width,
        probe_buf,
        table_buf,
        far_buf,
        enter_buf,
        trans_buf,
        sum_buf,
        count_ref,
        store,
        before_pair,
        table_copy.wait,
        lambda: wait_copies(rest),
        after_fields,
    )
    finish(0)
    finish(1)
    wait_copies(stores)


def shapes_of(*shapes):
    return tuple(jax.ShapeDtypeStruct(shape, jnp.float32) for shape in shapes)


def backward_rim(places, recv, tile, below, right, diag, probe, tables, fields_last, fields_side):
    comps, rows, cols = tile.shape
    corners = (rows // BLOCK) * (cols // BLOCK)
    sources = recv.shape[0]
    field = (len(places), 2 * SIDE, 2 * SIDE)
    outs = (
        (comps, BLOCK, cols),
        (comps, rows, SIDE),
        (comps, BLOCK, cols),
        (comps, rows // 2, SIDE),
        (comps, BLOCK // 2, SIDE),
    )
    return pl.pallas_call(
        functools.partial(backward_rim_kernel, places),
        out_shape=shapes_of(*outs, (corners, SIDE, SIDE))
        + (jax.ShapeDtypeStruct((corners + 1,), jnp.int32),),
        in_specs=in_hbm(11),
        out_specs=tuple(in_hbm(6)) + (pl.BlockSpec(memory_space=pltpu.SMEM),),
        scratch_shapes=[
            pltpu.VMEM((sources, CAP * SIDE, SIDE), jnp.float32),
            pltpu.SMEM((sources, SIDE), jnp.float32),
            pltpu.VMEM(tables.shape, tables.dtype),
            pltpu.VMEM(probe.shape, jnp.float32),
            pltpu.VMEM(field, jnp.float32),
            pltpu.VMEM(field, jnp.float32),
            extended_shape(tile, 2),
            pltpu.VMEM((corners + 1, SIDE, SIDE), jnp.float32),
            pltpu.VMEM((comps, SIDE, cols), jnp.float32),
            pltpu.VMEM((comps, SIDE, cols), jnp.float32),
            pltpu.VMEM((comps, rows, SIDE), jnp.float32),
            pltpu.VMEM((comps, rows, SIDE), jnp.float32),
        ]
        + [pltpu.VMEM(shape, jnp.float32) for shape in outs]
        + [pltpu.SemaphoreType.DMA((CHUNKS + 11,)), pltpu.SemaphoreType.DMA((21,))],
        compiler_params=pltpu.CompilerParams(vmem_limit_bytes=VMEM_LIMIT),
        cost_estimate=stage_cost(len(places)),
        name="backward_rim",
    )(recv, tile, below, right, diag, probe, tables, *fields_last, *fields_side)


def backward_inner(places, count, sums, tile, probe, tables, far, enter, row, col):
    comps, rows, cols = tile.shape
    return pl.pallas_call(
        functools.partial(backward_inner_kernel, places),
        out_shape=jax.ShapeDtypeStruct(tile.shape, jnp.float32),
        in_specs=[pl.BlockSpec(memory_space=pltpu.SMEM)] + in_hbm(8),
        out_specs=in_hbm(1)[0],
        scratch_shapes=[
            pltpu.VMEM(sums.shape, jnp.float32),
            pltpu.VMEM((2, rows, cols), jnp.float32),
            pltpu.VMEM(probe.shape, jnp.float32),
            pltpu.VMEM(tables.shape, tables.dtype),
            pltpu.VMEM(far.shape, jnp.float32),
            pltpu.VMEM(enter.shape, jnp.float32),
            pltpu.VMEM(row.shape, jnp.float32),
            pltpu.VMEM(col.shape, jnp.float32),
            pltpu.VMEM(tile.shape, jnp.float32),
            pltpu.VMEM((comps, rows, cols - SIDE), jnp.float32),
            pltpu.VMEM((comps, rows, cols - SIDE), jnp.float32),
            pltpu.SemaphoreType.DMA((2 * (rows // BLOCK - 1) + 6,)),
            pltpu.SemaphoreType.DMA((comps,)),
        ],
        compiler_params=pltpu.CompilerParams(vmem_limit_bytes=VMEM_LIMIT),
        cost_estimate=stage_cost(len(places)),
        name="backward_inner",
    )(count, sums, tile, probe, tables, far, enter, row, col)


def border_kernel(
    own_ref, above_ref, left_ref, diag_ref, out_ref, top_ref, side_ref, row_buf, col_buf, diag_buf, sems
):
    rows = out_ref.shape[1]
    half = rows // 2
    top = out_ref.at[:, pl.ds(0, BLOCK)]
    side = out_ref.at[:, pl.ds(BLOCK, rows - BLOCK), pl.ds(0, SIDE)]
    loads = start_copies(
        [
            (above_ref, row_buf),
            (top, top_ref),
            (left_ref, col_buf),
            (diag_ref, diag_buf),
            (side, side_ref),
        ],
        sems,
    )
    def unpacked(packed):
        low = low_lanes(packed.shape)
        upper = jnp.where(low, packed, 0.0)
        return upper, pltpu.roll(jnp.where(low, 0.0, packed), BLOCK, 2)

    wait_copies(loads[:2])
    top_ref[...] = top_ref[...] + row_buf[...]
    wait_copies(loads[2:4])
    upper, lower = unpacked(col_buf[...])
    corner = jnp.concatenate(unpacked(diag_buf[...]), axis=1)
    top_ref[:, :, :SIDE] = top_ref[:, :, :SIDE] + upper[:, :BLOCK] + corner
    stores = start_copies([(top_ref, top)], sems.at[pl.ds(5, 1)])
    wait_copies(loads[4:])
    side_ref[:, : half - BLOCK] = side_ref[:, : half - BLOCK] + upper[:, BLOCK:]
    side_ref[:, half - BLOCK :] = side_ref[:, half - BLOCK :] + lower
    stores += start_copies([(side_ref, side)], sems.at[pl.ds(6, 1)])
    wait_copies(stores)


def add_borders(own, above, left, diag):
    comps, rows, cols = own.shape
    return pl.pallas_call(
        border_kernel,
        out_shape=jax.ShapeDtypeStruct(own.shape, jnp.float32),
        in_specs=anywhere(4),
        out_specs=pl.BlockSpec(memory_space=pl.ANY),
        scratch_shapes=[
            pltpu.VMEM((comps, BLOCK, cols), jnp.float32),
            pltpu.VMEM((comps, rows - BLOCK, SIDE), jnp.float32),
            pltpu.VMEM(above.shape, jnp.float32),
            pltpu.VMEM(left.shape, jnp.float32),
            pltpu.VMEM(diag.shape, jnp.float32),
            pltpu.SemaphoreType.DMA((7,)),
        ],
        input_output_aliases={0: 0},
        compiler_params=pltpu.CompilerParams(vmem_limit_bytes=VMEM_LIMIT),
        name="add_borders",
    )(own, above, left, diag)


def row_strip_kernel(tile_ref, row_ref, sems):
    wait_copies(start_copies([(tile_ref.at[:, pl.ds(0, BLOCK)], row_ref)], sems))


def row_strip(tile):
    comps, rows, cols = tile.shape
    return pl.pallas_call(
        row_strip_kernel,
        out_shape=jax.ShapeDtypeStruct((comps, BLOCK, cols), jnp.float32),
        in_specs=in_hbm(1),
        out_specs=in_vmem(1)[0],
        scratch_shapes=[pltpu.SemaphoreType.DMA((1,))],
        compiler_params=pltpu.CompilerParams(vmem_limit_bytes=VMEM_LIMIT),
        name="row_strip",
    )(tile)


def column_strip_kernel(tile_ref, send_ref, out_ref, sems):
    wait_copies(start_copies([(tile_ref.at[:, :, pl.ds(0, SIDE)], out_ref)], sems))


def column_strip(tile, send):
    comps, rows, cols = tile.shape
    return pl.pallas_call(
        column_strip_kernel,
        out_shape=jax.ShapeDtypeStruct((comps, rows, SIDE), jnp.float32),
        in_specs=in_hbm(2),
        out_specs=pl.BlockSpec(memory_space=pltpu.VMEM),
        scratch_shapes=[pltpu.SemaphoreType.DMA((1,))],
        compiler_params=pltpu.CompilerParams(vmem_limit_bytes=VMEM_LIMIT),
        name="column_strip",
    )(tile, send)


def moved(shard, down, across):
    row_total = lax.axis_size("row")
    col_total = lax.axis_size("col")
    if across == 0:
        pairs = [(r, r + down) for r in range(row_total) if 0 <= r + down < row_total]
        return lax.ppermute(shard, "row", pairs)
    if down == 0:
        pairs = [(c, c + across) for c in range(col_total) if 0 <= c + across < col_total]
        return lax.ppermute(shard, "col", pairs)
    pairs = [
        (r * col_total + c, (r + down) * col_total + c + across)
        for r in range(row_total)
        for c in range(col_total)
        if 0 <= r + down < row_total and 0 <= c + across < col_total
    ]
    return lax.ppermute(shard, ("row", "col"), pairs)


def body(object_slices, probe, measured, offsets):
    slices, parts, tile_rows, tile_cols = object_slices.shape
    tile = object_slices.reshape(slices * parts, tile_rows, tile_cols)
    row_total = lax.axis_size("row")
    tables = jnp.asarray(TABLES)
    below = moved(row_strip(tile), -1, 0)
    send = pack(offsets, measured, row_total)
    recv = lax.all_to_all(send, "row", split_axis=0, concat_axis=0, tiled=True)
    right = moved(column_strip(tile, send), 0, -1)
    last, side, inner = pair_places(tile_rows, tile_cols)
    far_inner, enter_inner = forward_inner(inner, tile, probe, tables)
    right, far_inner = lax.optimization_barrier((right, far_inner))
    far_side, enter_side = forward_side(side, tile, right, probe, tables)
    below, far_side = lax.optimization_barrier((below, far_side))
    diag = moved(below[:, :, :SIDE], 0, -1)
    far_last, enter_last = forward_last(last, tile, below, right, diag, probe, tables)
    row, col, to_below, to_right, to_diag, sums, count = backward_rim(
        last + side,
        recv,
        tile,
        below,
        right,
        diag,
        probe,
        tables,
        (far_last, enter_last),
        (far_side, enter_side),
    )
    above = moved(to_below, 1, 0)
    left = moved(to_right, 0, 1)
    corner_part = moved(to_diag, 1, 1)
    own = backward_inner(
        inner, count, sums, tile, probe, tables, far_inner, enter_inner, row, col
    )
    result = add_borders(own, above, left, corner_part)
    return result.reshape(object_slices.shape)


def solution(mesh):
    placed = (
        P(None, None, "row", "col"),
        P(),
        P(("row", "col"), None, None),
        P(None, ("row", "col")),
    )
    return jax.shard_map(
        body, mesh=mesh, in_specs=placed, out_specs=P(None, None, "row", "col"), check_vma=False
    )
```
